32 devices in a mesh: dp: 16 (over z, y, x), tower: 2 (over core).
Axes of the slice: x: 2, y: 2, z: 4, core: 2. Of those that a mesh axis runs over, the one named last changes fastest.
Arguments:
- query_tokens: bfloat16 [32, 64, 768], P('dp'), may hold values from -8 to 8
- passage_tokens: bfloat16 [32, 512, 768], P('dp'), may hold values from -8 to 8
- lengths: int32 [2, 32], P('tower', 'dp'), may hold values from 1 to 512, as said below
- positives: int32 [32], replicated, may hold values from 0 to 31, each once
- query_weight: bfloat16 [768, 768], P('dp'), may hold values from -0.21875 to 0.21875
- key_weight: bfloat16 [768, 768], P('dp'), may hold values from -0.21875 to 0.21875
- value_weight: bfloat16 [768, 768], P('dp'), may hold values from -0.21875 to 0.21875
- output_weight: bfloat16 [768, 768], P('dp'), may hold values from -0.4375 to 0.4375
- inner_weight: bfloat16 [768, 3072], P('dp'), may hold values from -0.21875 to 0.21875
- outer_weight: bfloat16 [3072, 768], P('dp'), may hold values from -0.109375 to 0.109375
- query_bias: bfloat16 [768], P('dp'), may hold values from -1.75 to 1.75
- value_bias: bfloat16 [768], P('dp'), may hold values from -1.75 to 1.75
- output_bias: bfloat16 [768], P('dp'), may hold values from -0.625 to 0.625
- inner_bias: bfloat16 [3072], P('dp'), may hold values from -1.75 to 1.75
- outer_bias: bfloat16 [768], P('dp'), may hold values from -0.625 to 0.625
- first_gain: bfloat16 [768], P('dp'), may hold values from 0.5 to 1.5
- first_shift: bfloat16 [768], P('dp'), may hold values from -0.625 to 0.625
- second_gain: bfloat16 [768], P('dp'), may hold values from 0.5 to 1.5
- second_shift: bfloat16 [768], P('dp'), may hold values from -0.625 to 0.625
Outputs:
- loss_value: float32 [], replicated
- query_grads: float32 [32, 64, 768], P('dp')
- passage_grads: float32 [32, 512, 768], P('dp')
- grad_query: float32 [768, 768], P('dp')
- grad_key: float32 [768, 768], P('dp')
- grad_value: float32 [768, 768], P('dp')
- grad_output: float32 [768, 768], P('dp')
- grad_inner: float32 [768, 3072], P('dp')
- grad_outer: float32 [3072, 768], P('dp')
- grad_qbias: float32 [768], P('dp')
- grad_vbias: float32 [768], P('dp')
- grad_obias: float32 [768], P('dp')
- grad_inbias: float32 [3072], P('dp')
- grad_outbias: float32 [768], P('dp')
- grad_gainone: float32 [768], P('dp')
- grad_shiftone: float32 [768], P('dp')
- grad_gaintwo: float32 [768], P('dp')
- grad_shifttwo: float32 [768], P('dp')
The draws below stay inside these ranges and needn't reach their ends.
Inputs may be any that keep to these rules, and one draw needn't show every extreme that they name: Query lengths (row 0) are at most 64, and some query has exactly 64; some passage has exactly 512. `positives`: each passage is the positive of exactly one query.
All inputs are finite; a program needn't handle non-finite values.
Results may differ from the reference program's by a relative error of at most 0.014.
Values may be sent and summed in bfloat16 or wider, within the bound.
A program may use at most 256 MiB of HBM per device.

```python
import jax
import jax.numpy as jnp
from jax import lax

D = 768
HEADS = 12
HDIM = 64
FF = 3072
SEQ = 512
QMAX = 64
PAIRS = 32


def rows_with_common(key, count, slots):
    first_key, second_key = jax.random.split(key)
    common = 0.5 * jax.random.normal(first_key, (count, 1, D), jnp.float32)
    single = jax.random.normal(second_key, (count, slots, D), jnp.float32)
    return jnp.clip(common + single, -8.0, 8.0).astype(jnp.bfloat16)


def draw_query_tokens(key, part):
    key = jax.random.fold_in(key, 5)
    return rows_with_common(key, PAIRS, QMAX)


def draw_passage_tokens(key, part):
    key = jax.random.fold_in(key, 7)
    return rows_with_common(key, PAIRS, SEQ)


def draw_lengths(key, part):
    key = jax.random.fold_in(key, 11)
    first_key, second_key, third_key, fourth_key, fifth_random_key = jax.random.split(key, 5)
    factor_one = jax.random.randint(first_key, (PAIRS,), 1, SEQ + 1)
    factor_two = jax.random.randint(second_key, (PAIRS,), 1, SEQ + 1)
    passage = jnp.clip(SEQ // 8 + factor_one * factor_two // SEQ, 1, SEQ)
    longest = jax.random.randint(third_key, (), 0, PAIRS)
    positions = jnp.arange(PAIRS)
    passage = jnp.where(positions == longest, SEQ, passage)
    query = jax.random.randint(fourth_key, (PAIRS,), 1, QMAX + 1)
    longest_query = jax.random.randint(fifth_random_key, (), 0, PAIRS)
    query = jnp.where(positions == longest_query, QMAX, query)
    return jnp.stack([query, passage]).astype(jnp.int32)


def level_of(stream_key, extent, cuts, low, top_value):
    factor_of, own = 1.0, jax.random.fold_in(stream_key, 6)
    for axis_at, shards_of in cuts:
        steps = jnp.exp(jax.random.uniform(jax.random.fold_in(own, axis_at), (shards_of,), jnp.float32, low / len(cuts), top_value / len(cuts)))
        factor_of = factor_of * jnp.repeat(steps, extent[axis_at] // shards_of).reshape([-1 if axis == axis_at else 1 for axis in range(len(extent))])
    return factor_of


def centred(own_key, shape, width, limit, pieces=(), kind=jnp.bfloat16):
    drawn = jax.random.normal(own_key, shape, jnp.float32) * width
    if len(pieces) > 0:
        drawn = level_of(own_key, shape, pieces, -0.22, 0.18) * drawn
    return jnp.clip(drawn, min=-limit, max=limit).astype(kind)


def setup_inputs(seed: int = 0) -> dict:
    arg_keys = jax.random.split(jax.random.key(seed), 20)
    return {
        "query_tokens": draw_query_tokens(jax.random.fold_in(arg_keys[19], 71), 0),
        "passage_tokens": draw_passage_tokens(jax.random.fold_in(arg_keys[19], 71), 0),
        "lengths": draw_lengths(jax.random.fold_in(arg_keys[19], 71), 0),
        "positives": jax.random.permutation(arg_keys[3], PAIRS).astype(jnp.int32),
        "query_weight": centred(arg_keys[4], (D, D), D ** -0.5, 0.21875, ((0, 16),)),
        "key_weight": centred(arg_keys[5], (D, D), D ** -0.5, 0.21875, ((0, 16),)),
        "value_weight": centred(arg_keys[6], (D, D), D ** -0.5, 0.21875, ((0, 16),)),
        "output_weight": centred(arg_keys[7], (D, D), (D // 4) ** -0.5, 0.4375, ((0, 16),)),
        "inner_weight": centred(arg_keys[8], (D, FF), D ** -0.5, 0.21875, ((0, 16),)),
        "outer_weight": centred(arg_keys[9], (FF, D), FF ** -0.5, 0.109375, ((0, 16),)),
        "query_bias": centred(arg_keys[10], (D,), 0.3, 1.75, ((0, 16),)),
        "value_bias": centred(arg_keys[11], (D,), 0.3, 1.75, ((0, 16),)),
        "output_bias": centred(arg_keys[12], (D,), 0.1, 0.625, ((0, 16),)),
        "inner_bias": centred(arg_keys[13], (FF,), 0.3, 1.75, ((0, 16),)),
        "outer_bias": centred(arg_keys[14], (D,), 0.1, 0.625, ((0, 16),)),
        "first_gain": jnp.clip(1.0 + 0.1 * jax.random.normal(arg_keys[15], (D,), jnp.float32), 0.5, 1.5).astype(jnp.bfloat16),
        "first_shift": centred(arg_keys[16], (D,), 0.1, 0.625, ((0, 16),)),
        "second_gain": jnp.clip(1.0 + 0.1 * jax.random.normal(arg_keys[17], (D,), jnp.float32), 0.5, 1.5).astype(jnp.bfloat16),
        "second_shift": centred(arg_keys[18], (D,), 0.1, 0.625, ((0, 16),)),
    }


@jax.custom_vjp
def low(v):
    return lax.optimization_barrier(v.astype(jnp.bfloat16)).astype(jnp.float32)

@jax.custom_vjp
def low_back(v):
    return v

def low_keep(v):
    return (low(v), None)

def low_pass(kept, grad):
    return (grad,)

def back_keep(v):
    return (v, None)

def back_low(kept, grad):
    return (low(grad),)
low.defvjp(low_keep, low_pass)
low_back.defvjp(back_keep, back_low)
contrast_scale_divisor = 0.01
highest = lax.Precision.HIGHEST

def linear_product(left, right):
    return jnp.dot(left, right, precision=highest, preferred_element_type=jnp.float32)

def layer_norm(hidden, gain, shift):
    center = hidden - lax.optimization_barrier(jnp.mean(hidden, axis=-1, keepdims=True))
    spread = lax.optimization_barrier(jnp.mean(center * center, axis=-1, keepdims=True))
    return center * lax.rsqrt(spread + 1e-12) * gain + shift

def encode(token_row, length, params):
    query_w, key_w, value_w, output_w, inner_w, outer_w, query_b, value_b, output_b, inner_b, outer_b, gain_one, shift_one, second_norm_gain, shift_two = params
    seq_len = token_row.shape[0]
    head_scale = HDIM ** (-0.5)
    queries = low(low_back(linear_product(token_row, query_w) + query_b)).reshape(seq_len, HEADS, HDIM)
    lookup_sequence_states = low(low_back(linear_product(token_row, key_w))).reshape(seq_len, HEADS, HDIM)
    values_seq = low(low_back(linear_product(token_row, value_w) + value_b)).reshape(seq_len, HEADS, HDIM)
    scores = low_back(jnp.einsum('qhd,khd->hqk', queries, lookup_sequence_states, precision=highest) * head_scale)
    key_valid = jnp.arange(seq_len) < length
    scores = jnp.where(key_valid[None, None, :], scores, -1000000000.0)
    probs_low = low(jax.nn.softmax(scores, axis=-1))
    context = low(low_back(jnp.einsum('hqk,khd->qhd', probs_low, values_seq, precision=highest)))
    context = context.reshape(seq_len, HEADS * HDIM)
    attended = low_back(linear_product(context, output_w) + output_b)
    normed = layer_norm(token_row + attended, gain_one, shift_one)
    inner_pre = low_back(linear_product(low(normed), inner_w) + inner_b)
    activation = low(jax.nn.gelu(inner_pre, approximate=False))
    outer_out = low_back(linear_product(activation, outer_w) + outer_b)
    output_rows = layer_norm(normed + outer_out, second_norm_gain, shift_two)
    row_mask = key_valid.astype(output_rows.dtype)
    return lax.optimization_barrier(jnp.sum(output_rows * row_mask[:, None], axis=0)) / length.astype(output_rows.dtype)

def reference(query_tokens, passage_tokens, lengths, positives, query_weight, key_weight, value_weight, output_weight, inner_weight, outer_weight, query_bias, value_bias, output_bias, inner_bias, outer_bias, first_gain, first_shift, second_gain, second_shift):
    query_in = query_tokens.astype(jnp.float32)
    passage_in = passage_tokens.astype(jnp.float32)
    params = tuple((tensor.astype(jnp.float32) for tensor in (query_weight, key_weight, value_weight, output_weight, inner_weight, outer_weight, query_bias, value_bias, output_bias, inner_bias, outer_bias, first_gain, first_shift, second_gain, second_shift)))
    query_len = lengths[0].astype(jnp.int32)
    passage_len = lengths[1].astype(jnp.int32)

    def objective(query_rows, passage_rows, weights_in):

        def one_row(record):
            return encode(record[0], record[1], weights_in)
        pooled_q = lax.map(jax.checkpoint(one_row), (query_rows, query_len))
        pooled_p = lax.map(jax.checkpoint(one_row), (passage_rows, passage_len))
        normalized_question_vectors = pooled_q / jnp.sqrt(lax.optimization_barrier(jnp.sum(pooled_q * pooled_q, axis=-1, keepdims=True)) + 1e-06)
        normalized_document_vectors = pooled_p / jnp.sqrt(lax.optimization_barrier(jnp.sum(pooled_p * pooled_p, axis=-1, keepdims=True)) + 1e-06)
        pair_score_table = linear_product(normalized_question_vectors, normalized_document_vectors.T) / contrast_scale_divisor
        onehot = positives[:, None] == jnp.arange(PAIRS, dtype=jnp.int32)[None, :]
        picked = lax.optimization_barrier(jnp.sum(jnp.where(onehot, pair_score_table, 0.0), axis=-1))
        return jnp.mean(jax.nn.logsumexp(pair_score_table, axis=-1) - picked)
    loss_value, pullback = jax.vjp(objective, query_in, passage_in, params)
    query_grads, passage_grads, grads = pullback(jnp.ones_like(loss_value) * (PAIRS * SEQ))
    return (loss_value, query_grads, passage_grads, grads[0], grads[1], grads[2], grads[3], grads[4], grads[5], grads[6], grads[7], grads[8], grads[9], grads[10], grads[11], grads[12], grads[13], grads[14])
```

```python
import functools

import jax
import jax.numpy as jnp
from jax import lax
from jax.experimental import pallas as pl
from jax.experimental.pallas import tpu as pltpu
from jax.sharding import PartitionSpec as P

MESH = pl.DeviceIdType.MESH
ANY = pl.BlockSpec(memory_space=pl.ANY)
VM = pl.BlockSpec(memory_space=pltpu.VMEM)


class Place:
    def __init__(self, inner):
        dp = lax.axis_index("dp")
        self.c = lax.axis_index("tower")
        self.inner = inner
        self.low = lax.rem(dp, inner)
        self.me = dp // inner
        self.z = self.me // 4
        self.quad = lax.rem(self.me, 4)
        s1 = 1 + self.c
        s2 = 2 - self.c
        b1 = lax.rem(self.quad // s1, 2)
        b2 = lax.rem(self.quad // s2, 2)
        self.q1 = self.quad + s1 * (1 - 2 * b1)
        self.q2 = self.quad + s2 * (1 - 2 * b2)
        self.q12 = 3 - self.quad
        self.quads = (self.quad, self.q1, self.q2, self.q12)

    def ring(self, k):
        return lax.rem(self.z + k, 4)

    def dev(self, group):
        return {"dp": group * self.inner + self.low, "tower": self.c}

    def n1(self):
        return self.dev(self.z * 4 + self.q1)

    def n2(self):
        return self.dev(self.z * 4 + self.q2)

    def up(self, k):
        return self.dev(self.ring(k) * 4 + self.quad)

    def sib(self):
        return {"dp": self.me * self.inner + self.low, "tower": 1 - self.c}

    def barrier(self):
        sem = pltpu.get_barrier_semaphore()
        for target in (self.up(1), self.up(2), self.up(3), self.n1(), self.n2(), self.sib()):
            pl.semaphore_signal(sem, inc=1, device_id=target, device_id_type=MESH)
        pl.semaphore_wait(sem, 6)


def remote(src, dst, send_sem, recv_sem, target):
    return pltpu.make_async_remote_copy(
        src_ref=src, dst_ref=dst, send_sem=send_sem, recv_sem=recv_sem, device_id=target, device_id_type=MESH
    )


class Cut:
    def __init__(self, per):
        self.per = per
        self.each = 4 // per
        self.count = 3 * self.each

    def kind(self, g):
        return g // self.each, g % self.each

    def shape(self, kind):
        per = self.per
        return ((per, 48, 384), (48, 384 * per), (48 * per, 384))[kind]

    def whole(self, refs, g, s, which):
        per = self.per
        kind, n = self.kind(g)
        ref = refs[kind]
        if kind == 0:
            return ref.at[pl.ds(n * per, per), pl.ds(pl.multiple_of(s * 48, 16), 48), pl.ds(pl.multiple_of(which * 384, 128), 384)]
        if kind == 1:
            return ref.at[pl.ds(pl.multiple_of(s * 48, 16), 48), pl.ds(pl.multiple_of((2 * n + which) * 384 * per, 128), 384 * per)]
        return ref.at[pl.ds(pl.multiple_of(s * 192 + n * 48 * per, 16), 48 * per), pl.ds(pl.multiple_of(which * 384, 128), 384)]

    def shard(self, refs, g, which):
        per = self.per
        kind, n = self.kind(g)
        ref = refs[kind]
        if kind == 0:
            return ref.at[pl.ds(n * per, per), :, pl.ds(pl.multiple_of(which * 384, 128), 384)]
        if kind == 1:
            return ref.at[:, pl.ds(pl.multiple_of((2 * n + which) * 384 * per, 128), 384 * per)]
        return ref.at[pl.ds(n * 48 * per, 48 * per), pl.ds(pl.multiple_of(which * 384, 128), 384)]


def gather_kernel(inner, cut, v_in, a_in, i_in, o_in, len_in, v_out, a_out, i_out, o_out, len_out, ssem, rsem, lsem, xsem):
    p = Place(inner)
    c = p.c
    groups = cut.count + 1
    ins = (a_in, i_in, o_in)
    outs = (a_out, i_out, o_out)
    local = [pltpu.make_async_copy(len_in, len_out.at[c], lsem.at[0]), pltpu.make_async_copy(v_in, v_out.at[p.me], lsem.at[1])]
    rows = pl.ds(pl.multiple_of(p.me * 48, 16), 48)
    local.append(pltpu.make_async_copy(a_in, a_out.at[:, rows], lsem.at[2]))
    local.append(pltpu.make_async_copy(i_in, i_out.at[rows], lsem.at[3]))
    local.append(pltpu.make_async_copy(o_in, o_out.at[pl.ds(pl.multiple_of(p.me * 192, 16), 192)], lsem.at[4]))
    for copy in local:
        copy.start()
    p.barrier()

    def slot(t, s, which):
        if t == 0:
            return v_out.at[s, :, pl.ds(pl.multiple_of(which * 128, 128), 128)]
        return cut.whole(outs, t - 1, s, which)

    def own(t):
        if t == 0:
            return v_in.at[:, pl.ds(pl.multiple_of(c * 128, 128), 128)]
        return cut.shard(ins, t - 1, c)

    lens = remote(len_in, len_out.at[c], xsem.at[0], xsem.at[1], p.sib())
    lens.start()

    def push(t, src, s, k, target):
        remote(src, slot(t, s, c), ssem.at[t, k], rsem.at[t, k], target).start()

    def arrived(t, s, k, which):
        view = slot(t, s, which)
        remote(view, view, ssem.at[t, k], rsem.at[t, k], p.sib()).wait_recv()

    def shard(k, q):
        return p.ring(4 - k) * 4 + p.quads[q]

    def stage_own(t):
        for k in range(1, 4):
            push(t, own(t), p.me, k, p.up(k))
        push(t, own(t), p.me, 4, p.n1())
        push(t, own(t), p.me, 8, p.n2())

    def stage_z(t):
        for k in range(1, 4):
            s = shard(k, 0)
            arrived(t, s, k, c)
            view = slot(t, s, c)
            push(t, view, s, 4 + k, p.n1())
            push(t, view, s, 8 + k, p.n2())
            push(t, view, s, 16 + k, p.sib())

    def stage_one(t):
        for k in range(4):
            s = shard(k, 1)
            arrived(t, s, 4 + k, c)
            view = slot(t, s, c)
            push(t, view, s, 12 + k, p.n2())
            push(t, view, s, 20 + k, p.sib())

    def stage_two(t):
        for q in (2, 3):
            for k in range(4):
                s = shard(k, q)
                arrived(t, s, q * 4 + k, c)
                view = slot(t, s, c)
                push(t, view, s, 16 + q * 4 + k, p.sib())

    ahead = AHEAD
    for t in range(ahead):
        stage_own(t)
    for step in range(groups + 2):
        if step < groups:
            stage_z(step)
        if step + ahead < groups:
            stage_own(step + ahead)
        if 0 <= step - 1 < groups:
            stage_one(step - 1)
        if 0 <= step - 2 < groups:
            stage_two(step - 2)

    for t in range(groups):
        for q in range(4):
            sq = (0, 2, 1, 3)[q]
            for k in range(4):
                if q == 0 and k == 0:
                    continue
                s = shard(k, sq)
                arrived(t, s, 16 + q * 4 + k, 1 - c)
    for t in range(groups):
        for k in range(1, 32):
            if k == 16:
                continue
            view = slot(t, p.me, c)
            remote(view, view, ssem.at[t, k], rsem.at[t, k], p.sib()).wait_send()
    for copy in local:
        copy.wait()
    lens.wait_send()
    remote(len_in, len_out.at[1 - c], xsem.at[0], xsem.at[1], p.sib()).wait_recv()

AHEAD = 1

def gather_all(inner, cut, vec, wa, wi, wo, lens, cid=0):
    bf = jnp.bfloat16
    groups = cut.count + 1
    return pl.pallas_call(
        functools.partial(gather_kernel, inner, cut),
        out_shape=(
            jax.ShapeDtypeStruct((16,) + vec.shape, bf),
            jax.ShapeDtypeStruct((4, 768, 768), bf),
            jax.ShapeDtypeStruct((768, 3072), bf),
            jax.ShapeDtypeStruct((3072, 768), bf),
            jax.ShapeDtypeStruct((2,) + lens.shape, jnp.int32),
        ),
        in_specs=[ANY] * 5,
        out_specs=[ANY] * 5,
        scratch_shapes=[
            pltpu.SemaphoreType.DMA((groups, 32)),
            pltpu.SemaphoreType.DMA((groups, 32)),
            pltpu.SemaphoreType.DMA((5,)),
            pltpu.SemaphoreType.DMA((2,)),
        ],
        compiler_params=pltpu.CompilerParams(collective_id=cid, has_side_effects=True),
        name="gather_weights",
    )(vec, wa, wi, wo, lens)


def scatter_kernel(inner, cut, v_in, a_in, i_in, o_in, x_in, v_out, a_out, i_out, o_out, q_out, p_out, *scr):
    p = Place(inner)
    c = p.c
    groups = cut.count + 1
    bufs = [scr[4 * i : 4 * i + 4] for i in range(5)]
    ssem, rsem, lsem, xsem = scr[20:24]
    ins = (a_in, i_in, o_in)
    outs = (a_out, i_out, o_out)

    def buf(level, t):
        if t == 0:
            return bufs[level][0]
        kind, n = cut.kind(t - 1)
        return bufs[level][1 + kind].at[n]

    def part(t, s, which):
        if t == 0:
            return v_in.at[s, :, pl.ds(pl.multiple_of(which * 128, 128), 128)]
        return cut.whole(ins, t - 1, s, which)

    def result(t, which):
        if t == 0:
            return v_out.at[:, pl.ds(pl.multiple_of(which * 128, 128), 128)]
        return cut.shard(outs, t - 1, which)

    order = tuple(range(groups - 1, -1, -1))
    for t in order:
        @pl.loop(0, 16)
        def _(s):
            pltpu.make_async_copy(part(t, s, c), buf(0, t).at[s], lsem.at[t]).start()

    p_rows = x_in.at[pl.ds(0, p_out.shape[1])]
    q_rows = x_in.at[pl.ds(p_out.shape[1], q_out.shape[1])]
    mine = [pltpu.make_async_copy(p_rows, p_out.at[c], xsem.at[0]), pltpu.make_async_copy(q_rows, q_out.at[c], xsem.at[1])]
    for copy in mine:
        copy.start()
    p.barrier()
    theirs = [remote(p_rows, p_out.at[c], xsem.at[2], xsem.at[3], p.sib()), remote(q_rows, q_out.at[c], xsem.at[4], xsem.at[5], p.sib())]

    def share(t):
        for sq in (p.q12, p.q1, p.q2, p.quad):
            @pl.loop(0, 4)
            def _(z):
                s = z * 4 + sq
                remote(part(t, s, 1 - c), buf(1, t).at[s], ssem.at[t, s], rsem.at[t, s], p.sib()).start()

    def add(t, s, other):
        acc = buf(0, t)
        acc[s] = (acc[s].astype(jnp.float32) + other.astype(jnp.float32)).astype(acc.dtype)

    def recv(t, k, ref):
        remote(ref, ref, ssem.at[t, k], rsem.at[t, k], p.sib()).wait_recv()

    def stage0(t):
        acc, r0, r1 = buf(0, t), buf(1, t), buf(2, t)
        pltpu.make_async_copy(acc, acc, lsem.at[t]).wait()
        for j, q in enumerate((p.q2, p.q12)):
            @pl.loop(0, 4)
            def _(z):
                s = z * 4 + q
                recv(t, s, r0.at[s])
                add(t, s, r0[s])
                k = 16 + z * 2 + j
                remote(acc.at[s], r1.at[z * 2 + j], ssem.at[t, k], rsem.at[t, k], p.n2()).start()
        for q in (p.q1, p.quad):
            @pl.loop(0, 4)
            def _(z):
                s = z * 4 + q
                recv(t, s, r0.at[s])
                add(t, s, r0[s])

    def stage1(t):
        acc, r1, r2 = buf(0, t), buf(2, t), buf(3, t)
        @pl.loop(0, 4)
        def _(z):
            s = z * 4 + p.q1
            recv(t, 17 + z * 2, r1.at[z * 2 + 1])
            add(t, s, r1[z * 2 + 1])
            remote(acc.at[s], r2.at[z], ssem.at[t, 24 + z], rsem.at[t, 24 + z], p.n1()).start()
        @pl.loop(0, 4)
        def _(z):
            s = z * 4 + p.quad
            recv(t, 16 + z * 2, r1.at[z * 2])
            add(t, s, r1[z * 2])

    def stage2(t):
        acc, r2, r3 = buf(0, t), buf(3, t), buf(4, t)
        for k in range(1, 4):
            z = p.ring(k)
            s = z * 4 + p.quad
            recv(t, 24 + z, r2.at[z])
            add(t, s, r2[z])
            remote(acc.at[s], r3.at[k], ssem.at[t, 28 + k], rsem.at[t, 28 + k], p.up(k)).start()
        recv(t, 24 + p.z, r2.at[p.z])

    def stage3(t):
        acc, r2, r3 = buf(0, t), buf(3, t), buf(4, t)
        total = acc[p.me].astype(jnp.float32) + r2[p.z].astype(jnp.float32)
        for k in range(1, 4):
            recv(t, 28 + k, r3.at[k])
            total = total + r3[k].astype(jnp.float32)
        view = result(t, c)
        view[...] = total
        remote(view, view, ssem.at[t, 28], rsem.at[t, 28], p.sib()).start()

    ahead = AHEAD
    for t in order[:ahead]:
        share(t)
    for step in range(groups + 3):
        if step + ahead < groups:
            share(order[step + ahead])
        for lag, stage in enumerate((stage0, stage1, stage2, stage3)):
            if 0 <= step - lag < groups:
                stage(order[step - lag])
    for copy in theirs:
        copy.start()
    for copy in theirs:
        copy.wait_send()
    remote(p_rows, p_out.at[1 - c], xsem.at[2], xsem.at[3], p.sib()).wait_recv()
    remote(q_rows, q_out.at[1 - c], xsem.at[4], xsem.at[5], p.sib()).wait_recv()
    for copy in mine:
        copy.wait()
    for t in order:
        recv(t, 28, result(t, 1 - c))
        acc = buf(0, t)
        @pl.loop(0, 28)
        def _(k):
            remote(acc.at[0], acc.at[0], ssem.at[t, k], rsem.at[t, k], p.sib()).wait_send()
        for k in range(1, 4):
            remote(acc.at[0], acc.at[0], ssem.at[t, 28 + k], rsem.at[t, 28 + k], p.sib()).wait_send()
        remote(result(t, c), result(t, c), ssem.at[t, 28], rsem.at[t, 28], p.sib()).wait_send()


def scatter_all(inner, cut, vec, ga, gi, go, dx, cid=1):
    f32, bf = jnp.float32, jnp.bfloat16
    groups = cut.count + 1
    scratch = []
    for count in (16, 16, 8, 4, 4):
        scratch.append(pltpu.VMEM((count, 16, 128), f32))
        scratch += [pltpu.VMEM((cut.each, count) + cut.shape(kind), bf) for kind in range(3)]
    return pl.pallas_call(
        functools.partial(scatter_kernel, inner, cut),
        out_shape=(
            jax.ShapeDtypeStruct((16, 256), f32),
            jax.ShapeDtypeStruct((4, 48, 768), f32),
            jax.ShapeDtypeStruct((48, 3072), f32),
            jax.ShapeDtypeStruct((192, 768), f32),
            jax.ShapeDtypeStruct((2, Q, 768), f32),
            jax.ShapeDtypeStruct((2, S, 768), f32),
        ),
        in_specs=[ANY] * 5,
        out_specs=[VM] * 4 + [ANY] * 2,
        scratch_shapes=scratch + [
            pltpu.SemaphoreType.DMA((groups, 32)),
            pltpu.SemaphoreType.DMA((groups, 32)),
            pltpu.SemaphoreType.DMA((groups,)),
            pltpu.SemaphoreType.DMA((6,)),
        ],
        compiler_params=pltpu.CompilerParams(collective_id=cid, has_side_effects=True, vmem_limit_bytes=56 << 20),
        name="scatter_grads",
    )(vec, ga, gi, go, dx)


S, Q = 512, 64
T = S + Q


def dot(left, right):
    return jnp.dot(left, right, preferred_element_type=jnp.float32)


def dot_nt(left, right):
    return lax.dot_general(left, right, (((1,), (1,)), ((), ())), preferred_element_type=jnp.float32)


def block(index, size):
    return pl.ds(pl.multiple_of(index * size, size), size)


def low(x):
    return x.astype(jnp.bfloat16)


def wide(x):
    return x.astype(jnp.float32)


def head_mask(h):
    lane = lax.broadcasted_iota(jnp.int32, (1, 128), 1)
    return low(jnp.where(lane // 64 == h, 1.0, 0.0))


SPANS = ((0, S, 256), (S, Q, Q))


def forward_kernel(lens, x, vec, a_hbm, i_hbm, o_hbm,
                   q, k, v, prob, prob_q, x_t, q_t, ctx_t, norm_t, act_t, slope, y1, r1, y2, r2, pooled,
                   wa, wi, wo, ctx, normed, act, sem):
    loads = [pltpu.make_async_copy(a_hbm, wa, sem.at[0]), pltpu.make_async_copy(i_hbm, wi, sem.at[1]), pltpu.make_async_copy(o_hbm, wo, sem.at[2])]
    for load in loads:
        load.start()
    x_t[...] = x[...].T
    loads[0].wait()
    for m, (out, row) in enumerate(((q, 0), (k, None), (v, 1))):
        @pl.loop(0, 3)
        def _(n):
            cols = block(n, 256)
            acc = dot(x[...], wa[m, :, cols])
            if row is not None:
                acc = acc + vec[row : row + 1, cols]
            out[:, cols] = low(acc)
    q_t[...] = q[...].T

    @pl.loop(0, 6)
    def _(j):
        cols = block(j, 128)
        for (start, size, rb), probs, length in zip(SPANS, (prob, prob_q), (lens[0], lens[1])):
            rows = slice(start, start + size)
            kp, vp = k[rows, cols], v[rows, cols]
            valid = lax.broadcasted_iota(jnp.int32, (1, size), 1) < length
            for r in range(0, size, rb):
                qp = q[start + r : start + r + rb, cols]
                total = None
                for h in range(2):
                    mask = head_mask(h)
                    scores = dot_nt(qp * (mask * 0.125), kp)
                    scores = jnp.where(valid, scores, -1e9)
                    e = jnp.exp(scores - jnp.max(scores, axis=1, keepdims=True))
                    p = low(e * (1.0 / jnp.sum(e, axis=1, keepdims=True)))
                    probs[2 * j + h, r : r + rb] = p
                    part = dot(p, vp * mask)
                    total = part if total is None else total + part
                ctx[start + r : start + r + rb, cols] = low(total)
    ctx_t[...] = ctx[...].T

    @pl.loop(0, 3)
    def _(n):
        rows = block(n, 192)
        first = wide(x[rows]) + (dot(ctx[rows], wa[3]) + vec[2:3, :768])
        center = first - jnp.mean(first, axis=1, keepdims=True)
        scale = lax.rsqrt(jnp.mean(center * center, axis=1, keepdims=True) + 1e-12)
        y = center * scale
        y1[rows] = y
        r1[rows] = scale
        normed[rows] = low(y * vec[4:5, :768] + vec[5:6, :768])
    norm_t[...] = normed[...].T
    loads[1].wait()

    @pl.loop(0, 12)
    def _(n):
        cols = block(n, 256)
        u = dot(normed[...], wi[:, cols]) + vec[8:9, cols]
        cdf = 0.5 * (1.0 + lax.erf(u * 0.7071067811865476))
        a = low(u * cdf)
        act[:, cols] = a
        act_t[cols] = a.T
        slope[:, cols] = low(cdf + u * (0.3989422804014327 * jnp.exp(-0.5 * u * u)))
    loads[2].wait()
    pooled[...] = jnp.zeros_like(pooled)

    @pl.loop(0, 3)
    def _(n):
        rows = block(n, 192)
        second = y1[rows] * vec[4:5, :768] + vec[5:6, :768] + (dot(act[rows], wo[...]) + vec[3:4, :768])
        center = second - jnp.mean(second, axis=1, keepdims=True)
        scale = lax.rsqrt(jnp.mean(center * center, axis=1, keepdims=True) + 1e-12)
        y = center * scale
        y2[rows] = y
        r2[rows] = scale
        out = y * vec[6:7, :768] + vec[7:8, :768]
        at = lax.broadcasted_iota(jnp.int32, (192, 1), 0) + n * 192
        for row, keep in ((0, (at >= S) & (at - S < lens[1])), (1, (at < S) & (at < lens[0]))):
            pooled[row : row + 1] += jnp.sum(jnp.where(keep, out, 0.0), axis=0, keepdims=True)
    pooled[0:1] = pooled[0:1] / wide(jnp.full((1, 1), lens[1], jnp.int32))
    pooled[1:2] = pooled[1:2] / wide(jnp.full((1, 1), lens[0], jnp.int32))


def forward_call(lens, x, vec, wa, wi, wo):
    bf, f32 = jnp.bfloat16, jnp.float32
    sds = jax.ShapeDtypeStruct
    outs = [sds((T, 768), bf)] * 3 + [sds((12, S, S), bf), sds((12, Q, Q), bf)] + [sds((768, T), bf)] * 4 + [
        sds((3072, T), bf), sds((T, 3072), bf), sds((T, 768), f32), sds((T, 1), f32), sds((T, 768), f32), sds((T, 1), f32), sds((2, 768), f32)]
    return pl.pallas_call(
        forward_kernel,
        out_shape=outs,
        in_specs=[pl.BlockSpec(memory_space=pltpu.SMEM), VM, VM, ANY, ANY, ANY],
        out_specs=[VM] * len(outs),
        scratch_shapes=[
            pltpu.VMEM((4, 768, 768), bf), pltpu.VMEM((768, 3072), bf), pltpu.VMEM((3072, 768), bf),
            pltpu.VMEM((T, 768), bf), pltpu.VMEM((T, 768), bf), pltpu.VMEM((T, 3072), bf), pltpu.SemaphoreType.DMA((3,))],
        compiler_params=pltpu.CompilerParams(vmem_limit_bytes=60 << 20),
        name="layer_forward",
    )(lens, x, vec, wa, wi, wo)


def backward_kernel(lens, d_pool, vec, a_hbm, i_hbm, o_hbm, q, k, v, prob_hbm, prob_q, x_t, q_t, ctx_t, norm_t, act_t, slope, y1, r1, y2, r2,
                    d_x, d_vec, ga, gi, go,
                    wa, wi, wo, prob, stage, d_second, d_low, d_inner, d_ctx, d_ctx_t, dq, dk, dv, t_k, t_v, ds_buf, sem, gsem):
    loads = [pltpu.make_async_copy(o_hbm, wo, sem.at[0]), pltpu.make_async_copy(i_hbm, wi, sem.at[1]),
             pltpu.make_async_copy(a_hbm, wa, sem.at[2]), pltpu.make_async_copy(prob_hbm, prob, sem.at[3])]
    for load in loads:
        load.start()
    d_vec[...] = jnp.zeros_like(d_vec)

    def gain(row):
        return vec[row : row + 1, :768]

    def tally(row, value):
        d_vec[row : row + 1, :768] += jnp.sum(value, axis=0, keepdims=True)

    written = []

    def emit(value, target):
        i = len(written)
        if i >= 2:
            written[i - 2].wait()
        stage[i % 2] = low(value)
        copy = pltpu.make_async_copy(stage.at[i % 2], target, gsem.at[i % 2])
        copy.start()
        written.append(copy)

    len_p, len_q = lens[0], lens[1]
    pool_q = d_pool[0:1] / wide(jnp.full((1, 1), len_q, jnp.int32))
    pool_p = d_pool[1:2] / wide(jnp.full((1, 1), len_p, jnp.int32))

    @pl.loop(0, 3)
    def _(n):
        rows = block(n, 192)
        at = lax.broadcasted_iota(jnp.int32, (192, 1), 0) + n * 192
        d_rows = jnp.where(at < S, jnp.where(at < len_p, pool_p, 0.0), jnp.where(at - S < len_q, pool_q, 0.0))
        y = y2[rows]
        tally(6, d_rows * y)
        tally(7, d_rows)
        g = d_rows * gain(6)
        d = (g - jnp.mean(g, axis=1, keepdims=True) - y * jnp.mean(g * y, axis=1, keepdims=True)) * r2[rows]
        d_second[rows] = d
        d_low[rows] = low(d)
        tally(3, wide(low(d)))

    for n in range(4):
        emit(dot(act_t[n * 768 : (n + 1) * 768], d_low[...]), go.at[pl.ds(n * 768, 768)])
    loads[0].wait()

    @pl.loop(0, 12)
    def _(n):
        cols = block(n, 256)
        d = low(dot_nt(d_low[...], wo[cols]) * wide(slope[:, cols]))
        d_inner[:, cols] = d
        d_vec[8:9, cols] = jnp.sum(wide(d), axis=0, keepdims=True)

    for n in range(4):
        cols = slice(n * 768, (n + 1) * 768)
        emit(dot(norm_t[...], d_inner[:, cols]), gi.at[:, pl.ds(n * 768, 768)])
    loads[1].wait()

    @pl.loop(0, 3)
    def _(n):
        rows = block(n, 192)
        d_normed = d_second[rows] + dot_nt(d_inner[rows], wi[...])
        y = y1[rows]
        tally(4, d_normed * y)
        tally(5, d_normed)
        g = d_normed * gain(4)
        d = (g - jnp.mean(g, axis=1, keepdims=True) - y * jnp.mean(g * y, axis=1, keepdims=True)) * r1[rows]
        d_second[rows] = d
        d_low[rows] = low(d)
        tally(2, wide(low(d)))

    emit(dot(ctx_t[...], d_low[...]), ga.at[3])
    loads[2].wait()

    @pl.loop(0, 3)
    def _(n):
        rows = block(n, 192)
        d_ctx[rows] = low(dot_nt(d_low[rows], wa[3]))
    d_ctx_t[...] = d_ctx[...].T
    loads[3].wait()

    @pl.loop(0, 6)
    def _(j):
        cols = block(j, 128)
        for (start, size, rb), probs in zip(SPANS, (prob, prob_q)):
            rows = slice(start, start + size)
            kp, vp = k[rows, cols], v[rows, cols]
            dq_parts = [None] * (size // rb)
            for h in range(2):
                mask = head_mask(h)
                for r in range(0, size, rb):
                    d_p = dot_nt(d_ctx[start + r : start + r + rb, cols] * mask, vp)
                    p = wide(probs[2 * j + h, r : r + rb])
                    ds = low(p * (d_p - jnp.sum(p * d_p, axis=1, keepdims=True)))
                    ds_buf[h, r : r + rb, :size] = ds
                    part = dot(ds, kp * mask)
                    i = r // rb
                    dq_parts[i] = part if dq_parts[i] is None else dq_parts[i] + part
                head = block(2 * j + h, 64)
                t_v[head, rows] = low(dot(d_ctx_t[head, rows], probs[2 * j + h]))
                t_k[head, rows] = low(dot(q_t[head, rows], ds_buf[h, :size, :size]) * 0.125)
            for i, part in enumerate(dq_parts):
                dq[start + i * rb : start + (i + 1) * rb, cols] = low(part * 0.125)
    dk[...] = t_k[...].T
    dv[...] = t_v[...].T
    for n, d in enumerate((dq, dk, dv)):
        emit(dot(x_t[...], d[...]), ga.at[n])
    tally(0, wide(dq[...]))
    tally(1, wide(dv[...]))

    @pl.loop(0, 3)
    def _(n):
        rows = block(n, 192)
        d_x[rows] = d_second[rows] + dot_nt(dq[rows], wa[0]) + dot_nt(dk[rows], wa[1]) + dot_nt(dv[rows], wa[2])
    for copy in written[-2:]:
        copy.wait()


def backward_call(lens, d_pool, vec, wa, wi, wo, saved):
    bf, f32 = jnp.bfloat16, jnp.float32
    sds = jax.ShapeDtypeStruct
    outs = [sds((T, 768), f32), sds((16, 3072), f32), sds((4, 768, 768), bf), sds((768, 3072), bf), sds((3072, 768), bf)]
    specs = [VM] * 15
    specs[3] = ANY
    return pl.pallas_call(
        backward_kernel,
        out_shape=outs,
        in_specs=[pl.BlockSpec(memory_space=pltpu.SMEM), VM, VM, ANY, ANY, ANY] + specs,
        out_specs=[VM, VM, ANY, ANY, ANY],
        scratch_shapes=[
            pltpu.VMEM((4, 768, 768), bf), pltpu.VMEM((768, 3072), bf), pltpu.VMEM((3072, 768), bf),
            pltpu.VMEM((12, S, S), bf), pltpu.VMEM((2, 768, 768), bf), pltpu.VMEM((T, 768), f32), pltpu.VMEM((T, 768), bf),
            pltpu.VMEM((T, 3072), bf), pltpu.VMEM((T, 768), bf), pltpu.VMEM((768, T), bf)]
            + [pltpu.VMEM((T, 768), bf)] * 3 + [pltpu.VMEM((768, T), bf)] * 2 + [pltpu.VMEM((2, S, S), bf),
            pltpu.SemaphoreType.DMA((4,)), pltpu.SemaphoreType.DMA((2,))],
        compiler_params=pltpu.CompilerParams(vmem_limit_bytes=62 << 20),
        name="layer_backward",
    )(lens, d_pool, vec, wa, wi, wo, *saved)


def loss_kernel(pooled, targets, seq, d_pool, loss, rows, ssem, rsem):
    pairs = targets.shape[0]
    me = lax.axis_index("dp") * 2 + lax.axis_index("tower")

    def device(at):
        return {"dp": at // 2, "tower": lax.rem(at, 2)}

    sem = pltpu.get_barrier_semaphore()

    @pl.loop(1, pairs)
    def _(k):
        pl.semaphore_signal(sem, inc=1, device_id=device(lax.rem(me + k, pairs)), device_id_type=MESH)
    mine = pooled[...]
    root = jnp.sqrt(jnp.sum(mine * mine, axis=1, keepdims=True) + 1e-6)
    unit = mine / root
    rows[me] = unit
    pl.semaphore_wait(sem, pairs - 1)

    @pl.loop(1, pairs)
    def _(k):
        remote(rows.at[me], rows.at[me], ssem, rsem, device(lax.rem(me + k, pairs))).start()
    rest = rows.at[pl.ds(0, pairs - 1)]
    remote(rest, rest, ssem, rsem, device(me)).wait_recv()
    remote(rest, rest, ssem, rsem, device(me)).wait_send()
    exact = lax.Precision.HIGHEST
    qs, ps = rows[:, 0, :], rows[:, 1, :]
    logits = lax.dot_general(qs, ps, (((1,), (1,)), ((), ())), precision=exact, preferred_element_type=jnp.float32) / 0.01
    hit = targets[...] == lax.broadcasted_iota(jnp.int32, (pairs, pairs), 1)
    top = jnp.max(logits, axis=1, keepdims=True)
    lse = jnp.log(jnp.sum(jnp.exp(logits - top), axis=1, keepdims=True)) + top
    picked = jnp.sum(jnp.where(hit, logits, 0.0), axis=1, keepdims=True)
    loss[...] = jnp.broadcast_to(jnp.sum(lse - picked, axis=0, keepdims=True) / pairs, loss.shape)
    d_logits = seq * (jnp.exp(logits - lse) - jnp.where(hit, 1.0, 0.0))
    d_q = jnp.dot(d_logits, ps, precision=exact, preferred_element_type=jnp.float32) / 0.01
    d_p = lax.dot_general(d_logits, qs, (((0,), (0,)), ((), ())), precision=exact, preferred_element_type=jnp.float32) / 0.01
    own = lax.broadcasted_iota(jnp.int32, (pairs, 1), 0) == me
    for row, d in enumerate((d_q, d_p)):
        d_unit = jnp.sum(jnp.where(own, d, 0.0), axis=0, keepdims=True)
        u = unit[row : row + 1]
        d_pool[row : row + 1] = (d_unit - u * jnp.sum(u * d_unit, axis=1, keepdims=True)) / root[row : row + 1]


def loss_call(pooled, targets, seq, cid=2):
    pairs = targets.shape[0]
    return pl.pallas_call(
        lambda *refs: loss_kernel(refs[0], refs[1], float(seq), *refs[2:]),
        out_shape=(jax.ShapeDtypeStruct((2, 768), jnp.float32), jax.ShapeDtypeStruct((8, 128), jnp.float32)),
        in_specs=[VM] * 2,
        out_specs=[VM] * 2,
        scratch_shapes=[pltpu.VMEM((pairs, 2, 768), jnp.float32), pltpu.SemaphoreType.DMA, pltpu.SemaphoreType.DMA],
        compiler_params=pltpu.CompilerParams(collective_id=cid, has_side_effects=True),
        name="pair_loss",
    )(pooled, targets)


CUT = Cut(1)


def group_rows(x, groups):
    if groups is None:
        return x
    return lax.all_gather(x, "dp", axis=0, tiled=True, axis_index_groups=groups)


def per_device(
    query_tokens, passage_tokens, lengths, positives,
    query_weight, key_weight, value_weight, output_weight, inner_weight, outer_weight,
    query_bias, value_bias, output_bias, inner_bias, outer_bias,
    first_gain, first_shift, second_gain, second_shift,
):
    inner = lax.axis_size("dp") // 16
    groups = None if inner == 1 else [[h * inner + i for i in range(inner)] for h in range(16)]
    tower = lax.axis_index("tower")
    seq = passage_tokens.shape[1]

    def fetch(w):
        return group_rows(w, groups)

    wa = jnp.stack([fetch(w) for w in (query_weight, key_weight, value_weight, output_weight)])
    narrow = [fetch(w) for w in (query_bias, value_bias, output_bias, outer_bias, first_gain, first_shift, second_gain, second_shift)]
    vec = jnp.stack([jnp.pad(w, (0, 256 - w.shape[0])) for w in narrow + [fetch(inner_bias)]])
    vec = jnp.pad(vec, ((0, 7), (0, 0)))
    lens = jnp.pad(lengths, ((0, 7), (0, 126)))
    gv, ga, gi, go, gl = gather_all(inner, CUT, vec, wa, fetch(inner_weight), fetch(outer_weight), lens)
    full = jnp.pad(jnp.swapaxes(gv[:, :8, :48], 0, 1).reshape(8, 768), ((0, 0), (0, 2304)))
    full = jnp.pad(jnp.concatenate([full, gv[:, 8, :192].reshape(1, 3072)]), ((0, 7), (0, 0))).astype(jnp.float32)
    pair = lax.dynamic_index_in_dim(gl[:, 0, :2], tower, 1, keepdims=False)
    own = jnp.stack([pair[1], pair[0]])
    x = jnp.concatenate([
        lax.dynamic_index_in_dim(passage_tokens, tower, 0, keepdims=False),
        lax.dynamic_index_in_dim(query_tokens, tower, 0, keepdims=False),
    ])
    *saved, pooled = forward_call(own, x, full, ga, gi, go)
    d_pool, loss = loss_call(pooled, positives[:, None], seq)
    d_x, d_vec, da, di, do = backward_call(own, d_pool, full, ga, gi, go, saved)
    pv = jnp.swapaxes(d_vec[:8, :768].reshape(8, 16, 48), 0, 1)
    pv = jnp.pad(pv, ((0, 0), (0, 0), (0, 208)))
    pi = jnp.pad(d_vec[8].reshape(16, 1, 192), ((0, 0), (0, 7), (0, 64)))
    rv, ra, ri, ro, query_grads, passage_grads = scatter_all(inner, CUT, jnp.concatenate([pv, pi], axis=1), da, di, do, d_x)

    def finish(x):
        if groups is None:
            return x
        return lax.psum_scatter(x, "dp", scatter_dimension=0, tiled=True, axis_index_groups=groups)

    grads = [finish(ra[i]) for i in range(4)] + [finish(ri), finish(ro)]
    flat = [finish(rv[i, :48]) for i in range(8)] + [finish(rv[8, :192])]
    grads += [flat[0], flat[1], flat[2], flat[8], flat[3], flat[4], flat[5], flat[6], flat[7]]
    return (loss[0, 0], query_grads, passage_grads) + tuple(grads)


def solution(mesh):
    rows3, rows2, rows1 = P("dp", None, None), P("dp", None), P("dp")
    return jax.shard_map(
        per_device,
        mesh=mesh,
        in_specs=(rows3, rows3, P("tower", "dp"), P()) + (rows2,) * 6 + (rows1,) * 9,
        out_specs=(P(), rows3, rows3) + (rows2,) * 6 + (rows1,) * 9,
        check_vma=False,
    )
```

```python
import functools

import jax
import jax.numpy as jnp
from jax import lax
from jax.experimental import pallas as pl
from jax.experimental.pallas import tpu as pltpu
from jax.sharding import PartitionSpec as P

MESH = pl.DeviceIdType.MESH
ANY = pl.BlockSpec(memory_space=pl.ANY)
VM = pl.BlockSpec(memory_space=pltpu.VMEM)


class Place:
    def __init__(self, inner):
        dp = lax.axis_index("dp")
        self.c = lax.axis_index("tower")
        self.inner = inner
        self.low = lax.rem(dp, inner)
        self.me = dp // inner
        self.z = self.me // 4
        self.quad = lax.rem(self.me, 4)
        s1 = 1 + self.c
        s2 = 2 - self.c
        b1 = lax.rem(self.quad // s1, 2)
        b2 = lax.rem(self.quad // s2, 2)
        self.q1 = self.quad + s1 * (1 - 2 * b1)
        self.q2 = self.quad + s2 * (1 - 2 * b2)
        self.q12 = 3 - self.quad
        self.quads = (self.quad, self.q1, self.q2, self.q12)

    def ring(self, k):
        return lax.rem(self.z + k, 4)

    def dev(self, group):
        return {"dp": group * self.inner + self.low, "tower": self.c}

    def n1(self):
        return self.dev(self.z * 4 + self.q1)

    def n2(self):
        return self.dev(self.z * 4 + self.q2)

    def up(self, k):
        return self.dev(self.ring(k) * 4 + self.quad)

    def sib(self):
        return {"dp": self.me * self.inner + self.low, "tower": 1 - self.c}

    def barrier(self):
        sem = pltpu.get_barrier_semaphore()
        for target in (self.up(1), self.up(2), self.up(3), self.n1(), self.n2(), self.sib()):
            pl.semaphore_signal(sem, inc=1, device_id=target, device_id_type=MESH)
        pl.semaphore_wait(sem, 6)


def remote(src, dst, send_sem, recv_sem, target):
    return pltpu.make_async_remote_copy(
        src_ref=src, dst_ref=dst, send_sem=send_sem, recv_sem=recv_sem, device_id=target, device_id_type=MESH
    )


class Cut:
    def __init__(self, per):
        self.per = per
        self.each = 4 // per
        self.count = 3 * self.each

    def kind(self, g):
        return g // self.each, g % self.each

    def shape(self, kind):
        per = self.per
        return ((per, 48, 384), (48, 384 * per), (48 * per, 384))[kind]

    def whole(self, refs, g, s, which):
        per = self.per
        kind, n = self.kind(g)
        ref = refs[kind]
        if kind == 0:
            return ref.at[pl.ds(n * per, per), pl.ds(pl.multiple_of(s * 48, 16), 48), pl.ds(pl.multiple_of(which * 384, 128), 384)]
        if kind == 1:
            return ref.at[pl.ds(pl.multiple_of(s * 48, 16), 48), pl.ds(pl.multiple_of((2 * n + which) * 384 * per, 128), 384 * per)]
        return ref.at[pl.ds(pl.multiple_of(s * 192 + n * 48 * per, 16), 48 * per), pl.ds(pl.multiple_of(which * 384, 128), 384)]

    def shard(self, refs, g, which):
        per = self.per
        kind, n = self.kind(g)
        ref = refs[kind]
        if kind == 0:
            return ref.at[pl.ds(n * per, per), :, pl.ds(pl.multiple_of(which * 384, 128), 384)]
        if kind == 1:
            return ref.at[:, pl.ds(pl.multiple_of((2 * n + which) * 384 * per, 128), 384 * per)]
        return ref.at[pl.ds(n * 48 * per, 48 * per), pl.ds(pl.multiple_of(which * 384, 128), 384)]


def gather_kernel(inner, cut, v_in, a_in, i_in, o_in, len_in, v_out, a_out, i_out, o_out, len_out, ssem, rsem, lsem, xsem):
    p = Place(inner)
    c = p.c
    groups = cut.count + 1
    ins = (a_in, i_in, o_in)
    outs = (a_out, i_out, o_out)
    local = [pltpu.make_async_copy(len_in, len_out.at[c], lsem.at[0]), pltpu.make_async_copy(v_in, v_out.at[p.me], lsem.at[1])]
    rows = pl.ds(pl.multiple_of(p.me * 48, 16), 48)
    local.append(pltpu.make_async_copy(a_in, a_out.at[:, rows], lsem.at[2]))
    local.append(pltpu.make_async_copy(i_in, i_out.at[rows], lsem.at[3]))
    local.append(pltpu.make_async_copy(o_in, o_out.at[pl.ds(pl.multiple_of(p.me * 192, 16), 192)], lsem.at[4]))
    for copy in local:
        copy.start()
    p.barrier()

    def slot(t, s, which):
        if t == 0:
            return v_out.at[s, :, pl.ds(pl.multiple_of(which * 128, 128), 128)]
        return cut.whole(outs, t - 1, s, which)

    def own(t):
        if t == 0:
            return v_in.at[:, pl.ds(pl.multiple_of(c * 128, 128), 128)]
        return cut.shard(ins, t - 1, c)

    lens = remote(len_in, len_out.at[c], xsem.at[0], xsem.at[1], p.sib())
    lens.start()

    def push(t, src, s, k, target):
        remote(src, slot(t, s, c), ssem.at[t, k], rsem.at[t, k], target).start()

    def arrived(t, s, k, which):
        view = slot(t, s, which)
        remote(view, view, ssem.at[t, k], rsem.at[t, k], p.sib()).wait_recv()

    def shard(k, q):
        return p.ring(4 - k) * 4 + p.quads[q]

    def stage_own(t):
        for k in range(1, 4):
            push(t, own(t), p.me, k, p.up(k))
        push(t, own(t), p.me, 4, p.n1())
        push(t, own(t), p.me, 8, p.n2())

    def stage_z(t):
        for k in range(1, 4):
            s = shard(k, 0)
            arrived(t, s, k, c)
            view = slot(t, s, c)
            push(t, view, s, 4 + k, p.n1())
            push(t, view, s, 8 + k, p.n2())
            push(t, view, s, 16 + k, p.sib())

    def stage_one(t):
        for k in range(4):
            s = shard(k, 1)
            arrived(t, s, 4 + k, c)
            view = slot(t, s, c)
            push(t, view, s, 12 + k, p.n2())
            push(t, view, s, 20 + k, p.sib())

    def stage_two(t):
        for q in (2, 3):
            for k in range(4):
                s = shard(k, q)
                arrived(t, s, q * 4 + k, c)
                view = slot(t, s, c)
                push(t, view, s, 16 + q * 4 + k, p.sib())

    ahead = AHEAD
    for t in range(ahead):
        stage_own(t)
    for step in range(groups + 2):
        if step < groups:
            stage_z(step)
        if step + ahead < groups:
            stage_own(step + ahead)
        if 0 <= step - 1 < groups:
            stage_one(step - 1)
        if 0 <= step - 2 < groups:
            stage_two(step - 2)

    for t in range(groups):
        for q in range(4):
            sq = (0, 2, 1, 3)[q]
            for k in range(4):
                if q == 0 and k == 0:
                    continue
                s = shard(k, sq)
                arrived(t, s, 16 + q * 4 + k, 1 - c)
    for t in range(groups):
        for k in range(1, 32):
            if k == 16:
                continue
            view = slot(t, p.me, c)
            remote(view, view, ssem.at[t, k], rsem.at[t, k], p.sib()).wait_send()
    for copy in local:
        copy.wait()
    lens.wait_send()
    remote(len_in, len_out.at[1 - c], xsem.at[0], xsem.at[1], p.sib()).wait_recv()

AHEAD = 1

def gather_all(inner, cut, vec, wa, wi, wo, lens, cid=0):
    bf = jnp.bfloat16
    groups = cut.count + 1
    return pl.pallas_call(
        functools.partial(gather_kernel, inner, cut),
        out_shape=(
            jax.ShapeDtypeStruct((16,) + vec.shape, bf),
            jax.ShapeDtypeStruct((4, 768, 768), bf),
            jax.ShapeDtypeStruct((768, 3072), bf),
            jax.ShapeDtypeStruct((3072, 768), bf),
            jax.ShapeDtypeStruct((2,) + lens.shape, jnp.int32),
        ),
        in_specs=[ANY] * 5,
        out_specs=[ANY] * 5,
        scratch_shapes=[
            pltpu.SemaphoreType.DMA((groups, 32)),
            pltpu.SemaphoreType.DMA((groups, 32)),
            pltpu.SemaphoreType.DMA((5,)),
            pltpu.SemaphoreType.DMA((2,)),
        ],
        compiler_params=pltpu.CompilerParams(collective_id=cid, has_side_effects=True),
        name="gather_weights",
    )(vec, wa, wi, wo, lens)


S, Q = 512, 64
T = S + Q


def dot(left, right):
    return jnp.dot(left, right, preferred_element_type=jnp.float32)


def dot_nt(left, right):
    return lax.dot_general(left, right, (((1,), (1,)), ((), ())), preferred_element_type=jnp.float32)


def block(index, size):
    return pl.ds(pl.multiple_of(index * size, size), size)


def low(x):
    return x.astype(jnp.bfloat16)


def wide(x):
    return x.astype(jnp.float32)


def head_mask(h):
    lane = lax.broadcasted_iota(jnp.int32, (1, 128), 1)
    return low(jnp.where(lane // 64 == h, 1.0, 0.0))


SPANS = ((0, S, 256), (S, Q, Q))


def forward_kernel(lens, x, vec, a_hbm, i_hbm, o_hbm,
                   q, k, v, prob, prob_q, x_t, q_t, ctx_t, norm_t, act_t, slope, y1, r1, y2, r2, pooled,
                   wa, wi, wo, ctx, normed, act, sem):
    loads = [pltpu.make_async_copy(a_hbm, wa, sem.at[0]), pltpu.make_async_copy(i_hbm, wi, sem.at[1]), pltpu.make_async_copy(o_hbm, wo, sem.at[2])]
    for load in loads:
        load.start()
    x_t[...] = x[...].T
    loads[0].wait()
    for m, (out, row) in enumerate(((q, 0), (k, None), (v, 1))):
        @pl.loop(0, 3)
        def _(n):
            cols = block(n, 256)
            acc = dot(x[...], wa[m, :, cols])
            if row is not None:
                acc = acc + vec[row : row + 1, cols]
            out[:, cols] = low(acc)
    q_t[...] = q[...].T

    @pl.loop(0, 6)
    def _(j):
        cols = block(j, 128)
        for (start, size, rb), probs, length in zip(SPANS, (prob, prob_q), (lens[0], lens[1])):
            rows = slice(start, start + size)
            kp, vp = k[rows, cols], v[rows, cols]
            valid = lax.broadcasted_iota(jnp.int32, (1, size), 1) < length
            for r in range(0, size, rb):
                qp = q[start + r : start + r + rb, cols]
                total = None
                for h in range(2):
                    mask = head_mask(h)
                    scores = dot_nt(qp * (mask * 0.125), kp)
                    scores = jnp.where(valid, scores, -1e9)
                    e = jnp.exp(scores - jnp.max(scores, axis=1, keepdims=True))
                    p = low(e * (1.0 / jnp.sum(e, axis=1, keepdims=True)))
                    probs[2 * j + h, r : r + rb] = p
                    part = dot(p, vp * mask)
                    total = part if total is None else total + part
                ctx[start + r : start + r + rb, cols] = low(total)
    ctx_t[...] = ctx[...].T

    @pl.loop(0, 3)
    def _(n):
        rows = block(n, 192)
        first = wide(x[rows]) + (dot(ctx[rows], wa[3]) + vec[2:3, :768])
        center = first - jnp.mean(first, axis=1, keepdims=True)
        scale = lax.rsqrt(jnp.mean(center * center, axis=1, keepdims=True) + 1e-12)
        y = center * scale
        y1[rows] = y
        r1[rows] = scale
        normed[rows] = low(y * vec[4:5, :768] + vec[5:6, :768])
    norm_t[...] = normed[...].T
    loads[1].wait()

    @pl.loop(0, 12)
    def _(n):
        cols = block(n, 256)
        u = dot(normed[...], wi[:, cols]) + vec[8:9, cols]
        cdf = 0.5 * (1.0 + lax.erf(u * 0.7071067811865476))
        a = low(u * cdf)
        act[:, cols] = a
        slope[:, cols] = low(cdf + u * (0.3989422804014327 * jnp.exp(-0.5 * u * u)))
    for b in range(4):
        turned = act[:, b * 768 : (b + 1) * 768].T
        for s in range(4):
            for n in range(4):
                row = n * 768 + (b * 4 + s) * 48
                act_t[row : row + 48] = turned[s * 192 + n * 48 : s * 192 + n * 48 + 48]
    loads[2].wait()
    pooled[...] = jnp.zeros_like(pooled)

    @pl.loop(0, 3)
    def _(n):
        rows = block(n, 192)
        second = y1[rows] * vec[4:5, :768] + vec[5:6, :768] + (dot(act[rows], wo[...]) + vec[3:4, :768])
        center = second - jnp.mean(second, axis=1, keepdims=True)
        scale = lax.rsqrt(jnp.mean(center * center, axis=1, keepdims=True) + 1e-12)
        y = center * scale
        y2[rows] = y
        r2[rows] = scale
        out = y * vec[6:7, :768] + vec[7:8, :768]
        at = lax.broadcasted_iota(jnp.int32, (192, 1), 0) + n * 192
        for row, keep in ((0, (at >= S) & (at - S < lens[1])), (1, (at < S) & (at < lens[0]))):
            pooled[row : row + 1] += jnp.sum(jnp.where(keep, out, 0.0), axis=0, keepdims=True)
    pooled[0:1] = pooled[0:1] / wide(jnp.full((1, 1), lens[1], jnp.int32))
    pooled[1:2] = pooled[1:2] / wide(jnp.full((1, 1), lens[0], jnp.int32))


def forward_call(lens, x, vec, wa, wi, wo):
    bf, f32 = jnp.bfloat16, jnp.float32
    sds = jax.ShapeDtypeStruct
    outs = [sds((T, 768), bf)] * 3 + [sds((12, S, S), bf), sds((12, Q, Q), bf)] + [sds((768, T), bf)] * 4 + [
        sds((3072, T), bf), sds((T, 3072), bf), sds((T, 768), f32), sds((T, 1), f32), sds((T, 768), f32), sds((T, 1), f32), sds((2, 768), f32)]
    return pl.pallas_call(
        forward_kernel,
        out_shape=outs,
        in_specs=[pl.BlockSpec(memory_space=pltpu.SMEM), VM, VM, ANY, ANY, ANY],
        out_specs=[VM] * len(outs),
        scratch_shapes=[
            pltpu.VMEM((4, 768, 768), bf), pltpu.VMEM((768, 3072), bf), pltpu.VMEM((3072, 768), bf),
            pltpu.VMEM((T, 768), bf), pltpu.VMEM((T, 768), bf), pltpu.VMEM((T, 3072), bf), pltpu.SemaphoreType.DMA((3,))],
        compiler_params=pltpu.CompilerParams(vmem_limit_bytes=60 << 20),
        name="layer_forward",
    )(lens, x, vec, wa, wi, wo)


class Scatter:
    def __init__(self, p, refs, result):
        self.p = p
        self.stage, self.r0, self.acc, self.r1, self.r2, self.r3, self.ssem, self.rsem = refs
        self.result = result
        self.own = pl.ds(pl.multiple_of(p.c * 384, 128), 384)
        self.other = pl.ds(pl.multiple_of((1 - p.c) * 384, 128), 384)

    def copy(self, src, dst, e, k, target):
        return remote(src, dst, self.ssem.at[e, k], self.rsem.at[e, k], target)

    def recv(self, e, k, ref):
        self.copy(ref, ref, e, k, self.p.sib()).wait_recv()

    def emit(self, e, left, right, extra=None):
        if e >= 2:
            self.shared(e - 2).wait_send()

        @pl.loop(0, 3)
        def _(n):
            cols = block(n, 256)
            values = right(cols)
            self.stage[e % 2, :, :, cols] = low(dot(left(), values)).reshape(16, 48, 256)
            if extra is not None:
                extra(cols, values)
        self.shared(e).start()

    def shared(self, e):
        return self.copy(self.stage.at[e % 2, :, :, self.other], self.r0.at[e % 4], e, 0, self.p.sib())

    def stage0(self, e):
        p, acc = self.p, self.acc
        self.recv(e, 0, self.r0.at[e % 4])

        def add(s):
            acc[e, s] = self.stage[e % 2, s, :, self.own] + self.r0[e % 4, s]

        for j, q in enumerate((p.q2, p.q12)):
            @pl.loop(0, 4)
            def _(z):
                s = z * 4 + q
                add(s)
                self.copy(acc.at[e, s], self.r1.at[e, z * 2 + j], e, 16 + z * 2 + j, p.n2()).start()
        for q in (p.q1, p.quad):
            @pl.loop(0, 4)
            def _(z):
                add(z * 4 + q)

    def stage1(self, e):
        p, acc = self.p, self.acc

        @pl.loop(0, 4)
        def _(z):
            s = z * 4 + p.q1
            self.recv(e, 17 + z * 2, self.r1.at[e, z * 2 + 1])
            acc[e, s] += self.r1[e, z * 2 + 1]
            self.copy(acc.at[e, s], self.r2.at[e, z], e, 24 + z, p.n1()).start()

        @pl.loop(0, 4)
        def _(z):
            self.recv(e, 16 + z * 2, self.r1.at[e, z * 2])
            acc[e, z * 4 + p.quad] += self.r1[e, z * 2]

    def stage2(self, e):
        p, acc = self.p, self.acc
        for k in range(1, 4):
            z = p.ring(k)
            s = z * 4 + p.quad
            self.recv(e, 24 + z, self.r2.at[e, z])
            acc[e, s] += self.r2[e, z]
            self.copy(acc.at[e, s], self.r3.at[e, k - 1], e, 28 + k, p.up(k)).start()
        self.recv(e, 24 + p.z, self.r2.at[e, p.z])

    def stage3(self, e):
        p = self.p
        total = wide(self.acc[e, p.me]) + wide(self.r2[e, p.z])
        for k in range(1, 4):
            self.recv(e, 28 + k, self.r3.at[e, k - 1])
            total = total + wide(self.r3[e, k - 1])
        view = self.result(e, p.c)
        view[...] = total
        self.copy(view, view, e, 28, p.sib()).start()

    def finish(self, count):
        for e in range(count):
            self.recv(e, 28, self.result(e, 1 - self.p.c))
            self.copy(self.result(e, self.p.c), self.result(e, self.p.c), e, 28, self.p.sib()).wait_send()
        for e in range(count - 2, count):
            self.shared(e).wait_send()
        one = self.acc.at[0, 0]

        @pl.loop(0, count)
        def _(e):
            @pl.loop(16, 28)
            def _(k):
                self.copy(one, one, e, k, self.p.sib()).wait_send()

            @pl.loop(29, 32)
            def _(k):
                self.copy(one, one, e, k, self.p.sib()).wait_send()


def backward_kernel(inner, lens, d_pool, vec, a_hbm, i_hbm, o_hbm, k_hbm, v_hbm, prob_hbm, prob_q_hbm, x_t_hbm, q_t_hbm, ctx_t_hbm, norm_t_hbm,
                    act_t_hbm, slope_hbm, y1_hbm, r1_hbm, y2_hbm, r2_hbm,
                    dx_out, dvec_out, g_query, g_key, g_value, g_output, g_inner, g_outer,
                    wa, wi, act_t, slope, d_inner, y, scale_one, scale_two, d_second, d_low, norm_t, ctx_t, x_t, q_t, k, v, prob, prob_q, ds_buf,
                    d_vec, v_in, v_out, stage, r0, acc, r1, r2, r3, ssem, rsem, lsem, psem, vsem, xsem):
    p = Place(inner)

    def load(i, src, dst):
        return pltpu.make_async_copy(src, dst, lsem.at[i])

    loads = {
        "y2": load(0, y2_hbm, y), "r2": load(1, r2_hbm, scale_two), "act_t": load(2, act_t_hbm, act_t),
        "slope": load(7, slope_hbm, slope), "norm_t": load(8, norm_t_hbm, norm_t), "wi": load(9, i_hbm, wi),
        "y1": load(10, y1_hbm, y), "r1": load(11, r1_hbm, scale_one), "ctx_t": load(12, ctx_t_hbm, ctx_t), "wa": load(13, a_hbm, wa),
        "k": load(14, k_hbm, k), "v": load(15, v_hbm, v), "q_t": load(16, q_t_hbm, q_t), "x_t": load(17, x_t_hbm, x_t), "prob_q": load(18, prob_q_hbm, prob_q),
    }
    for n in range(4):
        loads["wo%d" % n] = load(3 + n, o_hbm.at[pl.ds(n * 768, 768)], wa.at[n])

    def start(*names):
        for name in names:
            loads[name].start()

    def need(*names):
        for name in names:
            loads[name].wait()

    def load_prob(j):
        return pltpu.make_async_copy(prob_hbm.at[pl.ds(j * 2, 2)], prob.at[lax.rem(j, 2)], psem.at[lax.rem(j, 2)])

    start("y2", "r2", "act_t", "wo0", "wo1", "wo2", "wo3", "slope", "norm_t", "wi", "r1", "ctx_t", "k", "v", "q_t", "x_t", "prob_q")
    load_prob(0).start()
    load_prob(1).start()
    p.barrier()

    def result(e, which):
        cols = pl.ds(pl.multiple_of(which * 384, 128), 384)
        if e < 4:
            return g_outer.at[pl.ds(e * 48, 48), cols]
        if e < 8:
            return g_inner.at[:, pl.ds(pl.multiple_of((e - 4) * 768 + which * 384, 128), 384)]
        return (g_output, g_query, g_key, g_value)[e - 8].at[:, cols]

    sc = Scatter(p, (stage, r0, acc, r1, r2, r3, ssem, rsem), result)
    d_vec[...] = jnp.zeros_like(d_vec)

    def gain(row):
        return vec[row : row + 1, :768]

    def tally(row, value):
        d_vec[row : row + 1] += jnp.sum(value, axis=0, keepdims=True)

    len_p, len_q = lens[0], lens[1]
    pool_q = d_pool[0:1] / wide(jnp.full((1, 1), len_q, jnp.int32))
    pool_p = d_pool[1:2] / wide(jnp.full((1, 1), len_p, jnp.int32))

    def norm_back(d, row, yy, scale, rows):
        tally(row, d * yy)
        tally(row + 1, d)
        g = d * gain(row)
        d = (g - jnp.mean(g, axis=1, keepdims=True) - yy * jnp.mean(g * yy, axis=1, keepdims=True)) * scale
        d_second[rows] = d
        d_low[rows] = low(d)
        return d

    need("y2", "r2")

    @pl.loop(0, 3)
    def _(n):
        rows = block(n, 192)
        at = lax.broadcasted_iota(jnp.int32, (192, 1), 0) + n * 192
        d_rows = jnp.where(at < S, jnp.where(at < len_p, pool_p, 0.0), jnp.where(at - S < len_q, pool_q, 0.0))
        d = norm_back(d_rows, 6, y[rows], scale_two[rows], rows)
        tally(3, wide(low(d)))

    start("y1")
    need("act_t")

    def emit_outer(n):
        sc.emit(n, lambda: act_t[n * 768 : (n + 1) * 768], lambda cols: d_low[:, cols])

    def emit_inner(n):
        def bias(cols, values):
            d_vec[8 + n : 9 + n, cols] = jnp.sum(wide(values), axis=0, keepdims=True)
        sc.emit(4 + n, lambda: norm_t[...], lambda cols: d_inner[:, pl.ds(pl.multiple_of(n * 768 + cols.start, 256), 256)], bias)

    emit_outer(0)
    emit_outer(1)
    sc.stage0(0)
    emit_outer(2)
    sc.stage0(1)
    emit_outer(3)
    sc.stage0(2)
    need("wo0", "wo1", "wo2", "wo3", "slope")

    def inner_back(low_n, high_n):
        @pl.loop(low_n, high_n)
        def _(n):
            cols = block(n, 256)
            d_inner[:, cols] = low(dot_nt(d_low[...], wa[n // 3, block(lax.rem(n, 3), 256)]) * wide(slope[:, cols]))

    inner_back(0, 6)
    sc.stage0(3)
    inner_back(6, 12)
    start("wa")
    sc.stage1(0)
    need("norm_t")
    emit_inner(0)
    sc.stage1(1)
    emit_inner(1)
    sc.stage0(4)
    sc.stage2(0)
    emit_inner(2)
    sc.stage0(5)
    sc.stage1(2)
    emit_inner(3)
    sc.stage0(6)
    sc.stage2(1)
    need("wi", "y1", "r1")

    @pl.loop(0, 3)
    def _(n):
        rows = block(n, 192)
        d = norm_back(d_second[rows] + dot_nt(d_inner[rows], wi[...]), 4, y[rows], scale_one[rows], rows)
        tally(2, wide(low(d)))

    sc.stage0(7)
    sc.stage1(3)
    sc.stage2(2)
    need("ctx_t", "wa")
    sc.emit(8, lambda: ctx_t[...], lambda cols: d_low[:, cols])

    def part(i):
        return pl.ds(i * 768, 768)

    def pair_cols(i, j):
        return pl.ds(pl.multiple_of(i * 768 + j * 128, 128), 128)

    def head_rows(i, head):
        return pl.ds(pl.multiple_of(i * 768 + head * 64, 64), 64)

    @pl.loop(0, 3)
    def _(n):
        rows = block(n, 192)
        d_inner[rows, part(3)] = low(dot_nt(d_low[rows], wa[3]))
    act_t[part(2)] = d_inner[:, part(3)].T
    need("k", "v", "q_t", "prob_q")
    sc.stage0(8)
    sc.stage1(4)
    sc.stage2(3)
    sc.stage3(0)

    def attention(low_j, high_j):
        @pl.loop(low_j, high_j)
        def _(j):
            load_prob(j).wait()
            slot = lax.rem(j, 2)
            cols = block(j, 128)
            for start, size, rb in SPANS:
                rows = slice(start, start + size)
                kp, vp = k[rows, cols], v[rows, cols]
                dq_parts = [None] * (size // rb)
                for h in range(2):
                    probs = (lambda sl: prob[slot, h, sl]) if size == S else (lambda sl: prob_q[2 * j + h, sl])
                    mask = head_mask(h)
                    for r in range(0, size, rb):
                        d_p = dot_nt(d_inner[start + r : start + r + rb, pair_cols(3, j)] * mask, vp)
                        w = wide(probs(slice(r, r + rb)))
                        ds = low(w * (d_p - jnp.sum(w * d_p, axis=1, keepdims=True)))
                        ds_buf[h, r : r + rb, :size] = ds
                        piece = dot(ds, kp * mask)
                        i = r // rb
                        dq_parts[i] = piece if dq_parts[i] is None else dq_parts[i] + piece
                    head = 2 * j + h
                    act_t[head_rows(1, head), rows] = low(dot(act_t[head_rows(2, head), rows], probs(slice(0, size))))
                    act_t[head_rows(0, head), rows] = low(dot(q_t[head_rows(0, head), rows], ds_buf[h, :size, :size]) * 0.125)
                for i, piece in enumerate(dq_parts):
                    d_inner[start + i * rb : start + (i + 1) * rb, pair_cols(0, j)] = low(piece * 0.125)

            @pl.when(j < 4)
            def _():
                load_prob(j + 2).start()

    attention(0, 2)
    sc.stage1(5)
    sc.stage2(4)
    sc.stage3(1)
    attention(2, 4)
    sc.stage1(6)
    sc.stage2(5)
    sc.stage3(2)
    attention(4, 6)
    sc.stage1(7)
    sc.stage2(6)
    sc.stage3(3)
    d_inner[:, part(1)] = act_t[part(0)].T
    d_inner[:, part(2)] = act_t[part(1)].T
    need("x_t")

    def emit_first(n):
        row = (0, None, 1)[n]

        def bias(cols, values):
            d_vec[row : row + 1, cols] = jnp.sum(wide(values), axis=0, keepdims=True)
        sc.emit(9 + n, lambda: x_t[...], lambda cols: d_inner[:, pl.ds(pl.multiple_of(n * 768 + cols.start, 256), 256)], None if row is None else bias)

    emit_first(0)
    sc.stage1(8)
    emit_first(1)
    sc.stage0(9)
    emit_first(2)

    def vector(i, src, target):
        return remote(src, v_in.at[i], vsem.at[0, i], vsem.at[1, i], target)

    def vector_recv(i):
        vector(i, v_in.at[i], p.sib()).wait_recv()
        return v_in[i]

    vector(0, d_vec.at[:, sc.other], p.sib()).start()
    sc.stage0(10)
    sc.stage2(7)

    @pl.loop(0, 3)
    def _(n):
        rows = block(n, 192)
        d = d_second[rows]
        for i in range(3):
            d = d + dot_nt(d_inner[rows, part(i)], wa[i])
        d_low[rows] = low(d)
    mine = pltpu.make_async_copy(d_low, dx_out.at[p.c], xsem.at[0])
    theirs = remote(d_low, dx_out.at[p.c], xsem.at[1], xsem.at[2], p.sib())
    mine.start()
    theirs.start()
    sc.stage0(11)
    v_out[0] = d_vec[:, sc.own] + vector_recv(0)
    vector(1, v_out.at[0], p.n2()).start()
    sc.stage3(4)
    sc.stage1(9)
    v_out[1] = v_out[0] + vector_recv(1)
    vector(2, v_out.at[1], p.n1()).start()
    sc.stage2(8)
    sc.stage3(5)
    sc.stage1(10)
    v_out[2] = v_out[1] + vector_recv(2)
    for i in range(1, 4):
        vector(2 + i, v_out.at[2], p.up(i)).start()
    sc.stage2(9)
    sc.stage3(6)
    sc.stage1(11)
    sc.stage2(10)
    sc.stage3(7)
    dvec_out[:, sc.own] = v_out[2] + vector_recv(3) + vector_recv(4) + vector_recv(5)
    last = remote(dvec_out.at[:, sc.own], dvec_out.at[:, sc.own], vsem.at[0, 6], vsem.at[1, 6], p.sib())
    last.start()
    sc.stage2(11)
    for e in range(8, 12):
        sc.stage3(e)
    mine.wait()
    theirs.wait_send()
    remote(dx_out.at[1 - p.c], dx_out.at[1 - p.c], xsem.at[1], xsem.at[2], p.sib()).wait_recv()
    remote(dvec_out.at[:, sc.other], dvec_out.at[:, sc.other], vsem.at[0, 6], vsem.at[1, 6], p.sib()).wait_recv()
    last.wait_send()
    for i in range(6):
        vector(i, v_in.at[i], p.sib()).wait_send()
    sc.finish(12)


def backward_call(inner, lens, d_pool, vec, wa, wi, wo, saved, cid=1):
    bf, f32 = jnp.bfloat16, jnp.float32
    sds = jax.ShapeDtypeStruct
    outs = [sds((2, T, 768), bf), sds((16, 768), f32)] + [sds((48, 768), f32)] * 4 + [sds((48, 3072), f32), sds((192, 768), f32)]
    vmem = pltpu.VMEM
    scratch = [
        vmem((4, 768, 768), bf), vmem((768, 3072), bf), vmem((3072, T), bf), vmem((T, 3072), bf), vmem((T, 3072), bf),
        vmem((T, 768), f32), vmem((T, 1), f32), vmem((T, 1), f32), vmem((T, 768), f32), vmem((T, 768), bf)]
    scratch += [vmem((768, T), bf)] * 4 + [vmem((T, 768), bf)] * 2
    scratch += [vmem((2, 2, S, S), bf), vmem((12, Q, Q), bf), vmem((2, S, S), bf), vmem((16, 768), f32), vmem((6, 16, 384), f32), vmem((3, 16, 384), f32)]
    scratch += [vmem((2, 16, 48, 768), bf), vmem((4, 16, 48, 384), bf)] + [vmem((12, n, 48, 384), bf) for n in (16, 8, 4, 3)]
    dma = pltpu.SemaphoreType.DMA
    scratch += [dma((12, 32)), dma((12, 32)), dma((19,)), dma((2,)), dma((2, 7)), dma((3,))]
    return pl.pallas_call(
        functools.partial(backward_kernel, inner),
        out_shape=outs,
        in_specs=[pl.BlockSpec(memory_space=pltpu.SMEM), VM, VM] + [ANY] * 17,
        out_specs=[ANY] + [VM] * 7,
        scratch_shapes=scratch,
        compiler_params=pltpu.CompilerParams(collective_id=cid, has_side_effects=True, vmem_limit_bytes=63 << 20),
        name="layer_backward",
    )(lens, d_pool, vec, wa, wi, wo, *saved)


def loss_kernel(pooled, targets, seq, d_pool, loss, rows, ssem, rsem):
    pairs = targets.shape[0]
    me = lax.axis_index("dp") * 2 + lax.axis_index("tower")

    def device(at):
        return {"dp": at // 2, "tower": lax.rem(at, 2)}

    sem = pltpu.get_barrier_semaphore()

    @pl.loop(1, pairs)
    def _(k):
        pl.semaphore_signal(sem, inc=1, device_id=device(lax.rem(me + k, pairs)), device_id_type=MESH)
    mine = pooled[...]
    root = jnp.sqrt(jnp.sum(mine * mine, axis=1, keepdims=True) + 1e-6)
    unit = mine / root
    rows[me] = unit
    pl.semaphore_wait(sem, pairs - 1)

    @pl.loop(1, pairs)
    def _(k):
        remote(rows.at[me], rows.at[me], ssem, rsem, device(lax.rem(me + k, pairs))).start()
    rest = rows.at[pl.ds(0, pairs - 1)]
    remote(rest, rest, ssem, rsem, device(me)).wait_recv()
    remote(rest, rest, ssem, rsem, device(me)).wait_send()
    exact = lax.Precision.HIGHEST
    qs, ps = rows[:, 0, :], rows[:, 1, :]
    logits = lax.dot_general(qs, ps, (((1,), (1,)), ((), ())), precision=exact, preferred_element_type=jnp.float32) / 0.01
    hit = targets[...] == lax.broadcasted_iota(jnp.int32, (pairs, pairs), 1)
    top = jnp.max(logits, axis=1, keepdims=True)
    lse = jnp.log(jnp.sum(jnp.exp(logits - top), axis=1, keepdims=True)) + top
    picked = jnp.sum(jnp.where(hit, logits, 0.0), axis=1, keepdims=True)
    loss[...] = jnp.broadcast_to(jnp.sum(lse - picked, axis=0, keepdims=True) / pairs, loss.shape)
    d_logits = seq * (jnp.exp(logits - lse) - jnp.where(hit, 1.0, 0.0))
    d_q = jnp.dot(d_logits, ps, precision=exact, preferred_element_type=jnp.float32) / 0.01
    d_p = lax.dot_general(d_logits, qs, (((0,), (0,)), ((), ())), precision=exact, preferred_element_type=jnp.float32) / 0.01
    own = lax.broadcasted_iota(jnp.int32, (pairs, 1), 0) == me
    for row, d in enumerate((d_q, d_p)):
        d_unit = jnp.sum(jnp.where(own, d, 0.0), axis=0, keepdims=True)
        u = unit[row : row + 1]
        d_pool[row : row + 1] = (d_unit - u * jnp.sum(u * d_unit, axis=1, keepdims=True)) / root[row : row + 1]


def loss_call(pooled, targets, seq, cid=2):
    pairs = targets.shape[0]
    return pl.pallas_call(
        lambda *refs: loss_kernel(refs[0], refs[1], float(seq), *refs[2:]),
        out_shape=(jax.ShapeDtypeStruct((2, 768), jnp.float32), jax.ShapeDtypeStruct((8, 128), jnp.float32)),
        in_specs=[VM] * 2,
        out_specs=[VM] * 2,
        scratch_shapes=[pltpu.VMEM((pairs, 2, 768), jnp.float32), pltpu.SemaphoreType.DMA, pltpu.SemaphoreType.DMA],
        compiler_params=pltpu.CompilerParams(collective_id=cid, has_side_effects=True),
        name="pair_loss",
    )(pooled, targets)


CUT = Cut(1)


def group_rows(x, groups):
    if groups is None:
        return x
    return lax.all_gather(x, "dp", axis=0, tiled=True, axis_index_groups=groups)


def per_device(
    query_tokens, passage_tokens, lengths, positives,
    query_weight, key_weight, value_weight, output_weight, inner_weight, outer_weight,
    query_bias, value_bias, output_bias, inner_bias, outer_bias,
    first_gain, first_shift, second_gain, second_shift,
):
    inner = lax.axis_size("dp") // 16
    groups = None if inner == 1 else [[h * inner + i for i in range(inner)] for h in range(16)]
    tower = lax.axis_index("tower")
    at = lax.axis_index("dp") // inner
    seq = passage_tokens.shape[1]

    def fetch(w):
        return group_rows(w, groups)

    wa = jnp.stack([fetch(w) for w in (query_weight, key_weight, value_weight, output_weight)])
    narrow = [fetch(w) for w in (query_bias, value_bias, output_bias, outer_bias, first_gain, first_shift, second_gain, second_shift)]
    vec = jnp.stack([jnp.pad(w, (0, 256 - w.shape[0])) for w in narrow + [fetch(inner_bias)]])
    vec = jnp.pad(vec, ((0, 7), (0, 0)))
    lens = jnp.pad(lengths, ((0, 7), (0, 126)))
    gv, ga, gi, go, gl = gather_all(inner, CUT, vec, wa, fetch(inner_weight), fetch(outer_weight), lens)
    full = jnp.pad(jnp.swapaxes(gv[:, :8, :48], 0, 1).reshape(8, 768), ((0, 0), (0, 2304)))
    full = jnp.pad(jnp.concatenate([full, gv[:, 8, :192].reshape(1, 3072)]), ((0, 7), (0, 0))).astype(jnp.float32)
    pair = lax.dynamic_index_in_dim(gl[:, 0, :2], tower, 1, keepdims=False)
    own = jnp.stack([pair[1], pair[0]])
    x = jnp.concatenate([
        lax.dynamic_index_in_dim(passage_tokens, tower, 0, keepdims=False),
        lax.dynamic_index_in_dim(query_tokens, tower, 0, keepdims=False),
    ])
    *saved, pooled = forward_call(own, x, full, ga, gi, go)
    d_pool, loss = loss_call(pooled, positives[:, None], seq)
    d_x, d_vec, *grads = backward_call(inner, own, d_pool, full, ga, gi, go, saved[1:])

    def finish(x):
        if groups is None:
            return x
        return lax.psum_scatter(x, "dp", scatter_dimension=0, tiled=True, axis_index_groups=groups)

    d_x = d_x.astype(jnp.float32)
    flat = lax.dynamic_slice_in_dim(d_vec[:8], at * 48, 48, 1)
    wide_bias = lax.dynamic_slice_in_dim(d_vec[8:12].reshape(3072), at * 192, 192, 0)
    rows = [finish(flat[i]) for i in range(8)]
    vectors = [rows[0], rows[1], rows[2], finish(wide_bias)] + rows[3:]
    return (loss[0, 0], d_x[:, seq:], d_x[:, :seq]) + tuple(finish(g) for g in grads) + tuple(vectors)


def solution(mesh):
    rows3, rows2, rows1 = P("dp", None, None), P("dp", None), P("dp")
    return jax.shard_map(
        per_device,
        mesh=mesh,
        in_specs=(rows3, rows3, P("tower", "dp"), P()) + (rows2,) * 6 + (rows1,) * 9,
        out_specs=(P(), rows3, rows3) + (rows2,) * 6 + (rows1,) * 9,
        check_vma=False,
    )
```

```python
import functools

import jax
import jax.numpy as jnp
from jax import lax
from jax.experimental import pallas as pl
from jax.experimental.pallas import tpu as pltpu
from jax.sharding import PartitionSpec as P

MESH = pl.DeviceIdType.MESH
ANY = pl.BlockSpec(memory_space=pl.ANY)
VM = pl.BlockSpec(memory_space=pltpu.VMEM)


class Place:
    def __init__(self, inner):
        dp = lax.axis_index("dp")
        self.c = lax.axis_index("tower")
        self.inner = inner
        self.low = lax.rem(dp, inner)
        self.me = dp // inner
        self.z = self.me // 4
        self.quad = lax.rem(self.me, 4)
        s1 = 1 + self.c
        s2 = 2 - self.c
        b1 = lax.rem(self.quad // s1, 2)
        b2 = lax.rem(self.quad // s2, 2)
        self.q1 = self.quad + s1 * (1 - 2 * b1)
        self.q2 = self.quad + s2 * (1 - 2 * b2)
        self.q12 = 3 - self.quad
        self.quads = (self.quad, self.q1, self.q2, self.q12)

    def ring(self, k):
        return lax.rem(self.z + k, 4)

    def dev(self, group):
        return {"dp": group * self.inner + self.low, "tower": self.c}

    def n1(self):
        return self.dev(self.z * 4 + self.q1)

    def n2(self):
        return self.dev(self.z * 4 + self.q2)

    def up(self, k):
        return self.dev(self.ring(k) * 4 + self.quad)

    def sib(self):
        return {"dp": self.me * self.inner + self.low, "tower": 1 - self.c}

    def barrier(self):
        sem = pltpu.get_barrier_semaphore()
        for target in (self.up(1), self.up(2), self.up(3), self.n1(), self.n2(), self.sib()):
            pl.semaphore_signal(sem, inc=1, device_id=target, device_id_type=MESH)
        pl.semaphore_wait(sem, 6)


def remote(src, dst, send_sem, recv_sem, target):
    return pltpu.make_async_remote_copy(
        src_ref=src, dst_ref=dst, send_sem=send_sem, recv_sem=recv_sem, device_id=target, device_id_type=MESH
    )


S, Q = 512, 64
T = S + Q


def dot(left, right):
    return jnp.dot(left, right, preferred_element_type=jnp.float32)


def dot_nt(left, right):
    return lax.dot_general(left, right, (((1,), (1,)), ((), ())), preferred_element_type=jnp.float32)


def block(index, size):
    return pl.ds(pl.multiple_of(index * size, size), size)


def low(x):
    return x.astype(jnp.bfloat16)


def wide(x):
    return x.astype(jnp.float32)


def head_mask(h):
    lane = lax.broadcasted_iota(jnp.int32, (1, 128), 1)
    return low(jnp.where(lane // 64 == h, 1.0, 0.0))


SPANS = ((0, S, 256), (S, Q, Q))


class Gather:
    def __init__(self, p, shards, wa, wi, wo, ssem, rsem, lsem):
        self.p, self.shards, self.wa, self.wi, self.wo = p, shards, wa, wi, wo
        self.ssem, self.rsem, self.lsem = ssem, rsem, lsem

    def cols(self, t, which):
        start = which * 384 if t < 4 or t > 7 else (t - 4) * 768 + which * 384
        return pl.ds(pl.multiple_of(start, 128), 384)

    def shard(self, t):
        ref = self.shards[t] if t < 4 else self.shards[4 if t < 8 else 5]
        return ref.at[:, self.cols(t, self.p.c)]

    def one(self, t, z):
        q, cols = self.p.quad, self.cols(t, self.p.c)
        if t < 4:
            return self.wa.at[t, z, q, :, cols]
        return (self.wi if t < 8 else self.wo).at[z, q, :, cols]

    def four(self, t, q, which):
        cols = self.cols(t, which)
        if t < 4:
            return self.wa.at[t, :, q, :, cols]
        if t < 8:
            return self.wi.at[:, q, :, cols]
        return self.wo.at[self.p.ring(12 - t), q, :, cols]

    def copy(self, src, dst, t, k, target):
        return remote(src, dst, self.ssem.at[t, k], self.rsem.at[t, k], target)

    def recv(self, t, k, ref):
        self.copy(ref, ref, t, k, self.p.sib()).wait_recv()

    def push(self, t, q, k, target):
        view = self.four(t, q, self.p.c)
        self.copy(view, view, t, k, target).start()

    def steps(self, t):
        return range(1, 4) if t < 8 else range(t - 8, t - 7) if t > 8 else ()

    def local(self, t):
        return pltpu.make_async_copy(self.shard(t), self.one(t, self.p.z), self.lsem.at[t])

    def stage_own(self, t):
        if t <= 8:
            self.local(t).start()
        for k in self.steps(t):
            self.copy(self.shard(t), self.one(t, self.p.z), t, k, self.p.up(k)).start()

    def stage_z(self, t):
        p = self.p
        if t <= 8:
            self.local(t).wait()
        for k in self.steps(t):
            self.recv(t, k, self.one(t, p.ring(4 - k)))
        self.push(t, p.quad, 4, p.n1())
        self.push(t, p.quad, 5, p.n2())
        self.push(t, p.quad, 8, p.sib())

    def stage_one(self, t):
        p = self.p
        self.recv(t, 4, self.four(t, p.q1, p.c))
        self.push(t, p.q1, 6, p.n2())
        self.push(t, p.q1, 9, p.sib())

    def stage_two(self, t):
        p = self.p
        for k, q in ((5, p.q2), (6, p.q12)):
            self.recv(t, k, self.four(t, q, p.c))
            self.push(t, q, k + 5, p.sib())

    def stage_sib(self, t):
        p = self.p
        for k, q in ((8, p.quad), (9, p.q2), (10, p.q1), (11, p.q12)):
            self.recv(t, k, self.four(t, q, 1 - p.c))

    def tick(self, i):
        for lag, stage in ((0, self.stage_z), (-AHEAD, self.stage_own), (1, self.stage_one), (2, self.stage_two), (3, self.stage_sib)):
            if 0 <= i - lag < 12:
                stage(i - lag)

    def finish(self):
        for t in range(12):
            for k in self.steps(t):
                self.copy(self.shard(t), self.one(t, self.p.z), t, k, self.p.sib()).wait_send()
            view = self.four(t, self.p.quad, self.p.c)
            for k in (4, 5, 6, 8, 9, 10, 11):
                self.copy(view, view, t, k, self.p.sib()).wait_send()


def expand_vectors(shards, vec):
    def split(size, shape, axis):
        at = wide(lax.broadcasted_iota(jnp.int32, shape, axis))
        which = jnp.floor((at + 0.5) * (1.0 / size))
        return which, at - which * size

    lane, _ = split(48, (1, 640), 1)
    spread = jnp.concatenate([jnp.where(lane == i, shards, 0.0) for i in range(8)])
    _, at_row = split(48, (640, 1), 0)
    owner, at_col = split(48, (1, 768), 1)
    rows = dot(low(spread), low(jnp.where(at_row == at_col, 1.0, 0.0)))
    own = wide(lax.broadcasted_iota(jnp.int32, (16, 1), 0))
    for i in range(8):
        vec[i : i + 1, :768] = jnp.sum(jnp.where(owner == own, rows[16 * i : 16 * i + 16], 0.0), axis=0, keepdims=True)
    at_row = wide(lax.broadcasted_iota(jnp.int32, (256, 1), 0))
    for n in range(4):
        owner, at_col = split(192, (1, 768), 1)
        rows = dot(low(shards[:, 384:]), low(jnp.where(at_row == at_col, 1.0, 0.0)))
        vec[8:9, n * 768 : (n + 1) * 768] = jnp.sum(jnp.where(owner + 4.0 * n == own, rows, 0.0), axis=0, keepdims=True)


def forward_kernel(inner, seq, lengths, v_shard, targets, w_query, w_key, w_value, w_output, w_inner, w_outer, query_tokens, passage_tokens,
                   d_pool, loss, lens, vec, wa_out, wi_out, wo_out,
                   k_out, v_out, prob_out, prob_q_out, x_t_out, q_t_out, ctx_t_out, norm_t_out, act_t_out, slope_out, y1_out, r1_out, y2_out, r2_out,
                   wa, wi, wo, x, q, k, v, prob, prob_q, ctx, normed, act, act_t, slope, x_t, q_t, ctx_t, norm_t, y1, r1, y2, r2, pooled, rows, vectors, len_buf,
                   ssem, rsem, lsem, vsem, osem, psem, xsem):
    p = Place(inner)
    pairs = targets.shape[0]
    me = lax.axis_index("dp") * 2 + p.c

    def device(at):
        return {"dp": at // 2, "tower": lax.rem(at, 2)}

    x_loads = [pltpu.make_async_copy(passage_tokens.at[p.c], x.at[pl.ds(0, S)], xsem.at[0]), pltpu.make_async_copy(query_tokens.at[p.c], x.at[pl.ds(S, Q)], xsem.at[1])]
    for copy in x_loads:
        copy.start()
    barrier = pltpu.get_barrier_semaphore()

    @pl.loop(1, pairs)
    def _(i):
        pl.semaphore_signal(barrier, inc=1, device_id=device(lax.rem(me + i, pairs)), device_id_type=MESH)
    lane = lax.broadcasted_iota(jnp.int32, (8, 128), 1)
    len_buf[p.c] = jnp.where(lane == 0, lengths[0, 0].astype(jnp.float32), lengths[0, 1].astype(jnp.float32))
    vectors[p.z, p.quad] = v_shard[...]
    pl.semaphore_wait(barrier, pairs - 1)

    gather = Gather(p, (w_query, w_key, w_value, w_output, w_inner, w_outer), wa, wi, wo, ssem, rsem, lsem)
    for t in range(AHEAD):
        gather.stage_own(t)
    len_copy = remote(len_buf.at[p.c], len_buf.at[p.c], xsem.at[2], xsem.at[3], p.sib())
    len_copy.start()

    def vector(i, q, target):
        view = vectors.at[p.z, p.quad] if i < 4 else vectors.at[:, q]
        return remote(view, view, vsem.at[0, i], vsem.at[1, i], target)

    for i in range(1, 4):
        vector(i, None, p.up(i)).start()
    saves = []

    def save(src, dst):
        copy = pltpu.make_async_copy(src, dst, osem.at[len(saves)])
        copy.start()
        saves.append(copy)

    for copy in x_loads:
        copy.wait()
    x_t[...] = x[...].T
    save(x_t, x_t_out)
    gather.tick(0)
    for i in range(1, 4):
        view = vectors.at[p.ring(4 - i), p.quad]
        remote(view, view, vsem.at[0, i], vsem.at[1, i], p.sib()).wait_recv()
    vector(4, p.quad, p.n1()).start()
    vector(5, p.quad, p.n2()).start()
    gather.tick(1)
    vector(4, p.q1, p.sib()).wait_recv()
    vector(6, p.q1, p.n2()).start()
    gather.tick(2)
    vector(5, p.q2, p.sib()).wait_recv()
    vector(6, p.q12, p.sib()).wait_recv()
    expand_vectors(jnp.concatenate([vectors[i // 4, i % 4] for i in range(16)]), vec)
    remote(len_buf.at[1 - p.c], len_buf.at[1 - p.c], xsem.at[2], xsem.at[3], p.sib()).wait_recv()
    len_q, len_p = [jnp.sum(jnp.where(lane[:1] == p.c, len_buf[i, 0:1], 0.0), axis=1, keepdims=True) for i in range(2)]
    lens[0:1] = jnp.broadcast_to(len_p, (1, 128))
    lens[1:2] = jnp.broadcast_to(len_q, (1, 128))
    lens[2:8] = jnp.zeros((6, 128), jnp.float32)

    def project(m, out, row):
        @pl.loop(0, 3)
        def _(n):
            cols = block(n, 256)
            acc = dot(x[...], wa[m, :, :, :, cols].reshape(768, 256))
            if row is not None:
                acc = acc + vec[row : row + 1, cols]
            out[:, cols] = low(acc)

    gather.tick(3)
    project(0, q, 0)
    gather.tick(4)
    project(1, k, None)
    q_t[...] = q[...].T
    save(q_t, q_t_out)
    save(k, k_out)
    gather.tick(5)
    project(2, v, 1)
    save(v, v_out)

    def store_prob(j):
        return pltpu.make_async_copy(prob.at[lax.rem(j, 2)], prob_out.at[pl.ds(j * 2, 2)], psem.at[lax.rem(j, 2)])

    def attention(low_j, high_j):
        @pl.loop(low_j, high_j)
        def _(j):
            cols = block(j, 128)
            slot = lax.rem(j, 2)

            @pl.when(j >= 2)
            def _():
                store_prob(j - 2).wait()

            for (start, size, rb), length in zip(SPANS, (len_p, len_q)):
                span = slice(start, start + size)
                kp, vp = k[span, cols], v[span, cols]
                valid = wide(lax.broadcasted_iota(jnp.int32, (1, size), 1)) < length
                for r in range(0, size, rb):
                    qp = q[start + r : start + r + rb, cols]
                    total = None
                    for h in range(2):
                        mask = head_mask(h)
                        scores = dot_nt(qp * (mask * 0.125), kp)
                        scores = jnp.where(valid, scores, -1e9)
                        e = jnp.exp(scores - jnp.max(scores, axis=1, keepdims=True))
                        w = low(e * (1.0 / jnp.sum(e, axis=1, keepdims=True)))
                        if size == S:
                            prob[slot, h, r : r + rb] = w
                        else:
                            prob_q[2 * j + h] = w
                        piece = dot(w, vp * mask)
                        total = piece if total is None else total + piece
                    ctx[start + r : start + r + rb, cols] = low(total)
            store_prob(j).start()

    gather.tick(6)
    save(wa, wa_out)
    attention(0, 2)
    gather.tick(7)
    attention(2, 4)
    gather.tick(8)
    attention(4, 6)
    save(prob_q, prob_q_out)
    ctx_t[...] = ctx[...].T
    save(ctx_t, ctx_t_out)

    def gain(row):
        return vec[row : row + 1, :768]

    @pl.loop(0, 3)
    def _(n):
        span = block(n, 192)
        first = wide(x[span]) + (dot(ctx[span], wa[3].reshape(768, 768)) + gain(2))
        center = first - jnp.mean(first, axis=1, keepdims=True)
        scale = lax.rsqrt(jnp.mean(center * center, axis=1, keepdims=True) + 1e-12)
        y = center * scale
        y1[span] = y
        r1[span] = scale
        normed[span] = low(y * gain(4) + gain(5))
    save(y1, y1_out)
    save(r1, r1_out)
    norm_t[...] = normed[...].T
    save(norm_t, norm_t_out)

    def hidden(low_n, high_n):
        @pl.loop(low_n, high_n)
        def _(n):
            cols = block(n, 256)
            u = dot(normed[...], wi[:, :, :, cols].reshape(768, 256)) + vec[8:9, cols]
            cdf = 0.5 * (1.0 + lax.erf(u * 0.7071067811865476))
            act[:, cols] = low(u * cdf)
            slope[:, cols] = low(cdf + u * (0.3989422804014327 * jnp.exp(-0.5 * u * u)))

    gather.tick(9)
    hidden(0, 9)
    gather.tick(10)
    save(wi, wi_out)
    hidden(9, 12)
    save(slope, slope_out)

    for b in range(4):
        turned = act[:, b * 768 : (b + 1) * 768].T
        for s in range(4):
            for n in range(4):
                row = n * 768 + (b * 4 + s) * 48
                act_t[row : row + 48] = turned[s * 192 + n * 48 : s * 192 + n * 48 + 48]
    save(act_t, act_t_out)
    pooled[...] = jnp.zeros_like(pooled)

    def outer(i):
        plane = p.ring(4 - i)

        @pl.loop(0, 3)
        def _(n):
            span = block(n, 192)
            add = dot(act[span, pl.ds(pl.multiple_of(plane * 768, 128), 768)], wo[plane].reshape(768, 768))
            if i == 0:
                add = add + (y1[span] * gain(4) + gain(5) + gain(3))
            else:
                add = add + y2[span]
            if i < 3:
                y2[span] = add
                return
            center = add - jnp.mean(add, axis=1, keepdims=True)
            scale = lax.rsqrt(jnp.mean(center * center, axis=1, keepdims=True) + 1e-12)
            y = center * scale
            y2[span] = y
            r2[span] = scale
            out = y * gain(6) + gain(7)
            at = wide(lax.broadcasted_iota(jnp.int32, (192, 1), 0) + n * 192)
            for row, keep in ((0, (at >= S) & (at - S < len_q)), (1, (at < S) & (at < len_p))):
                pooled[row : row + 1] += jnp.sum(jnp.where(keep, out, 0.0), axis=0, keepdims=True)

    for i in range(4):
        gather.tick(11 + i)
        outer(i)
    save(y2, y2_out)
    save(r2, r2_out)
    save(wo, wo_out)

    mine = jnp.concatenate([pooled[0:1] / len_q, pooled[1:2] / len_p])
    root = jnp.sqrt(jnp.sum(mine * mine, axis=1, keepdims=True) + 1e-6)
    unit = mine / root
    rows[me] = unit

    @pl.loop(1, pairs)
    def _(i):
        remote(rows.at[me], rows.at[me], xsem.at[4], xsem.at[5], device(lax.rem(me + i, pairs))).start()
    rest = rows.at[pl.ds(0, pairs - 1)]
    remote(rest, rest, xsem.at[4], xsem.at[5], p.sib()).wait_recv()
    exact = lax.Precision.HIGHEST
    qs, ps = rows[:, 0, :], rows[:, 1, :]
    logits = lax.dot_general(qs, ps, (((1,), (1,)), ((), ())), precision=exact, preferred_element_type=jnp.float32) / 0.01
    hit = targets[...] == lax.broadcasted_iota(jnp.int32, (pairs, pairs), 1)
    top = jnp.max(logits, axis=1, keepdims=True)
    lse = jnp.log(jnp.sum(jnp.exp(logits - top), axis=1, keepdims=True)) + top
    picked = jnp.sum(jnp.where(hit, logits, 0.0), axis=1, keepdims=True)
    loss[...] = jnp.broadcast_to(jnp.sum(lse - picked, axis=0, keepdims=True) / pairs, loss.shape)
    d_logits = seq * (jnp.exp(logits - lse) - jnp.where(hit, 1.0, 0.0))
    d_q = jnp.dot(d_logits, ps, precision=exact, preferred_element_type=jnp.float32) / 0.01
    d_p = lax.dot_general(d_logits, qs, (((0,), (0,)), ((), ())), precision=exact, preferred_element_type=jnp.float32) / 0.01
    own = lax.broadcasted_iota(jnp.int32, (pairs, 1), 0) == me
    for row, d in enumerate((d_q, d_p)):
        d_unit = jnp.sum(jnp.where(own, d, 0.0), axis=0, keepdims=True)
        u = unit[row : row + 1]
        d_pool[row : row + 1] = (d_unit - u * jnp.sum(u * d_unit, axis=1, keepdims=True)) / root[row : row + 1]

    remote(rest, rest, xsem.at[4], xsem.at[5], p.sib()).wait_send()
    gather.finish()
    len_copy.wait_send()
    for i in range(1, 7):
        vector(i, p.quad, p.sib()).wait_send()
    for copy in saves:
        copy.wait()
    store_prob(4).wait()
    store_prob(5).wait()


AHEAD = 2


def forward_call(inner, seq, lengths, v_shard, targets, weights, query_tokens, passage_tokens, cid=0):
    bf, f32 = jnp.bfloat16, jnp.float32
    sds, vmem, dma = jax.ShapeDtypeStruct, pltpu.VMEM, pltpu.SemaphoreType.DMA
    pairs = targets.shape[0]
    stored = [((T, 768), bf)] * 2 + [((12, S, S), bf), ((12, Q, Q), bf)] + [((768, T), bf)] * 4 + [
        ((3072, T), bf), ((T, 3072), bf), ((T, 768), f32), ((T, 1), f32), ((T, 768), f32), ((T, 1), f32)]
    full = [((4, 4, 4, 48, 768), bf), ((4, 4, 48, 3072), bf), ((4, 4, 192, 768), bf)]
    outs = [((2, 768), f32), ((8, 128), f32), ((8, 128), f32), ((16, 3072), f32)] + full + stored
    rows = (T, 768)
    scratch = [vmem(*w) for w in full] + [vmem(rows, bf)] * 4 + [vmem((2, 2, S, S), bf), vmem((12, Q, Q), bf)] + [vmem(rows, bf)] * 2
    scratch += [vmem((T, 3072), bf), vmem((3072, T), bf), vmem((T, 3072), bf)] + [vmem((768, T), bf)] * 4
    scratch += [vmem(rows, f32), vmem((T, 1), f32), vmem(rows, f32), vmem((T, 1), f32), vmem((2, 768), f32)]
    scratch += [vmem((pairs, 2, 768), f32), vmem((4, 4, 1, 640), f32), vmem((2, 8, 128), f32)]
    scratch += [dma((12, 12)), dma((12, 12)), dma((9,)), dma((2, 7)), dma((17,)), dma((2,)), dma((6,))]
    return pl.pallas_call(
        functools.partial(forward_kernel, inner, seq),
        out_shape=[sds(*o) for o in outs],
        in_specs=[pl.BlockSpec(memory_space=pltpu.SMEM), VM, VM] + [ANY] * 8,
        out_specs=[VM] * 4 + [ANY] * 17,
        scratch_shapes=scratch,
        compiler_params=pltpu.CompilerParams(collective_id=cid, has_side_effects=True, vmem_limit_bytes=62 << 20),
        name="layer_forward",
    )(lengths, v_shard, targets, *weights, query_tokens, passage_tokens)


class Scatter:
    def __init__(self, p, refs, result):
        self.p = p
        self.stage, self.r0, self.acc, self.r1, self.r2, self.r3, self.ssem, self.rsem = refs
        self.result = result
        self.own = pl.ds(pl.multiple_of(p.c * 384, 128), 384)
        self.other = pl.ds(pl.multiple_of((1 - p.c) * 384, 128), 384)

    def copy(self, src, dst, e, k, target):
        return remote(src, dst, self.ssem.at[e, k], self.rsem.at[e, k], target)

    def recv(self, e, k, ref):
        self.copy(ref, ref, e, k, self.p.sib()).wait_recv()

    def emit(self, e, left, right, extra=None):
        if e >= 2:
            self.shared(e - 2).wait_send()

        @pl.loop(0, 3)
        def _(n):
            cols = block(n, 256)
            values = right(cols)
            self.stage[e % 2, :, :, :, cols] = low(dot(left(), values)).reshape(4, 4, 48, 256)
            if extra is not None:
                extra(cols, values)
        self.shared(e).start()

    def shared(self, e):
        return self.copy(self.stage.at[e % 2, :, :, :, self.other], self.r0.at[e % 4], e, 0, self.p.sib())

    def stage0(self, e):
        p, acc = self.p, self.acc
        self.recv(e, 0, self.r0.at[e % 4])
        for j, q in enumerate((p.q2, p.q12, p.q1, p.quad)):
            acc[e, :, q] = self.stage[e % 2, :, q, :, self.own] + self.r0[e % 4, :, q]
            if j < 2:
                self.copy(acc.at[e, :, q], self.r1.at[e, j], e, 1 + j, p.n2()).start()

    def stage1(self, e):
        p, acc = self.p, self.acc
        self.recv(e, 2, self.r1.at[e, 1])
        acc[e, :, p.q1] += self.r1[e, 1]
        self.copy(acc.at[e, :, p.q1], self.r2.at[e], e, 3, p.n1()).start()
        self.recv(e, 1, self.r1.at[e, 0])
        acc[e, :, p.quad] += self.r1[e, 0]

    def stage2(self, e):
        p, acc = self.p, self.acc
        self.recv(e, 3, self.r2.at[e])
        acc[e, :, p.quad] += self.r2[e]
        for k in range(1, 4):
            self.copy(acc.at[e, p.ring(k), p.quad], self.r3.at[e, k - 1], e, 3 + k, p.up(k)).start()

    def stage3(self, e):
        p = self.p
        total = wide(self.acc[e, p.z, p.quad])
        for k in range(1, 4):
            self.recv(e, 3 + k, self.r3.at[e, k - 1])
            total = total + wide(self.r3[e, k - 1])
        view = self.result(e, p.c)
        view[...] = total
        self.copy(view, view, e, 7, p.sib()).start()

    def finish(self, count):
        for e in range(count):
            self.recv(e, 7, self.result(e, 1 - self.p.c))
            self.copy(self.result(e, self.p.c), self.result(e, self.p.c), e, 7, self.p.sib()).wait_send()
        for e in range(count - 2, count):
            self.shared(e).wait_send()
        four, one = self.r2.at[0], self.r3.at[0, 0]

        @pl.loop(0, count)
        def _(e):
            for k in range(1, 7):
                view = four if k < 4 else one
                self.copy(view, view, e, k, self.p.sib()).wait_send()


def backward_kernel(inner, lens, d_pool, vec, a_hbm, i_hbm, o_hbm, k_hbm, v_hbm, prob_hbm, prob_q_hbm, x_t_hbm, q_t_hbm, ctx_t_hbm, norm_t_hbm,
                    act_t_hbm, slope_hbm, y1_hbm, r1_hbm, y2_hbm, r2_hbm,
                    dx_out, dvec_out, g_query, g_key, g_value, g_output, g_inner, g_outer,
                    wa, wi, act_t, slope, d_inner, y, scale_one, scale_two, d_second, d_low, norm_t, ctx_t, x_t, q_t, k, v, prob, prob_q, ds_buf,
                    d_vec, v_in, v_out, stage, r0, acc, r1, r2, r3, ssem, rsem, lsem, psem, vsem, xsem):
    p = Place(inner)

    def load(i, src, dst):
        return pltpu.make_async_copy(src, dst, lsem.at[i])

    loads = {
        "y2": load(0, y2_hbm, y), "r2": load(1, r2_hbm, scale_two), "act_t": load(2, act_t_hbm, act_t),
        "slope": load(7, slope_hbm, slope), "norm_t": load(8, norm_t_hbm, norm_t), "wi": load(9, i_hbm, wi),
        "y1": load(10, y1_hbm, y), "r1": load(11, r1_hbm, scale_one), "ctx_t": load(12, ctx_t_hbm, ctx_t), "wa": load(13, a_hbm, wa),
        "k": load(14, k_hbm, k), "v": load(15, v_hbm, v), "q_t": load(16, q_t_hbm, q_t), "x_t": load(17, x_t_hbm, x_t), "prob_q": load(18, prob_q_hbm, prob_q),
    }
    for n in range(4):
        loads["wo%d" % n] = load(3 + n, o_hbm.at[pl.ds(n * 768, 768)], wa.at[n])

    def start(*names):
        for name in names:
            loads[name].start()

    def need(*names):
        for name in names:
            loads[name].wait()

    def load_prob(j):
        return pltpu.make_async_copy(prob_hbm.at[pl.ds(j * 2, 2)], prob.at[lax.rem(j, 2)], psem.at[lax.rem(j, 2)])

    start("y2", "r2", "act_t", "wo0", "wo1", "wo2", "wo3", "slope", "norm_t", "wi", "r1", "ctx_t", "k", "v", "q_t", "x_t", "prob_q")
    load_prob(0).start()
    load_prob(1).start()
    p.barrier()

    def result(e, which):
        cols = pl.ds(pl.multiple_of(which * 384, 128), 384)
        if e < 4:
            return g_outer.at[pl.ds(e * 48, 48), cols]
        if e < 8:
            return g_inner.at[:, pl.ds(pl.multiple_of((e - 4) * 768 + which * 384, 128), 384)]
        return (g_output, g_query, g_key, g_value)[e - 8].at[:, cols]

    sc = Scatter(p, (stage, r0, acc, r1, r2, r3, ssem, rsem), result)
    d_vec[...] = jnp.zeros_like(d_vec)

    def gain(row):
        return vec[row : row + 1, :768]

    def tally(row, value):
        d_vec[row : row + 1] += jnp.sum(value, axis=0, keepdims=True)

    len_p, len_q = lens[0:1, 0:1], lens[1:2, 0:1]
    pool_q = d_pool[0:1] / len_q
    pool_p = d_pool[1:2] / len_p

    def norm_back(d, row, yy, scale, rows):
        tally(row, d * yy)
        tally(row + 1, d)
        g = d * gain(row)
        d = (g - jnp.mean(g, axis=1, keepdims=True) - yy * jnp.mean(g * yy, axis=1, keepdims=True)) * scale
        d_second[rows] = d
        d_low[rows] = low(d)
        return d

    need("y2", "r2")

    @pl.loop(0, 3)
    def _(n):
        rows = block(n, 192)
        at = wide(lax.broadcasted_iota(jnp.int32, (192, 1), 0) + n * 192)
        d_rows = jnp.where(at < S, jnp.where(at < len_p, pool_p, 0.0), jnp.where(at - S < len_q, pool_q, 0.0))
        d = norm_back(d_rows, 6, y[rows], scale_two[rows], rows)
        tally(3, wide(low(d)))

    start("y1")
    need("act_t")

    def emit_outer(n):
        sc.emit(n, lambda: act_t[n * 768 : (n + 1) * 768], lambda cols: d_low[:, cols])

    def emit_inner(n):
        def bias(cols, values):
            d_vec[8 + n : 9 + n, cols] = jnp.sum(wide(values), axis=0, keepdims=True)
        sc.emit(4 + n, lambda: norm_t[...], lambda cols: d_inner[:, pl.ds(pl.multiple_of(n * 768 + cols.start, 256), 256)], bias)

    emit_outer(0)
    emit_outer(1)
    sc.stage0(0)
    emit_outer(2)
    sc.stage0(1)
    emit_outer(3)
    sc.stage0(2)
    need("wo0", "wo1", "wo2", "wo3", "slope")

    def inner_back(low_n, high_n):
        @pl.loop(low_n, high_n)
        def _(n):
            cols = block(n, 256)
            d_inner[:, cols] = low(dot_nt(d_low[...], wa[n // 3, block(lax.rem(n, 3), 256)]) * wide(slope[:, cols]))

    inner_back(0, 6)
    sc.stage0(3)
    inner_back(6, 12)
    start("wa")
    sc.stage1(0)
    need("norm_t")
    emit_inner(0)
    sc.stage1(1)
    emit_inner(1)
    sc.stage0(4)
    sc.stage2(0)
    emit_inner(2)
    sc.stage0(5)
    sc.stage1(2)
    emit_inner(3)
    sc.stage0(6)
    sc.stage2(1)
    need("wi", "y1", "r1")

    @pl.loop(0, 3)
    def _(n):
        rows = block(n, 192)
        d = norm_back(d_second[rows] + dot_nt(d_inner[rows], wi[...]), 4, y[rows], scale_one[rows], rows)
        tally(2, wide(low(d)))

    sc.stage0(7)
    sc.stage1(3)
    sc.stage2(2)
    need("ctx_t", "wa")
    sc.emit(8, lambda: ctx_t[...], lambda cols: d_low[:, cols])

    def part(i):
        return pl.ds(i * 768, 768)

    def pair_cols(i, j):
        return pl.ds(pl.multiple_of(i * 768 + j * 128, 128), 128)

    def head_rows(i, head):
        return pl.ds(pl.multiple_of(i * 768 + head * 64, 64), 64)

    @pl.loop(0, 3)
    def _(n):
        rows = block(n, 192)
        d_inner[rows, part(3)] = low(dot_nt(d_low[rows], wa[3]))
    act_t[part(2)] = d_inner[:, part(3)].T
    need("k", "v", "q_t", "prob_q")
    sc.stage0(8)
    sc.stage1(4)
    sc.stage2(3)
    sc.stage3(0)

    def attention(low_j, high_j):
        @pl.loop(low_j, high_j)
        def _(j):
            load_prob(j).wait()
            slot = lax.rem(j, 2)
            cols = block(j, 128)
            for start, size, rb in SPANS:
                rows = slice(start, start + size)
                kp, vp = k[rows, cols], v[rows, cols]
                dq_parts = [None] * (size // rb)
                for h in range(2):
                    probs = (lambda sl: prob[slot, h, sl]) if size == S else (lambda sl: prob_q[2 * j + h, sl])
                    mask = head_mask(h)
                    for r in range(0, size, rb):
                        d_p = dot_nt(d_inner[start + r : start + r + rb, pair_cols(3, j)] * mask, vp)
                        w = wide(probs(slice(r, r + rb)))
                        ds = low(w * (d_p - jnp.sum(w * d_p, axis=1, keepdims=True)))
                        ds_buf[h, r : r + rb, :size] = ds
                        piece = dot(ds, kp * mask)
                        i = r // rb
                        dq_parts[i] = piece if dq_parts[i] is None else dq_parts[i] + piece
                    head = 2 * j + h
                    act_t[head_rows(1, head), rows] = low(dot(act_t[head_rows(2, head), rows], probs(slice(0, size))))
                    act_t[head_rows(0, head), rows] = low(dot(q_t[head_rows(0, head), rows], ds_buf[h, :size, :size]) * 0.125)
                for i, piece in enumerate(dq_parts):
                    d_inner[start + i * rb : start + (i + 1) * rb, pair_cols(0, j)] = low(piece * 0.125)

            @pl.when(j < 4)
            def _():
                load_prob(j + 2).start()

    attention(0, 2)
    sc.stage1(5)
    sc.stage2(4)
    sc.stage3(1)
    attention(2, 4)
    sc.stage1(6)
    sc.stage2(5)
    sc.stage3(2)
    attention(4, 6)
    sc.stage1(7)
    sc.stage2(6)
    sc.stage3(3)
    d_inner[:, part(1)] = act_t[part(0)].T
    d_inner[:, part(2)] = act_t[part(1)].T
    need("x_t")

    def emit_first(n):
        row = (0, None, 1)[n]

        def bias(cols, values):
            d_vec[row : row + 1, cols] = jnp.sum(wide(values), axis=0, keepdims=True)
        sc.emit(9 + n, lambda: x_t[...], lambda cols: d_inner[:, pl.ds(pl.multiple_of(n * 768 + cols.start, 256), 256)], None if row is None else bias)

    emit_first(0)
    sc.stage1(8)
    emit_first(1)
    sc.stage0(9)
    emit_first(2)

    def vector(i, src, target):
        return remote(src, v_in.at[i], vsem.at[0, i], vsem.at[1, i], target)

    def vector_recv(i):
        vector(i, v_in.at[i], p.sib()).wait_recv()
        return v_in[i]

    vector(0, d_vec.at[:, sc.other], p.sib()).start()
    sc.stage0(10)
    sc.stage2(7)

    @pl.loop(0, 3)
    def _(n):
        rows = block(n, 192)
        d = d_second[rows]
        for i in range(3):
            d = d + dot_nt(d_inner[rows, part(i)], wa[i])
        d_low[rows] = low(d)
    mine = pltpu.make_async_copy(d_low, dx_out.at[p.c], xsem.at[0])
    theirs = remote(d_low, dx_out.at[p.c], xsem.at[1], xsem.at[2], p.sib())
    mine.start()
    theirs.start()
    sc.stage0(11)
    v_out[0] = d_vec[:, sc.own] + vector_recv(0)
    vector(1, v_out.at[0], p.n2()).start()
    sc.stage3(4)
    sc.stage1(9)
    v_out[1] = v_out[0] + vector_recv(1)
    vector(2, v_out.at[1], p.n1()).start()
    sc.stage2(8)
    sc.stage3(5)
    sc.stage1(10)
    v_out[2] = v_out[1] + vector_recv(2)
    for i in range(1, 4):
        vector(2 + i, v_out.at[2], p.up(i)).start()
    sc.stage2(9)
    sc.stage3(6)
    sc.stage1(11)
    sc.stage2(10)
    sc.stage3(7)
    dvec_out[:, sc.own] = v_out[2] + vector_recv(3) + vector_recv(4) + vector_recv(5)
    last = remote(dvec_out.at[:, sc.own], dvec_out.at[:, sc.own], vsem.at[0, 6], vsem.at[1, 6], p.sib())
    last.start()
    sc.stage2(11)
    for e in range(8, 12):
        sc.stage3(e)
    mine.wait()
    theirs.wait_send()
    remote(dx_out.at[1 - p.c], dx_out.at[1 - p.c], xsem.at[1], xsem.at[2], p.sib()).wait_recv()
    remote(dvec_out.at[:, sc.other], dvec_out.at[:, sc.other], vsem.at[0, 6], vsem.at[1, 6], p.sib()).wait_recv()
    last.wait_send()
    for i in range(6):
        vector(i, v_in.at[i], p.sib()).wait_send()
    sc.finish(12)


def backward_call(inner, lens, d_pool, vec, wa, wi, wo, saved, cid=1):
    bf, f32 = jnp.bfloat16, jnp.float32
    sds = jax.ShapeDtypeStruct
    outs = [sds((2, T, 768), bf), sds((16, 768), f32)] + [sds((48, 768), f32)] * 4 + [sds((48, 3072), f32), sds((192, 768), f32)]
    vmem = pltpu.VMEM
    scratch = [
        vmem((4, 768, 768), bf), vmem((768, 3072), bf), vmem((3072, T), bf), vmem((T, 3072), bf), vmem((T, 3072), bf),
        vmem((T, 768), f32), vmem((T, 1), f32), vmem((T, 1), f32), vmem((T, 768), f32), vmem((T, 768), bf)]
    scratch += [vmem((768, T), bf)] * 4 + [vmem((T, 768), bf)] * 2
    scratch += [vmem((2, 2, S, S), bf), vmem((12, Q, Q), bf), vmem((2, S, S), bf), vmem((16, 768), f32), vmem((6, 16, 384), f32), vmem((3, 16, 384), f32)]
    scratch += [vmem((2, 4, 4, 48, 768), bf), vmem((4, 4, 4, 48, 384), bf), vmem((12, 4, 4, 48, 384), bf), vmem((12, 2, 4, 48, 384), bf), vmem((12, 4, 48, 384), bf), vmem((12, 3, 48, 384), bf)]
    dma = pltpu.SemaphoreType.DMA
    scratch += [dma((12, 8)), dma((12, 8)), dma((19,)), dma((2,)), dma((2, 7)), dma((3,))]
    return pl.pallas_call(
        functools.partial(backward_kernel, inner),
        out_shape=outs,
        in_specs=[VM] * 3 + [ANY] * 17,
        out_specs=[ANY] + [VM] * 7,
        scratch_shapes=scratch,
        compiler_params=pltpu.CompilerParams(collective_id=cid, has_side_effects=True, vmem_limit_bytes=63 << 20),
        name="layer_backward",
    )(lens, d_pool, vec, wa, wi, wo, *saved)


def per_device(
    query_tokens, passage_tokens, lengths, positives,
    query_weight, key_weight, value_weight, output_weight, inner_weight, outer_weight,
    query_bias, value_bias, output_bias, inner_bias, outer_bias,
    first_gain, first_shift, second_gain, second_shift,
):
    inner = lax.axis_size("dp") // 16
    groups = None if inner == 1 else [[h * inner + i for i in range(inner)] for h in range(16)]
    at = lax.axis_index("dp") // inner
    seq = passage_tokens.shape[1]

    def fetch(w):
        if groups is None:
            return w
        return lax.all_gather(w, "dp", axis=0, tiled=True, axis_index_groups=groups)

    weights = [fetch(w) for w in (query_weight, key_weight, value_weight, output_weight, inner_weight, outer_weight)]
    vectors = (query_bias, value_bias, output_bias, outer_bias, first_gain, first_shift, second_gain, second_shift, inner_bias)
    v_shard = jnp.concatenate([fetch(w) for w in vectors] + [jnp.zeros((64,), query_bias.dtype)])
    d_pool, loss, lens, vec, wa, wi, wo, *saved = forward_call(
        inner, float(seq), lengths, v_shard.astype(jnp.float32)[None], positives[:, None], weights, query_tokens, passage_tokens)
    wa, wi, wo = wa.reshape(4, 768, 768), wi.reshape(768, 3072), wo.reshape(3072, 768)
    d_x, d_vec, *grads = backward_call(inner, lens, d_pool, vec, wa, wi, wo, saved)

    def finish(x):
        if groups is None:
            return x
        return lax.psum_scatter(x, "dp", scatter_dimension=0, tiled=True, axis_index_groups=groups)

    d_x = d_x.astype(jnp.float32)
    flat = lax.dynamic_slice_in_dim(d_vec[:8], at * 48, 48, 1)
    wide_bias = lax.dynamic_slice_in_dim(d_vec[8:12].reshape(3072), at * 192, 192, 0)
    rows = [finish(flat[i]) for i in range(8)]
    tail = [rows[0], rows[1], rows[2], finish(wide_bias)] + rows[3:]
    return (loss[0, 0], d_x[:, seq:], d_x[:, :seq]) + tuple(finish(g) for g in grads) + tuple(tail)


def solution(mesh):
    rows3, rows2, rows1 = P("dp", None, None), P("dp", None), P("dp")
    return jax.shard_map(
        per_device,
        mesh=mesh,
        in_specs=(rows3, rows3, P("tower", "dp"), P()) + (rows2,) * 6 + (rows1,) * 9,
        out_specs=(P(), rows3, rows3) + (rows2,) * 6 + (rows1,) * 9,
        check_vma=False,
    )
```

```python
import functools

import jax
import jax.numpy as jnp
from jax import lax
from jax.experimental import pallas as pl
from jax.experimental.pallas import tpu as pltpu
from jax.sharding import PartitionSpec as P

MESH = pl.DeviceIdType.MESH
ANY = pl.BlockSpec(memory_space=pl.ANY)
VM = pl.BlockSpec(memory_space=pltpu.VMEM)


class Place:
    def __init__(self, inner):
        dp = lax.axis_index("dp")
        self.c = lax.axis_index("tower")
        self.inner = inner
        self.low = lax.rem(dp, inner)
        self.me = dp // inner
        self.z = self.me // 4
        self.quad = lax.rem(self.me, 4)
        s1 = 1 + self.c
        s2 = 2 - self.c
        b1 = lax.rem(self.quad // s1, 2)
        b2 = lax.rem(self.quad // s2, 2)
        self.q1 = self.quad + s1 * (1 - 2 * b1)
        self.q2 = self.quad + s2 * (1 - 2 * b2)
        self.q12 = 3 - self.quad
        self.quads = (self.quad, self.q1, self.q2, self.q12)

    def ring(self, k):
        return lax.rem(self.z + k, 4)

    def dev(self, group):
        return {"dp": group * self.inner + self.low, "tower": self.c}

    def n1(self):
        return self.dev(self.z * 4 + self.q1)

    def n2(self):
        return self.dev(self.z * 4 + self.q2)

    def up(self, k):
        return self.dev(self.ring(k) * 4 + self.quad)

    def sib(self):
        return {"dp": self.me * self.inner + self.low, "tower": 1 - self.c}

    def barrier(self):
        sem = pltpu.get_barrier_semaphore()
        for target in (self.up(1), self.up(2), self.up(3), self.n1(), self.n2(), self.sib()):
            pl.semaphore_signal(sem, inc=1, device_id=target, device_id_type=MESH)
        pl.semaphore_wait(sem, 6)


def remote(src, dst, send_sem, recv_sem, target):
    return pltpu.make_async_remote_copy(
        src_ref=src, dst_ref=dst, send_sem=send_sem, recv_sem=recv_sem, device_id=target, device_id_type=MESH
    )


S, Q = 512, 64
T = S + Q


def dot(left, right):
    return jnp.dot(left, right, preferred_element_type=jnp.float32)


def dot_nt(left, right):
    return lax.dot_general(left, right, (((1,), (1,)), ((), ())), preferred_element_type=jnp.float32)


def block(index, size):
    return pl.ds(pl.multiple_of(index * size, size), size)


def low(x):
    return x.astype(jnp.bfloat16)


def wide(x):
    return x.astype(jnp.float32)


def head_mask(h):
    lane = lax.broadcasted_iota(jnp.int32, (1, 128), 1)
    return low(jnp.where(lane // 64 == h, 1.0, 0.0))


SPANS = ((0, S, 256), (S, Q, Q))


class Gather:
    def __init__(self, p, shards, wa, wi, wo, ssem, rsem, lsem):
        self.p, self.shards, self.wa, self.wi, self.wo = p, shards, wa, wi, wo
        self.ssem, self.rsem, self.lsem = ssem, rsem, lsem

    def cols(self, t, which):
        start = which * 384 if t < 4 or t > 7 else (t - 4) * 768 + which * 384
        return pl.ds(pl.multiple_of(start, 128), 384)

    def shard(self, t):
        ref = self.shards[t] if t < 4 else self.shards[4 if t < 8 else 5]
        return ref.at[:, self.cols(t, self.p.c)]

    def one(self, t, z, q):
        cols = self.cols(t, self.p.c)
        if t < 4:
            return self.wa.at[t, z, q, :, cols]
        return (self.wi if t < 8 else self.wo).at[z, q, :, cols]

    def four(self, t, q, which):
        cols = self.cols(t, which)
        if t < 4:
            return self.wa.at[t, :, q, :, cols]
        if t < 8:
            return self.wi.at[:, q, :, cols]
        return self.wo.at[self.p.ring(12 - t), q, :, cols]

    def copy(self, src, dst, t, k, target):
        return remote(src, dst, self.ssem.at[t, k], self.rsem.at[t, k], target)

    def recv(self, t, k, ref):
        self.copy(ref, ref, t, k, self.p.sib()).wait_recv()

    def push(self, t, q, k, target):
        view = self.four(t, q, self.p.c)
        self.copy(view, view, t, k, target).start()

    def steps(self, t):
        return range(1, 4) if t < 8 else range(t - 8, t - 7) if t > 8 else ()

    def local(self, t):
        return pltpu.make_async_copy(self.shard(t), self.one(t, self.p.z, self.p.quad), self.lsem.at[t])

    def push_one(self, t, z, q, k, target):
        view = self.one(t, z, q)
        self.copy(view, view, t, k, target).start()

    def direct(self, t):
        return t not in TURNED

    def stage_own(self, t):
        p = self.p
        if t <= 8:
            self.local(t).start()
        for k in self.steps(t):
            self.copy(self.shard(t), self.one(t, p.z, p.quad), t, k, p.up(k)).start()
        if t <= 8:
            self.copy(self.shard(t), self.one(t, p.z, p.quad), t, 4, p.n1()).start()
            self.copy(self.shard(t), self.one(t, p.z, p.quad), t, 5, p.n2()).start()

    def stage_z(self, t):
        p = self.p
        if not self.direct(t):
            self.recv(t, 4, self.one(t, p.z, p.q1))
            for k in range(1, 4):
                self.push_one(t, p.z, p.q1, 11 + k, p.up(k))
            self.push_one(t, p.z, p.q1, 6, p.n2())
        for k in self.steps(t):
            z = p.ring(4 - k)
            self.recv(t, k, self.one(t, z, p.quad))
            if self.direct(t):
                self.push_one(t, z, p.quad, 4, p.n1())
            self.push_one(t, z, p.quad, 5, p.n2())
        if t <= 8:
            self.local(t).wait()
        self.push(t, p.quad, 8, p.sib())

    def stage_one(self, t):
        p = self.p
        if self.direct(t):
            self.recv(t, 4, self.four(t, p.q1, p.c))
            self.push(t, p.q1, 6, p.n2())
        else:
            for k in range(1, 4):
                z = p.ring(4 - k)
                self.recv(t, 11 + k, self.one(t, z, p.q1))
                self.push_one(t, z, p.q1, 6, p.n2())
        self.push(t, p.q1, 9, p.sib())

    def stage_two(self, t):
        p = self.p
        for k, q in ((5, p.q2), (6, p.q12)):
            self.recv(t, k, self.four(t, q, p.c))
            self.push(t, q, k + 5, p.sib())

    def stage_sib(self, t):
        p = self.p
        for k, q in ((8, p.quad), (9, p.q2), (10, p.q1), (11, p.q12)):
            self.recv(t, k, self.four(t, q, 1 - p.c))

    def tick(self, i):
        for lag, stage in ((0, self.stage_z), (-AHEAD, self.stage_own), (LAGS[0], self.stage_one), (LAGS[1], self.stage_two), (LAGS[2], self.stage_sib)):
            if 0 <= i - lag < 12:
                stage(i - lag)

    def finish(self):
        p = self.p
        for t in range(12):
            single, view = self.one(t, p.z, p.quad), self.four(t, p.quad, p.c)
            for k in self.steps(t):
                self.copy(single, single, t, k, p.sib()).wait_send()
            for k in (4, 5, 6, 8, 9, 10, 11):
                shape = single if k == 4 and not self.direct(t) else view
                self.copy(shape, shape, t, k, p.sib()).wait_send()
            for k in () if self.direct(t) else (12, 13, 14):
                self.copy(single, single, t, k, p.sib()).wait_send()


def expand_vectors(shards, vec):
    at = wide(lax.broadcasted_iota(jnp.int32, (1, 768), 1))
    owner = jnp.floor((at + 0.5) * (1.0 / 48))
    lane = wide(lax.broadcasted_iota(jnp.int32, (128, 1), 0))
    rows = dot(shards.reshape(256, 128), low(jnp.where(lane == at - owner * 48, 1.0, 0.0))).reshape(16, 16, 768)
    shard = wide(lax.broadcasted_iota(jnp.int32, (16, 1, 1), 0))
    vec[:8, :768] = jnp.sum(jnp.where(owner[None] == shard, rows[:, :8], 0.0), axis=0)
    piece = wide(lax.broadcasted_iota(jnp.int32, (4, 4, 1), 0) * 4 + lax.broadcasted_iota(jnp.int32, (4, 4, 1), 1))
    for n in range(4):
        mine = jnp.sum(jnp.where(owner[None] == piece, rows[4 * n : 4 * n + 4, 8:12], 0.0), axis=0)
        vec[8:9, n * 768 : (n + 1) * 768] = jnp.sum(mine, axis=0, keepdims=True)


def forward_kernel(inner, seq, lengths, targets, b_query, b_value, b_output, b_outer, gain_one, shift_one, gain_two, shift_two, b_inner, w_query, w_key, w_value, w_output, w_inner, w_outer, query_tokens, passage_tokens,
                   d_pool, loss, lens, vec, wa_out, wi_out, wo_out,
                   k_out, v_out, prob_out, prob_q_out, x_t_out, q_t_out, ctx_t_out, norm_t_out, act_t_out, slope_out, y1_out, r1_out, y2_out, r2_out,
                   wa, wi, wo, x, q, k, v, prob, prob_q, ctx, normed, act, act_t, slope, x_t, q_t, ctx_t, norm_t, y1, r1, y2, r2, pooled, rows, packed, vectors, len_buf,
                   ssem, rsem, lsem, vsem, osem, psem, xsem):
    p = Place(inner)
    pairs = targets.shape[1]
    me = lax.axis_index("dp") * 2 + p.c

    def device(at):
        return {"dp": at // 2, "tower": lax.rem(at, 2)}

    x_loads = [pltpu.make_async_copy(passage_tokens.at[p.c], x.at[pl.ds(0, S)], xsem.at[0]), pltpu.make_async_copy(query_tokens.at[p.c], x.at[pl.ds(S, Q)], xsem.at[1])]
    for copy in x_loads:
        copy.start()
    barrier = pltpu.get_barrier_semaphore()

    @pl.loop(1, pairs)
    def _(i):
        pl.semaphore_signal(barrier, inc=1, device_id=device(lax.rem(me + i, pairs)), device_id_type=MESH)
    lane = lax.broadcasted_iota(jnp.int32, (8, 128), 1)
    len_buf[p.c] = jnp.where(lane == 0, lengths[0, 0].astype(jnp.float32), lengths[0, 1].astype(jnp.float32))
    packed[...] = jnp.zeros((16, 128), jnp.float32)
    for i, ref in enumerate((b_query, b_value, b_output, b_outer, gain_one, shift_one, gain_two, shift_two)):
        packed[i : i + 1, :48] = wide(ref[...])
    last = wide(b_inner[...]).reshape(1, 192)
    for i in range(4):
        packed[8 + i : 9 + i, :48] = last[:, i * 48 : i * 48 + 48]
    vectors[p.z, p.quad] = low(packed[...])
    pl.semaphore_wait(barrier, pairs - 1)

    gather = Gather(p, (w_query, w_key, w_value, w_output, w_inner, w_outer), wa, wi, wo, ssem, rsem, lsem)
    for t in range(AHEAD):
        gather.stage_own(t)
    len_copy = remote(len_buf.at[p.c], len_buf.at[p.c], xsem.at[2], xsem.at[3], p.sib())
    len_copy.start()

    def vector(i, q, target):
        view = vectors.at[p.z, p.quad] if i < 4 else vectors.at[:, q]
        return remote(view, view, vsem.at[0, i], vsem.at[1, i], target)

    for i in range(1, 4):
        vector(i, None, p.up(i)).start()
    saves = []

    def save(src, dst):
        copy = pltpu.make_async_copy(src, dst, osem.at[len(saves)])
        copy.start()
        saves.append(copy)

    for copy in x_loads:
        copy.wait()
    x_t[...] = x[...].T
    save(x_t, x_t_out)
    gather.tick(0)
    for i in range(1, 4):
        view = vectors.at[p.ring(4 - i), p.quad]
        remote(view, view, vsem.at[0, i], vsem.at[1, i], p.sib()).wait_recv()
    vector(4, p.quad, p.n1()).start()
    vector(5, p.quad, p.n2()).start()
    gather.tick(1)
    vector(4, p.q1, p.sib()).wait_recv()
    vector(6, p.q1, p.n2()).start()
    for i in range(2, LAGS[2]):
        gather.tick(i)
    vector(5, p.q2, p.sib()).wait_recv()
    vector(6, p.q12, p.sib()).wait_recv()
    expand_vectors(vectors[...], vec)
    remote(len_buf.at[1 - p.c], len_buf.at[1 - p.c], xsem.at[2], xsem.at[3], p.sib()).wait_recv()
    len_q, len_p = [jnp.sum(jnp.where(lane[:1] == p.c, len_buf[i, 0:1], 0.0), axis=1, keepdims=True) for i in range(2)]
    lens[0:1] = jnp.broadcast_to(len_p, (1, 128))
    lens[1:2] = jnp.broadcast_to(len_q, (1, 128))
    lens[2:8] = jnp.zeros((6, 128), jnp.float32)

    def project(m, out, row):
        @pl.loop(0, 3)
        def _(n):
            cols = block(n, 256)
            acc = dot(x[...], wa[m, :, :, :, cols].reshape(768, 256))
            if row is not None:
                acc = acc + vec[row : row + 1, cols]
            out[:, cols] = low(acc)

    gather.tick(LAGS[2] + 0)
    project(0, q, 0)
    gather.tick(LAGS[2] + 1)
    project(1, k, None)
    q_t[...] = q[...].T
    save(q_t, q_t_out)
    save(k, k_out)
    gather.tick(LAGS[2] + 2)
    project(2, v, 1)
    save(v, v_out)

    def store_prob(j):
        return pltpu.make_async_copy(prob.at[lax.rem(j, 2)], prob_out.at[pl.ds(j * 2, 2)], psem.at[lax.rem(j, 2)])

    def attention(low_j, high_j):
        @pl.loop(low_j, high_j)
        def _(j):
            cols = block(j, 128)
            slot = lax.rem(j, 2)

            @pl.when(j >= 2)
            def _():
                store_prob(j - 2).wait()

            for (start, size, rb), length in zip(SPANS, (len_p, len_q)):
                span = slice(start, start + size)
                kp, vp = k[span, cols], v[span, cols]
                valid = wide(lax.broadcasted_iota(jnp.int32, (1, size), 1)) < length
                for r in range(0, size, rb):
                    qp = q[start + r : start + r + rb, cols]
                    total = None
                    for h in range(2):
                        mask = head_mask(h)
                        scores = dot_nt(qp * (mask * 0.125), kp)
                        scores = jnp.where(valid, scores, -1e9)
                        e = jnp.exp(scores - jnp.max(scores, axis=1, keepdims=True))
                        w = low(e * (1.0 / jnp.sum(e, axis=1, keepdims=True)))
                        if size == S:
                            prob[slot, h, r : r + rb] = w
                        else:
                            prob_q[2 * j + h] = w
                        piece = dot(w, vp * mask)
                        total = piece if total is None else total + piece
                    ctx[start + r : start + r + rb, cols] = low(total)
            store_prob(j).start()

    gather.tick(LAGS[2] + 3)
    save(wa, wa_out)
    attention(0, 2)
    gather.tick(LAGS[2] + 4)
    attention(2, 4)
    gather.tick(LAGS[2] + 5)
    attention(4, 6)
    save(prob_q, prob_q_out)
    ctx_t[...] = ctx[...].T
    save(ctx_t, ctx_t_out)

    def gain(row):
        return vec[row : row + 1, :768]

    @pl.loop(0, 3)
    def _(n):
        span = block(n, 192)
        first = wide(x[span]) + (dot(ctx[span], wa[3].reshape(768, 768)) + gain(2))
        center = first - jnp.mean(first, axis=1, keepdims=True)
        scale = lax.rsqrt(jnp.mean(center * center, axis=1, keepdims=True) + 1e-12)
        y = center * scale
        y1[span] = y
        r1[span] = scale
        normed[span] = low(y * gain(4) + gain(5))
    save(y1, y1_out)
    save(r1, r1_out)
    norm_t[...] = normed[...].T
    save(norm_t, norm_t_out)

    def hidden(low_n, high_n):
        @pl.loop(low_n, high_n)
        def _(n):
            cols = block(n, 256)
            u = dot(normed[...], wi[:, :, :, cols].reshape(768, 256)) + vec[8:9, cols]
            cdf = 0.5 * (1.0 + lax.erf(u * 0.7071067811865476))
            act[:, cols] = low(u * cdf)
            slope[:, cols] = low(cdf + u * (0.3989422804014327 * jnp.exp(-0.5 * u * u)))

    gather.tick(LAGS[2] + 6)
    hidden(0, 9)
    gather.tick(LAGS[2] + 7)
    save(wi, wi_out)
    hidden(9, 12)
    save(slope, slope_out)

    for b in range(4):
        turned = act[:, b * 768 : (b + 1) * 768].T
        for s in range(4):
            for n in range(4):
                row = n * 768 + (b * 4 + s) * 48
                act_t[row : row + 48] = turned[s * 192 + n * 48 : s * 192 + n * 48 + 48]
    save(act_t, act_t_out)
    pooled[...] = jnp.zeros_like(pooled)

    def outer(i):
        plane = p.ring(4 - i)

        @pl.loop(0, 3)
        def _(n):
            span = block(n, 192)
            add = dot(act[span, pl.ds(pl.multiple_of(plane * 768, 128), 768)], wo[plane].reshape(768, 768))
            if i == 0:
                add = add + (y1[span] * gain(4) + gain(5) + gain(3))
            else:
                add = add + y2[span]
            if i < 3:
                y2[span] = add
                return
            center = add - jnp.mean(add, axis=1, keepdims=True)
            scale = lax.rsqrt(jnp.mean(center * center, axis=1, keepdims=True) + 1e-12)
            y = center * scale
            y2[span] = y
            r2[span] = scale
            out = y * gain(6) + gain(7)
            at = wide(lax.broadcasted_iota(jnp.int32, (192, 1), 0) + n * 192)
            for row, keep in ((0, (at >= S) & (at - S < len_q)), (1, (at < S) & (at < len_p))):
                pooled[row : row + 1] += jnp.sum(jnp.where(keep, out, 0.0), axis=0, keepdims=True)

    for i in range(4):
        gather.tick(LAGS[2] + 8 + i)
        outer(i)

    mine = jnp.concatenate([pooled[0:1] / len_q, pooled[1:2] / len_p])
    root = jnp.sqrt(jnp.sum(mine * mine, axis=1, keepdims=True) + 1e-6)
    unit = mine / root
    rows[me] = unit

    @pl.loop(1, pairs)
    def _(i):
        remote(rows.at[me], rows.at[me], xsem.at[4], xsem.at[5], device(lax.rem(me + i, pairs))).start()
    save(y2, y2_out)
    save(r2, r2_out)
    save(wo, wo_out)
    gather.finish()
    len_copy.wait_send()
    for i in range(1, 7):
        vector(i, p.quad, p.sib()).wait_send()
    store_prob(4).wait()
    store_prob(5).wait()
    rest = rows.at[pl.ds(0, pairs - 1)]
    remote(rest, rest, xsem.at[4], xsem.at[5], p.sib()).wait_recv()
    exact = lax.Precision.HIGHEST
    qs, ps = rows[:, 0, :], rows[:, 1, :]
    logits = lax.dot_general(ps, qs, (((1,), (1,)), ((), ())), precision=exact, preferred_element_type=jnp.float32) / 0.01
    hit = targets[...] == lax.broadcasted_iota(jnp.int32, (pairs, pairs), 0)
    top = jnp.max(logits, axis=0, keepdims=True)
    lse = jnp.log(jnp.sum(jnp.exp(logits - top), axis=0, keepdims=True)) + top
    picked = jnp.sum(jnp.where(hit, logits, 0.0), axis=0, keepdims=True)
    loss[...] = jnp.broadcast_to(jnp.sum(lse - picked, axis=1, keepdims=True) / pairs, loss.shape)
    d_logits = seq * (jnp.exp(logits - lse) - jnp.where(hit, 1.0, 0.0))
    d_p = jnp.dot(d_logits, qs, precision=exact, preferred_element_type=jnp.float32) / 0.01
    d_q = lax.dot_general(d_logits, ps, (((0,), (0,)), ((), ())), precision=exact, preferred_element_type=jnp.float32) / 0.01
    own = lax.broadcasted_iota(jnp.int32, (pairs, 1), 0) == me
    for row, d in enumerate((d_q, d_p)):
        d_unit = jnp.sum(jnp.where(own, d, 0.0), axis=0, keepdims=True)
        u = unit[row : row + 1]
        d_pool[row : row + 1] = (d_unit - u * jnp.sum(u * d_unit, axis=1, keepdims=True)) / root[row : row + 1]
    remote(rest, rest, xsem.at[4], xsem.at[5], p.sib()).wait_send()
    for copy in saves:
        copy.wait()


AHEAD = 2
LAGS = (1, 3, 4)
TURNED = ()


def forward_call(inner, seq, lengths, targets, vectors, weights, query_tokens, passage_tokens, cid=0):
    bf, f32 = jnp.bfloat16, jnp.float32
    sds, vmem, dma = jax.ShapeDtypeStruct, pltpu.VMEM, pltpu.SemaphoreType.DMA
    pairs = targets.shape[1]
    stored = [((T, 768), bf)] * 2 + [((12, S, S), bf), ((12, Q, Q), bf)] + [((768, T), bf)] * 4 + [
        ((3072, T), bf), ((T, 3072), bf), ((T, 768), f32), ((T, 1), f32), ((T, 768), f32), ((T, 1), f32)]
    full = [((4, 4, 4, 48, 768), bf), ((4, 4, 48, 3072), bf), ((4, 4, 192, 768), bf)]
    outs = [((2, 768), f32), ((8, 128), f32), ((8, 128), f32), ((16, 3072), f32)] + full + stored
    rows = (T, 768)
    scratch = [vmem(*w) for w in full] + [vmem(rows, bf)] * 4 + [vmem((2, 2, S, S), bf), vmem((12, Q, Q), bf)] + [vmem(rows, bf)] * 2
    scratch += [vmem((T, 3072), bf), vmem((3072, T), bf), vmem((T, 3072), bf)] + [vmem((768, T), bf)] * 4
    scratch += [vmem(rows, f32), vmem((T, 1), f32), vmem(rows, f32), vmem((T, 1), f32), vmem((2, 768), f32)]
    scratch += [vmem((pairs, 2, 768), f32), vmem((16, 128), f32), vmem((4, 4, 16, 128), bf), vmem((2, 8, 128), f32)]
    scratch += [dma((12, 16)), dma((12, 16)), dma((9,)), dma((2, 7)), dma((17,)), dma((2,)), dma((6,))]
    return pl.pallas_call(
        functools.partial(forward_kernel, inner, seq),
        out_shape=[sds(*o) for o in outs],
        in_specs=[pl.BlockSpec(memory_space=pltpu.SMEM)] + [VM] * 10 + [ANY] * 8,
        out_specs=[VM] * 4 + [ANY] * 17,
        scratch_shapes=scratch,
        compiler_params=pltpu.CompilerParams(collective_id=cid, has_side_effects=True, vmem_limit_bytes=62 << 20),
        name="layer_forward",
    )(lengths, targets, *vectors, *weights, query_tokens, passage_tokens)


class Scatter:
    def __init__(self, p, refs, result):
        self.p = p
        self.stage, self.r0, self.acc, self.r1, self.r2, self.r3, self.ssem, self.rsem = refs
        self.result = result
        self.own = pl.ds(pl.multiple_of(p.c * 384, 128), 384)
        self.other = pl.ds(pl.multiple_of((1 - p.c) * 384, 128), 384)

    def copy(self, src, dst, e, k, target):
        return remote(src, dst, self.ssem.at[e, k], self.rsem.at[e, k], target)

    def recv(self, e, k, ref):
        self.copy(ref, ref, e, k, self.p.sib()).wait_recv()

    def emit(self, e, left, right, extra=None):
        if e >= 2:
            self.shared(e - 2).wait_send()

        @pl.loop(0, 3)
        def _(n):
            cols = block(n, 256)
            values = right(cols)
            self.stage[e % 2, :, :, :, cols] = low(dot(left(), values)).reshape(4, 4, 48, 256)
            if extra is not None:
                extra(cols, values)
        self.shared(e).start()

    def shared(self, e):
        return self.copy(self.stage.at[e % 2, :, :, :, self.other], self.r0.at[e % 4], e, 0, self.p.sib())

    def stage0(self, e):
        p, acc = self.p, self.acc
        self.recv(e, 0, self.r0.at[e % 4])
        for j, q in enumerate((p.q2, p.q12, p.q1, p.quad)):
            acc[e, :, q] = self.stage[e % 2, :, q, :, self.own] + self.r0[e % 4, :, q]
            if j < 2:
                self.copy(acc.at[e, :, q], self.r1.at[e, j], e, 1 + j, p.n2()).start()

    def stage1(self, e):
        p, acc = self.p, self.acc
        self.recv(e, 2, self.r1.at[e, 1])
        acc[e, :, p.q1] += self.r1[e, 1]
        self.copy(acc.at[e, :, p.q1], self.r2.at[e], e, 3, p.n1()).start()
        self.recv(e, 1, self.r1.at[e, 0])
        acc[e, :, p.quad] += self.r1[e, 0]

    def stage2(self, e):
        p, acc = self.p, self.acc
        self.recv(e, 3, self.r2.at[e])
        acc[e, :, p.quad] += self.r2[e]
        for k in range(1, 4):
            self.copy(acc.at[e, p.ring(k), p.quad], self.r3.at[e, k - 1], e, 3 + k, p.up(k)).start()

    def stage3(self, e):
        p = self.p
        total = wide(self.acc[e, p.z, p.quad])
        for k in range(1, 4):
            self.recv(e, 3 + k, self.r3.at[e, k - 1])
            total = total + wide(self.r3[e, k - 1])
        view = self.result(e, p.c)
        view[...] = total
        self.copy(view, view, e, 7, p.sib()).start()

    def finish(self, count):
        for e in range(count):
            self.recv(e, 7, self.result(e, 1 - self.p.c))
            self.copy(self.result(e, self.p.c), self.result(e, self.p.c), e, 7, self.p.sib()).wait_send()
        for e in range(count - 2, count):
            self.shared(e).wait_send()
        four, one = self.r2.at[0], self.r3.at[0, 0]

        @pl.loop(0, count)
        def _(e):
            for k in range(1, 7):
                view = four if k < 4 else one
                self.copy(view, view, e, k, self.p.sib()).wait_send()


def backward_kernel(inner, lens, d_pool, vec, a_hbm, i_hbm, o_hbm, k_hbm, v_hbm, prob_hbm, prob_q_hbm, x_t_hbm, q_t_hbm, ctx_t_hbm, norm_t_hbm,
                    act_t_hbm, slope_hbm, y1_hbm, r1_hbm, y2_hbm, r2_hbm,
                    dxq_out, dxp_out, dvec_out, g_query, g_key, g_value, g_output, g_inner, g_outer,
                    wa, wi, act_t, slope, d_inner, y, scale_one, scale_two, d_second, d_low, norm_t, ctx_t, x_t, q_t, k, v, prob, prob_q, ds_buf,
                    d_vec, v_in, v_out, stage, r0, acc, r1, r2, r3, ssem, rsem, lsem, psem, vsem, xsem):
    p = Place(inner)

    def load(i, src, dst):
        return pltpu.make_async_copy(src, dst, lsem.at[i])

    loads = {
        "y2": load(0, y2_hbm, y), "r2": load(1, r2_hbm, scale_two), "act_t": load(2, act_t_hbm, act_t),
        "slope": load(7, slope_hbm, slope), "norm_t": load(8, norm_t_hbm, norm_t), "wi": load(9, i_hbm, wi),
        "y1": load(10, y1_hbm, y), "r1": load(11, r1_hbm, scale_one), "ctx_t": load(12, ctx_t_hbm, ctx_t), "wa": load(13, a_hbm, wa),
        "k": load(14, k_hbm, k), "v": load(15, v_hbm, v), "q_t": load(16, q_t_hbm, q_t), "x_t": load(17, x_t_hbm, x_t), "prob_q": load(18, prob_q_hbm, prob_q),
    }
    for n in range(4):
        loads["wo%d" % n] = load(3 + n, o_hbm.at[pl.ds(n * 768, 768)], wa.at[n])

    def start(*names):
        for name in names:
            loads[name].start()

    def need(*names):
        for name in names:
            loads[name].wait()

    def load_prob(j):
        return pltpu.make_async_copy(prob_hbm.at[pl.ds(j * 2, 2)], prob.at[lax.rem(j, 2)], psem.at[lax.rem(j, 2)])

    start("y2", "r2", "act_t", "wo0", "wo1", "wo2", "wo3", "slope", "norm_t", "wi", "r1", "ctx_t", "k", "v", "q_t", "x_t", "prob_q")
    load_prob(0).start()
    load_prob(1).start()
    p.barrier()

    def result(e, which):
        cols = pl.ds(pl.multiple_of(which * 384, 128), 384)
        if e < 4:
            return g_outer.at[pl.ds(e * 48, 48), cols]
        if e < 8:
            return g_inner.at[:, pl.ds(pl.multiple_of((e - 4) * 768 + which * 384, 128), 384)]
        return (g_output, g_query, g_key, g_value)[e - 8].at[:, cols]

    sc = Scatter(p, (stage, r0, acc, r1, r2, r3, ssem, rsem), result)
    d_vec[...] = jnp.zeros_like(d_vec)

    def gain(row):
        return vec[row : row + 1, :768]

    def tally(row, value):
        d_vec[row : row + 1] += jnp.sum(value, axis=0, keepdims=True)

    len_p, len_q = lens[0:1, 0:1], lens[1:2, 0:1]
    pool_q = d_pool[0:1] / len_q
    pool_p = d_pool[1:2] / len_p

    def norm_back(d, row, yy, scale, rows):
        tally(row, d * yy)
        tally(row + 1, d)
        g = d * gain(row)
        d = (g - jnp.mean(g, axis=1, keepdims=True) - yy * jnp.mean(g * yy, axis=1, keepdims=True)) * scale
        d_second[rows] = d
        d_low[rows] = low(d)
        return d

    need("y2", "r2")

    @pl.loop(0, 3)
    def _(n):
        rows = block(n, 192)
        at = wide(lax.broadcasted_iota(jnp.int32, (192, 1), 0) + n * 192)
        d_rows = jnp.where(at < S, jnp.where(at < len_p, pool_p, 0.0), jnp.where(at - S < len_q, pool_q, 0.0))
        d = norm_back(d_rows, 6, y[rows], scale_two[rows], rows)
        tally(3, wide(low(d)))

    start("y1")
    need("act_t")

    def emit_outer(n):
        sc.emit(n, lambda: act_t[n * 768 : (n + 1) * 768], lambda cols: d_low[:, cols])

    def emit_inner(n):
        def bias(cols, values):
            d_vec[8 + n : 9 + n, cols] = jnp.sum(wide(values), axis=0, keepdims=True)
        sc.emit(4 + n, lambda: norm_t[...], lambda cols: d_inner[:, pl.ds(pl.multiple_of(n * 768 + cols.start, 256), 256)], bias)

    emit_outer(0)
    emit_outer(1)
    sc.stage0(0)
    emit_outer(2)
    sc.stage0(1)
    emit_outer(3)
    sc.stage0(2)
    need("wo0", "wo1", "wo2", "wo3", "slope")

    def inner_back(low_n, high_n):
        @pl.loop(low_n, high_n)
        def _(n):
            cols = block(n, 256)
            d_inner[:, cols] = low(dot_nt(d_low[...], wa[n // 3, block(lax.rem(n, 3), 256)]) * wide(slope[:, cols]))

    inner_back(0, 6)
    sc.stage0(3)
    inner_back(6, 12)
    start("wa")
    sc.stage1(0)
    need("norm_t")
    emit_inner(0)
    sc.stage1(1)
    emit_inner(1)
    sc.stage0(4)
    sc.stage2(0)
    emit_inner(2)
    sc.stage0(5)
    sc.stage1(2)
    emit_inner(3)
    sc.stage0(6)
    sc.stage2(1)
    need("wi", "y1", "r1")

    @pl.loop(0, 3)
    def _(n):
        rows = block(n, 192)
        d = norm_back(d_second[rows] + dot_nt(d_inner[rows], wi[...]), 4, y[rows], scale_one[rows], rows)
        tally(2, wide(low(d)))

    sc.stage0(7)
    sc.stage1(3)
    sc.stage2(2)
    need("ctx_t", "wa")
    sc.emit(8, lambda: ctx_t[...], lambda cols: d_low[:, cols])

    def part(i):
        return pl.ds(i * 768, 768)

    def pair_cols(i, j):
        return pl.ds(pl.multiple_of(i * 768 + j * 128, 128), 128)

    def head_rows(i, head):
        return pl.ds(pl.multiple_of(i * 768 + head * 64, 64), 64)

    @pl.loop(0, 3)
    def _(n):
        rows = block(n, 192)
        d_inner[rows, part(3)] = low(dot_nt(d_low[rows], wa[3]))
    act_t[part(2)] = d_inner[:, part(3)].T
    need("k", "v", "q_t", "prob_q")
    sc.stage0(8)
    sc.stage1(4)
    sc.stage2(3)
    sc.stage3(0)

    def attention(low_j, high_j):
        @pl.loop(low_j, high_j)
        def _(j):
            load_prob(j).wait()
            slot = lax.rem(j, 2)
            cols = block(j, 128)
            for start, size, rb in SPANS:
                rows = slice(start, start + size)
                kp, vp = k[rows, cols], v[rows, cols]
                dq_parts = [None] * (size // rb)
                for h in range(2):
                    probs = (lambda sl: prob[slot, h, sl]) if size == S else (lambda sl: prob_q[2 * j + h, sl])
                    mask = head_mask(h)
                    for r in range(0, size, rb):
                        d_p = dot_nt(d_inner[start + r : start + r + rb, pair_cols(3, j)] * mask, vp)
                        w = wide(probs(slice(r, r + rb)))
                        ds = low(w * (d_p - jnp.sum(w * d_p, axis=1, keepdims=True)))
                        ds_buf[h, r : r + rb, :size] = ds
                        piece = dot(ds, kp * mask)
                        i = r // rb
                        dq_parts[i] = piece if dq_parts[i] is None else dq_parts[i] + piece
                    head = 2 * j + h
                    act_t[head_rows(1, head), rows] = low(dot(act_t[head_rows(2, head), rows], probs(slice(0, size))))
                    act_t[head_rows(0, head), rows] = low(dot(q_t[head_rows(0, head), rows], ds_buf[h, :size, :size]) * 0.125)
                for i, piece in enumerate(dq_parts):
                    d_inner[start + i * rb : start + (i + 1) * rb, pair_cols(0, j)] = low(piece * 0.125)

            @pl.when(j < 4)
            def _():
                load_prob(j + 2).start()

    attention(0, 2)
    sc.stage1(5)
    sc.stage2(4)
    sc.stage3(1)
    attention(2, 4)
    sc.stage1(6)
    sc.stage2(5)
    sc.stage3(2)
    attention(4, 6)
    sc.stage1(7)
    sc.stage2(6)
    sc.stage3(3)
    d_inner[:, part(1)] = act_t[part(0)].T
    d_inner[:, part(2)] = act_t[part(1)].T
    need("x_t")

    def emit_first(n):
        row = (0, None, 1)[n]

        def bias(cols, values):
            d_vec[row : row + 1, cols] = jnp.sum(wide(values), axis=0, keepdims=True)
        sc.emit(9 + n, lambda: x_t[...], lambda cols: d_inner[:, pl.ds(pl.multiple_of(n * 768 + cols.start, 256), 256)], None if row is None else bias)

    emit_first(0)
    sc.stage1(8)
    emit_first(1)
    sc.stage0(9)
    emit_first(2)

    def vector(i, src, target):
        return remote(src, v_in.at[i], vsem.at[0, i], vsem.at[1, i], target)

    def vector_recv(i):
        vector(i, v_in.at[i], p.sib()).wait_recv()
        return v_in[i]

    vector(0, d_vec.at[:, sc.other], p.sib()).start()
    sc.stage0(10)
    sc.stage2(7)

    @pl.loop(0, 3)
    def _(n):
        rows = block(n, 192)
        d = d_second[rows]
        for i in range(3):
            d = d + dot_nt(d_inner[rows, part(i)], wa[i])
        d_low[rows] = low(d)
    tokens = [(d_low.at[pl.ds(0, S)], dxp_out), (d_low.at[pl.ds(S, Q)], dxq_out)]
    mine = [pltpu.make_async_copy(src, out.at[p.c], xsem.at[i]) for i, (src, out) in enumerate(tokens)]
    theirs = [remote(src, out.at[p.c], xsem.at[2 + i], xsem.at[4 + i], p.sib()) for i, (src, out) in enumerate(tokens)]
    for copy in mine + theirs:
        copy.start()
    sc.stage0(11)
    v_out[0] = d_vec[:, sc.own] + vector_recv(0)
    vector(1, v_out.at[0], p.n2()).start()
    sc.stage3(4)
    sc.stage1(9)
    v_out[1] = v_out[0] + vector_recv(1)
    vector(2, v_out.at[1], p.n1()).start()
    sc.stage2(8)
    sc.stage3(5)
    sc.stage1(10)
    v_out[2] = v_out[1] + vector_recv(2)
    for i in range(1, 4):
        vector(2 + i, v_out.at[2], p.up(i)).start()
    sc.stage2(9)
    sc.stage3(6)
    sc.stage1(11)
    sc.stage2(10)
    sc.stage3(7)
    dvec_out[:, sc.own] = v_out[2] + vector_recv(3) + vector_recv(4) + vector_recv(5)
    last = remote(dvec_out.at[:, sc.own], dvec_out.at[:, sc.own], vsem.at[0, 6], vsem.at[1, 6], p.sib())
    last.start()
    sc.stage2(11)
    for e in range(8, 12):
        sc.stage3(e)
    for i, (src, out) in enumerate(tokens):
        mine[i].wait()
        theirs[i].wait_send()
        remote(out.at[1 - p.c], out.at[1 - p.c], xsem.at[2 + i], xsem.at[4 + i], p.sib()).wait_recv()
    remote(dvec_out.at[:, sc.other], dvec_out.at[:, sc.other], vsem.at[0, 6], vsem.at[1, 6], p.sib()).wait_recv()
    last.wait_send()
    for i in range(6):
        vector(i, v_in.at[i], p.sib()).wait_send()
    sc.finish(12)


def backward_call(inner, lens, d_pool, vec, wa, wi, wo, saved, cid=1):
    bf, f32 = jnp.bfloat16, jnp.float32
    sds = jax.ShapeDtypeStruct
    outs = [sds((2, Q, 768), bf), sds((2, S, 768), bf), sds((16, 768), f32)] + [sds((48, 768), f32)] * 4 + [sds((48, 3072), f32), sds((192, 768), f32)]
    vmem = pltpu.VMEM
    scratch = [
        vmem((4, 768, 768), bf), vmem((768, 3072), bf), vmem((3072, T), bf), vmem((T, 3072), bf), vmem((T, 3072), bf),
        vmem((T, 768), f32), vmem((T, 1), f32), vmem((T, 1), f32), vmem((T, 768), f32), vmem((T, 768), bf)]
    scratch += [vmem((768, T), bf)] * 4 + [vmem((T, 768), bf)] * 2
    scratch += [vmem((2, 2, S, S), bf), vmem((12, Q, Q), bf), vmem((2, S, S), bf), vmem((16, 768), f32), vmem((6, 16, 384), f32), vmem((3, 16, 384), f32)]
    scratch += [vmem((2, 4, 4, 48, 768), bf), vmem((4, 4, 4, 48, 384), bf), vmem((12, 4, 4, 48, 384), bf), vmem((12, 2, 4, 48, 384), bf), vmem((12, 4, 48, 384), bf), vmem((12, 3, 48, 384), bf)]
    dma = pltpu.SemaphoreType.DMA
    scratch += [dma((12, 8)), dma((12, 8)), dma((19,)), dma((2,)), dma((2, 7)), dma((6,))]
    return pl.pallas_call(
        functools.partial(backward_kernel, inner),
        out_shape=outs,
        in_specs=[VM] * 3 + [ANY] * 17,
        out_specs=[ANY] * 2 + [VM] * 7,
        scratch_shapes=scratch,
        compiler_params=pltpu.CompilerParams(collective_id=cid, has_side_effects=True, vmem_limit_bytes=63 << 20),
        name="layer_backward",
    )(lens, d_pool, vec, wa, wi, wo, *saved)


def outputs_kernel(inner, loss_in, dxq, dxp, d_vec, *refs):
    grads, (loss, q_out, p_out), g_outs, v_outs = refs[:6], refs[6:9], refs[9:15], refs[15:24]
    q_low, p_low, q_wide, p_wide, isem, osem, gsem = refs[24:]
    copies = [pltpu.make_async_copy(src, dst, gsem.at[i]) for i, (src, dst) in enumerate(zip(grads, g_outs))]
    parts = [(dxp.at[i, pl.ds(r, 256)], p_low.at[i, pl.ds(r, 256)], p_wide.at[i, pl.ds(r, 256)], p_out.at[i, pl.ds(r, 256)]) for i in range(2) for r in (0, 256)]
    parts.append((dxq, q_low, q_wide, q_out))
    loads = [pltpu.make_async_copy(part[0], part[1], isem.at[i]) for i, part in enumerate(parts)]
    for copy in loads + copies:
        copy.start()
    loss[...] = loss_in[0:1, 0:1]
    shard = lax.axis_index("dp") // inner
    for size, first, outs in ((48, 0, v_outs[:8]), (192, 8, v_outs[8:])):
        at = lax.broadcasted_iota(jnp.int32, (768, 1), 0) - lax.rem(shard * size, 768)
        pick = jnp.where(at == lax.broadcasted_iota(jnp.int32, (1, size), 1), 1.0, 0.0)
        rows = d_vec[0:8] if size == 48 else d_vec[8:16]
        mine = jnp.dot(rows, pick, precision=lax.Precision.HIGHEST, preferred_element_type=jnp.float32)
        if size == 48:
            for i in range(8):
                outs[i][...] = mine[i : i + 1]
        else:
            row = lax.broadcasted_iota(jnp.int32, (8, 1), 0)
            outs[0][...] = jnp.sum(jnp.where(row == shard // 4, mine, 0.0), axis=0, keepdims=True)
    stores = []
    for i, (_, source, wider, out) in enumerate(parts):
        loads[i].wait()
        wider[...] = wide(source[...])
        stores.append(pltpu.make_async_copy(wider, out, osem.at[i]))
        stores[-1].start()
    for copy in stores + copies:
        copy.wait()


def outputs_call(inner, loss, dxq, dxp, d_vec, grads):
    sds, f32, vmem, dma = jax.ShapeDtypeStruct, jnp.float32, pltpu.VMEM, pltpu.SemaphoreType.DMA
    outs = [sds((1, 1), f32), sds(dxq.shape, f32), sds(dxp.shape, f32)] + [sds(g.shape, f32) for g in grads]
    outs += [sds((1, 48), f32)] * 8 + [sds((1, 192), f32)]
    return pl.pallas_call(
        functools.partial(outputs_kernel, inner),
        out_shape=outs,
        in_specs=[VM, ANY, ANY, VM] + [VM] * 6,
        out_specs=[VM] + [ANY] * 8 + [VM] * 9,
        scratch_shapes=[vmem(dxq.shape, dxq.dtype), vmem(dxp.shape, dxp.dtype), vmem(dxq.shape, f32), vmem(dxp.shape, f32), dma((5,)), dma((5,)), dma((6,))],
        compiler_params=pltpu.CompilerParams(vmem_limit_bytes=62 << 20),
        name="write_outputs",
    )(loss, dxq, dxp, d_vec, *grads)


def per_device(
    query_tokens, passage_tokens, lengths, positives,
    query_weight, key_weight, value_weight, output_weight, inner_weight, outer_weight,
    query_bias, value_bias, output_bias, inner_bias, outer_bias,
    first_gain, first_shift, second_gain, second_shift,
):
    inner = lax.axis_size("dp") // 16
    groups = None if inner == 1 else [[h * inner + i for i in range(inner)] for h in range(16)]
    seq = passage_tokens.shape[1]

    def fetch(w):
        if groups is None:
            return w
        return lax.all_gather(w, "dp", axis=0, tiled=True, axis_index_groups=groups)

    weights = [fetch(w) for w in (query_weight, key_weight, value_weight, output_weight, inner_weight, outer_weight)]
    vectors = (query_bias, value_bias, output_bias, outer_bias, first_gain, first_shift, second_gain, second_shift, inner_bias)
    vectors = [fetch(w)[None] for w in vectors[:8]] + [fetch(inner_bias)]
    d_pool, loss, lens, vec, wa, wi, wo, *saved = forward_call(
        inner, float(seq), lengths, positives[None], vectors, weights, query_tokens, passage_tokens)
    wa, wi, wo = wa.reshape(4, 768, 768), wi.reshape(768, 3072), wo.reshape(3072, 768)
    dxq, dxp, d_vec, *grads = backward_call(inner, lens, d_pool, vec, wa, wi, wo, saved)
    loss, dxq, dxp, *grads = outputs_call(inner, loss, dxq, dxp, d_vec, grads)
    grads = [g.reshape(-1) if g.shape[0] == 1 else g for g in grads]

    def finish(x):
        if groups is None:
            return x
        return lax.psum_scatter(x, "dp", scatter_dimension=0, tiled=True, axis_index_groups=groups)

    grads = [finish(g) for g in grads]
    flat = grads[6:]
    return (loss[0, 0], dxq, dxp, *grads[:6], flat[0], flat[1], flat[2], flat[8], *flat[3:8])


def solution(mesh):
    rows3, rows2, rows1 = P("dp", None, None), P("dp", None), P("dp")
    return jax.shard_map(
        per_device,
        mesh=mesh,
        in_specs=(rows3, rows3, P("tower", "dp"), P()) + (rows2,) * 6 + (rows1,) * 9,
        out_specs=(P(), rows3, rows3) + (rows2,) * 6 + (rows1,) * 9,
        check_vma=False,
    )
```

```python
import functools

import jax
import jax.numpy as jnp
from jax import lax
from jax.experimental import pallas as pl
from jax.experimental.pallas import tpu as pltpu
from jax.sharding import PartitionSpec as P

MESH = pl.DeviceIdType.MESH
ANY = pl.BlockSpec(memory_space=pl.ANY)
VM = pl.BlockSpec(memory_space=pltpu.VMEM)


class Place:
    def __init__(self, inner):
        dp = lax.axis_index("dp")
        self.c = lax.axis_index("tower")
        self.inner = inner
        self.low = lax.rem(dp, inner)
        self.me = dp // inner
        self.z = self.me // 4
        self.quad = lax.rem(self.me, 4)
        s1 = 1 + self.c
        s2 = 2 - self.c
        b1 = lax.rem(self.quad // s1, 2)
        b2 = lax.rem(self.quad // s2, 2)
        self.q1 = self.quad + s1 * (1 - 2 * b1)
        self.q2 = self.quad + s2 * (1 - 2 * b2)
        self.q12 = 3 - self.quad
        self.quads = (self.quad, self.q1, self.q2, self.q12)

    def ring(self, k):
        return lax.rem(self.z + k, 4)

    def dev(self, group):
        return {"dp": group * self.inner + self.low, "tower": self.c}

    def n1(self):
        return self.dev(self.z * 4 + self.q1)

    def n2(self):
        return self.dev(self.z * 4 + self.q2)

    def up(self, k):
        return self.dev(self.ring(k) * 4 + self.quad)

    def sib(self):
        return {"dp": self.me * self.inner + self.low, "tower": 1 - self.c}

    def barrier(self):
        sem = pltpu.get_barrier_semaphore()
        for target in (self.up(1), self.up(2), self.up(3), self.n1(), self.n2(), self.sib()):
            pl.semaphore_signal(sem, inc=1, device_id=target, device_id_type=MESH)
        pl.semaphore_wait(sem, 6)


def remote(src, dst, send_sem, recv_sem, target):
    return pltpu.make_async_remote_copy(
        src_ref=src, dst_ref=dst, send_sem=send_sem, recv_sem=recv_sem, device_id=target, device_id_type=MESH
    )


S, Q = 512, 64
T = S + Q


def dot(left, right):
    return jnp.dot(left, right, preferred_element_type=jnp.float32)


def dot_nt(left, right):
    return lax.dot_general(left, right, (((1,), (1,)), ((), ())), preferred_element_type=jnp.float32)


def block(index, size):
    return pl.ds(pl.multiple_of(index * size, size), size)


def low(x):
    return x.astype(jnp.bfloat16)


def wide(x):
    return x.astype(jnp.float32)


def head_mask(h):
    lane = lax.broadcasted_iota(jnp.int32, (1, 128), 1)
    return low(jnp.where(lane // 64 == h, 1.0, 0.0))


SPANS = ((0, S, 256), (S, Q, Q))


class Gather:
    def __init__(self, p, shards, wa, wi, wo, ssem, rsem, lsem):
        self.p, self.shards, self.wa, self.wi, self.wo = p, shards, wa, wi, wo
        self.ssem, self.rsem, self.lsem = ssem, rsem, lsem

    def cols(self, t, which):
        start = which * 384 if t < 4 or t > 7 else (t - 4) * 768 + which * 384
        return pl.ds(pl.multiple_of(start, 128), 384)

    def shard(self, t):
        ref = self.shards[t] if t < 4 else self.shards[4 if t < 8 else 5]
        return ref.at[:, self.cols(t, self.p.c)]

    def one(self, t, z, q):
        cols = self.cols(t, self.p.c)
        if t < 4:
            return self.wa.at[t, z, q, :, cols]
        return (self.wi if t < 8 else self.wo).at[z, q, :, cols]

    def four(self, t, q, which):
        cols = self.cols(t, which)
        if t < 4:
            return self.wa.at[t, :, q, :, cols]
        if t < 8:
            return self.wi.at[:, q, :, cols]
        return self.wo.at[self.p.ring(12 - t), q, :, cols]

    def copy(self, src, dst, t, k, target):
        return remote(src, dst, self.ssem.at[t, k], self.rsem.at[t, k], target)

    def recv(self, t, k, ref):
        self.copy(ref, ref, t, k, self.p.sib()).wait_recv()

    def push(self, t, q, k, target):
        view = self.four(t, q, self.p.c)
        self.copy(view, view, t, k, target).start()

    def steps(self, t):
        return range(1, 4) if t < 8 else range(t - 8, t - 7) if t > 8 else ()

    def local(self, t):
        return pltpu.make_async_copy(self.shard(t), self.one(t, self.p.z, self.p.quad), self.lsem.at[t])

    def push_one(self, t, z, q, k, target):
        view = self.one(t, z, q)
        self.copy(view, view, t, k, target).start()

    def direct(self, t):
        return t not in TURNED

    def stage_own(self, t):
        p = self.p
        if t <= 8:
            self.local(t).start()
        for k in self.steps(t):
            self.copy(self.shard(t), self.one(t, p.z, p.quad), t, k, p.up(k)).start()
        if t <= 8:
            self.copy(self.shard(t), self.one(t, p.z, p.quad), t, 4, p.n1()).start()
            self.copy(self.shard(t), self.one(t, p.z, p.quad), t, 5, p.n2()).start()

    def stage_z(self, t):
        p = self.p
        if not self.direct(t):
            self.recv(t, 4, self.one(t, p.z, p.q1))
            for k in range(1, 4):
                self.push_one(t, p.z, p.q1, 11 + k, p.up(k))
            self.push_one(t, p.z, p.q1, 6, p.n2())
        for k in self.steps(t):
            z = p.ring(4 - k)
            self.recv(t, k, self.one(t, z, p.quad))
            if self.direct(t):
                self.push_one(t, z, p.quad, 4, p.n1())
            self.push_one(t, z, p.quad, 5, p.n2())
        if t <= 8:
            self.local(t).wait()
        self.push(t, p.quad, 8, p.sib())

    def stage_one(self, t):
        p = self.p
        if self.direct(t):
            self.recv(t, 4, self.four(t, p.q1, p.c))
            self.push(t, p.q1, 6, p.n2())
        else:
            for k in range(1, 4):
                z = p.ring(4 - k)
                self.recv(t, 11 + k, self.one(t, z, p.q1))
                self.push_one(t, z, p.q1, 6, p.n2())
        self.push(t, p.q1, 9, p.sib())

    def stage_two(self, t):
        p = self.p
        for k, q in ((5, p.q2), (6, p.q12)):
            self.recv(t, k, self.four(t, q, p.c))
            self.push(t, q, k + 5, p.sib())

    def stage_sib(self, t):
        p = self.p
        for k, q in ((8, p.quad), (9, p.q2), (10, p.q1), (11, p.q12)):
            self.recv(t, k, self.four(t, q, 1 - p.c))

    def tick(self, i):
        for lag, stage in ((0, self.stage_z), (-AHEAD, self.stage_own), (LAGS[0], self.stage_one), (LAGS[1], self.stage_two), (LAGS[2], self.stage_sib)):
            if 0 <= i - lag < 12:
                stage(i - lag)

    def finish(self):
        p = self.p
        for t in range(12):
            single, view = self.one(t, p.z, p.quad), self.four(t, p.quad, p.c)
            for k in self.steps(t):
                self.copy(single, single, t, k, p.sib()).wait_send()
            for k in (4, 5, 6, 8, 9, 10, 11):
                shape = single if k == 4 and not self.direct(t) else view
                self.copy(shape, shape, t, k, p.sib()).wait_send()
            for k in () if self.direct(t) else (12, 13, 14):
                self.copy(single, single, t, k, p.sib()).wait_send()


def expand_vectors(shards, vec):
    at = wide(lax.broadcasted_iota(jnp.int32, (1, 768), 1))
    owner = jnp.floor((at + 0.5) * (1.0 / 48))
    lane = wide(lax.broadcasted_iota(jnp.int32, (128, 1), 0))
    rows = dot(shards.reshape(256, 128), low(jnp.where(lane == at - owner * 48, 1.0, 0.0))).reshape(16, 16, 768)
    shard = wide(lax.broadcasted_iota(jnp.int32, (16, 1, 1), 0))
    vec[:8, :768] = jnp.sum(jnp.where(owner[None] == shard, rows[:, :8], 0.0), axis=0)
    piece = wide(lax.broadcasted_iota(jnp.int32, (4, 4, 1), 0) * 4 + lax.broadcasted_iota(jnp.int32, (4, 4, 1), 1))
    for n in range(4):
        mine = jnp.sum(jnp.where(owner[None] == piece, rows[4 * n : 4 * n + 4, 8:12], 0.0), axis=0)
        vec[8:9, n * 768 : (n + 1) * 768] = jnp.sum(mine, axis=0, keepdims=True)


AHEAD = 2
LAGS = (1, 3, 4)
TURNED = ()


class Scatter:
    def __init__(self, p, refs, result):
        self.p = p
        self.stage, self.r0, self.acc, self.r1, self.r2, self.r3, self.ssem, self.rsem = refs
        self.result = result
        self.own = pl.ds(pl.multiple_of(p.c * 384, 128), 384)
        self.other = pl.ds(pl.multiple_of((1 - p.c) * 384, 128), 384)

    def copy(self, src, dst, e, k, target):
        return remote(src, dst, self.ssem.at[e, k], self.rsem.at[e, k], target)

    def recv(self, e, k, ref):
        self.copy(ref, ref, e, k, self.p.sib()).wait_recv()

    def emit(self, e, left, right, extra=None):
        if e >= 2:
            self.shared(e - 2).wait_send()

        @pl.loop(0, 3)
        def _(n):
            cols = block(n, 256)
            values = right(cols)
            self.stage[e % 2, :, :, :, cols] = low(dot(left(), values)).reshape(4, 4, 48, 256)
            if extra is not None:
                extra(cols, values)
        self.shared(e).start()

    def shared(self, e):
        return self.copy(self.stage.at[e % 2, :, :, :, self.other], self.r0.at[e % 4], e, 0, self.p.sib())

    def stage0(self, e):
        p, acc = self.p, self.acc
        self.recv(e, 0, self.r0.at[e % 4])
        for j, q in enumerate((p.q2, p.q12, p.q1, p.quad)):
            acc[e, :, q] = self.stage[e % 2, :, q, :, self.own] + self.r0[e % 4, :, q]
            if j < 2:
                self.copy(acc.at[e, :, q], self.r1.at[e, j], e, 1 + j, p.n2()).start()

    def stage1(self, e):
        p, acc = self.p, self.acc
        self.recv(e, 2, self.r1.at[e, 1])
        acc[e, :, p.q1] += self.r1[e, 1]
        self.copy(acc.at[e, :, p.q1], self.r2.at[e], e, 3, p.n1()).start()
        self.recv(e, 1, self.r1.at[e, 0])
        acc[e, :, p.quad] += self.r1[e, 0]

    def stage2(self, e):
        p, acc = self.p, self.acc
        self.recv(e, 3, self.r2.at[e])
        acc[e, :, p.quad] += self.r2[e]
        for k in range(1, 4):
            self.copy(acc.at[e, p.ring(k), p.quad], self.r3.at[e, k - 1], e, 3 + k, p.up(k)).start()

    def stage3(self, e):
        p = self.p
        total = wide(self.acc[e, p.z, p.quad])
        for k in range(1, 4):
            self.recv(e, 3 + k, self.r3.at[e, k - 1])
            total = total + wide(self.r3[e, k - 1])
        view = self.result(e, p.c)
        view[...] = total
        self.copy(view, view, e, 7, p.sib()).start()

    def finish(self, count):
        for e in range(count):
            self.recv(e, 7, self.result(e, 1 - self.p.c))
            self.copy(self.result(e, self.p.c), self.result(e, self.p.c), e, 7, self.p.sib()).wait_send()
        for e in range(count - 2, count):
            self.shared(e).wait_send()
        four, one = self.r2.at[0], self.r3.at[0, 0]

        @pl.loop(0, count)
        def _(e):
            for k in range(1, 7):
                view = four if k < 4 else one
                self.copy(view, view, e, k, self.p.sib()).wait_send()


def forward_part(p, seq, lengths, targets, vector_shards, weights, query_tokens, passage_tokens, d_pool, loss, prob_out, vec, prob, prob_q,
                 wa, wi, wo, x, q, k, v, act, act_t, slope, x_t, q_t, ctx_t, norm_t, y1, r1, y2, r2, pooled, rows, packed, vectors, len_buf,
                 ssem, rsem, lsem, vsem, psem, xsem):
    normed = q
    pairs = targets.shape[1]
    me = lax.axis_index("dp") * 2 + p.c

    def device(at):
        return {"dp": at // 2, "tower": lax.rem(at, 2)}

    x_loads = [pltpu.make_async_copy(passage_tokens.at[p.c], x.at[pl.ds(0, S)], xsem.at[0]), pltpu.make_async_copy(query_tokens.at[p.c], x.at[pl.ds(S, Q)], xsem.at[1])]
    for copy in x_loads:
        copy.start()
    barrier = pltpu.get_barrier_semaphore()

    @pl.loop(1, pairs)
    def _(i):
        pl.semaphore_signal(barrier, inc=1, device_id=device(lax.rem(me + i, pairs)), device_id_type=MESH)
    lane = lax.broadcasted_iota(jnp.int32, (8, 128), 1)
    len_buf[p.c] = jnp.where(lane == 0, lengths[0, 0].astype(jnp.float32), lengths[0, 1].astype(jnp.float32))
    packed[...] = jnp.zeros((16, 128), jnp.float32)
    for i, ref in enumerate(vector_shards[:8]):
        packed[i : i + 1, :48] = wide(ref[...])
    last = wide(vector_shards[8][...]).reshape(1, 192)
    for i in range(4):
        packed[8 + i : 9 + i, :48] = last[:, i * 48 : i * 48 + 48]
    vectors[p.z, p.quad] = low(packed[...])
    pl.semaphore_wait(barrier, pairs - 1)

    gather = Gather(p, weights, wa, wi, wo, ssem, rsem, lsem)
    for t in range(AHEAD):
        gather.stage_own(t)
    len_copy = remote(len_buf.at[p.c], len_buf.at[p.c], xsem.at[2], xsem.at[3], p.sib())
    len_copy.start()

    def vector(i, q, target):
        view = vectors.at[p.z, p.quad] if i < 4 else vectors.at[:, q]
        return remote(view, view, vsem.at[0, i], vsem.at[1, i], target)

    for i in range(1, 4):
        vector(i, None, p.up(i)).start()
    gather.tick(0)
    for i in range(1, 4):
        view = vectors.at[p.ring(4 - i), p.quad]
        remote(view, view, vsem.at[0, i], vsem.at[1, i], p.sib()).wait_recv()
    vector(4, p.quad, p.n1()).start()
    vector(5, p.quad, p.n2()).start()
    gather.tick(1)
    vector(4, p.q1, p.sib()).wait_recv()
    vector(6, p.q1, p.n2()).start()
    for copy in x_loads:
        copy.wait()
    x_t[...] = x[...].T
    for i in range(2, LAGS[2]):
        gather.tick(i)
    vector(5, p.q2, p.sib()).wait_recv()
    vector(6, p.q12, p.sib()).wait_recv()
    expand_vectors(vectors[...], vec)
    remote(len_buf.at[1 - p.c], len_buf.at[1 - p.c], xsem.at[2], xsem.at[3], p.sib()).wait_recv()
    len_q, len_p = [jnp.sum(jnp.where(lane[:1] == p.c, len_buf[i, 0:1], 0.0), axis=1, keepdims=True) for i in range(2)]

    def project(m, out, row):
        @pl.loop(0, 3)
        def _(n):
            cols = block(n, 256)
            acc = dot(x[...], wa[m, :, :, :, cols].reshape(768, 256))
            if row is not None:
                acc = acc + vec[row : row + 1, cols]
            out[:, cols] = low(acc)

    def store_prob(j):
        return pltpu.make_async_copy(prob.at[lax.rem(j, 2)], prob_out.at[pl.ds(j * 2, 2)], psem.at[lax.rem(j, 2)])

    def attention(low_j, high_j):
        @pl.loop(low_j, high_j)
        def _(j):
            cols = block(j, 128)
            slot = lax.rem(j, 2)

            @pl.when(j >= 2)
            def _():
                store_prob(j - 2).wait()

            for (start, size, rb), length in zip(SPANS, (len_p, len_q)):
                span = slice(start, start + size)
                kp, vp = k[span, cols], v[span, cols]
                valid = wide(lax.broadcasted_iota(jnp.int32, (1, size), 1)) < length
                for r in range(0, size, rb):
                    qp = q[start + r : start + r + rb, cols]
                    total = None
                    for h in range(2):
                        mask = head_mask(h)
                        scores = dot_nt(qp * (mask * 0.125), kp)
                        scores = jnp.where(valid, scores, -1e9)
                        e = jnp.exp(scores - jnp.max(scores, axis=1, keepdims=True))
                        w = low(e * (1.0 / jnp.sum(e, axis=1, keepdims=True)))
                        if size == S:
                            prob[slot, h, r : r + rb] = w
                        else:
                            prob_q[2 * j + h] = w
                        piece = dot(w, vp * mask)
                        total = piece if total is None else total + piece
                    act[start + r : start + r + rb, cols] = low(total)
            store_prob(j).start()

    gather.tick(LAGS[2] + 0)
    project(0, q, 0)
    gather.tick(LAGS[2] + 1)
    project(1, k, None)
    q_t[...] = q[...].T
    gather.tick(LAGS[2] + 2)
    project(2, v, 1)
    attention(0, 1)

    gather.tick(LAGS[2] + 3)
    attention(1, 3)
    gather.tick(LAGS[2] + 4)
    attention(3, 5)
    gather.tick(LAGS[2] + 5)
    attention(5, 6)
    ctx_t[...] = act[:, :768].T

    def gain(row):
        return vec[row : row + 1, :768]

    @pl.loop(0, 3)
    def _(n):
        span = block(n, 192)
        first = wide(x[span]) + (dot(act[span, :768], wa[3].reshape(768, 768)) + gain(2))
        center = first - jnp.mean(first, axis=1, keepdims=True)
        scale = lax.rsqrt(jnp.mean(center * center, axis=1, keepdims=True) + 1e-12)
        y = center * scale
        y1[span] = y
        r1[span] = scale
        normed[span] = low(y * gain(4) + gain(5))

    def hidden(low_n, high_n):
        @pl.loop(low_n, high_n)
        def _(n):
            cols = block(n, 256)
            u = dot(normed[...], wi[:, :, :, cols].reshape(768, 256)) + vec[8:9, cols]
            cdf = 0.5 * (1.0 + lax.erf(u * 0.7071067811865476))
            act[:, cols] = low(u * cdf)
            slope[:, cols] = low(cdf + u * (0.3989422804014327 * jnp.exp(-0.5 * u * u)))

    gather.tick(LAGS[2] + 6)
    norm_t[...] = normed[...].T
    hidden(0, 6)
    gather.tick(LAGS[2] + 7)
    hidden(6, 12)

    pooled[...] = jnp.zeros_like(pooled)

    def turn_act():
        for b in range(4):
            turned = act[:, b * 768 : (b + 1) * 768].T
            for s in range(4):
                for n in range(4):
                    row = n * 768 + (b * 4 + s) * 48
                    act_t[row : row + 48] = turned[s * 192 + n * 48 : s * 192 + n * 48 + 48]

    def outer(i):
        plane = p.ring(4 - i)

        @pl.loop(0, 3)
        def _(n):
            span = block(n, 192)
            add = dot(act[span, pl.ds(pl.multiple_of(plane * 768, 128), 768)], wo[plane].reshape(768, 768))
            if i == 0:
                add = add + (y1[span] * gain(4) + gain(5) + gain(3))
            else:
                add = add + y2[span]
            if i < 3:
                y2[span] = add
                return
            center = add - jnp.mean(add, axis=1, keepdims=True)
            scale = lax.rsqrt(jnp.mean(center * center, axis=1, keepdims=True) + 1e-12)
            y = center * scale
            y2[span] = y
            r2[span] = scale
            out = y * gain(6) + gain(7)
            at = wide(lax.broadcasted_iota(jnp.int32, (192, 1), 0) + n * 192)
            for row, keep in ((0, (at >= S) & (at - S < len_q)), (1, (at < S) & (at < len_p))):
                pooled[row : row + 1] += jnp.sum(jnp.where(keep, out, 0.0), axis=0, keepdims=True)

    for i in range(4):
        gather.tick(LAGS[2] + 8 + i)
        if i == 0:
            turn_act()
        outer(i)

    mine = jnp.concatenate([pooled[0:1] / len_q, pooled[1:2] / len_p])
    root = jnp.sqrt(jnp.sum(mine * mine, axis=1, keepdims=True) + 1e-6)
    unit = mine / root
    rows[me, :, :768] = unit[0:1]
    rows[me, :, 768:] = unit[1:2]

    @pl.loop(1, pairs)
    def _(i):
        remote(rows.at[me], rows.at[me], xsem.at[4], xsem.at[5], device(lax.rem(me + i, pairs))).start()
    gather.finish()
    len_copy.wait_send()
    for i in range(1, 7):
        vector(i, p.quad, p.sib()).wait_send()
    store_prob(4).wait()
    store_prob(5).wait()
    rest = rows.at[pl.ds(0, pairs - 1)]
    remote(rest, rest, xsem.at[4], xsem.at[5], p.sib()).wait_recv()
    step = 768 if pairs <= 64 else 128
    logits = None
    for at in range(0, 768, step):
        part = lax.dot_general(
            rows[:, 0, 768 + at : 768 + at + step], rows[:, 0, at : at + step], (((1,), (1,)), ((), ())),
            precision=lax.Precision.HIGHEST, preferred_element_type=jnp.float32)
        logits = part if logits is None else logits + part
    logits = logits / 0.01
    hit = targets[...] == lax.broadcasted_iota(jnp.int32, (pairs, pairs), 0)
    top = jnp.max(logits, axis=0, keepdims=True)
    lse = jnp.log(jnp.sum(jnp.exp(logits - top), axis=0, keepdims=True)) + top
    picked = jnp.sum(jnp.where(hit, logits, 0.0), axis=0, keepdims=True)
    loss[...] = jnp.broadcast_to(jnp.sum(lse - picked, axis=1, keepdims=True) / pairs, loss.shape)
    d_logits = seq * (jnp.exp(logits - lse) - jnp.where(hit, 1.0, 0.0))
    across = lax.broadcasted_iota(jnp.int32, (pairs, pairs), 1)
    down = lax.broadcasted_iota(jnp.int32, (pairs, pairs), 0)
    for_q = jnp.sum(jnp.where(across == me, d_logits, 0.0), axis=1, keepdims=True)
    for_p = jnp.sum(jnp.where(down == me, d_logits, 0.0), axis=0, keepdims=True)
    for_p = jnp.sum(jnp.where(across == down, for_p, 0.0), axis=1, keepdims=True)
    for row, weight in enumerate((for_q, for_p)):
        d_unit = jnp.sum(weight * rows[:, 0, (1 - row) * 768 : (2 - row) * 768], axis=0, keepdims=True) / 0.01
        u = unit[row : row + 1]
        d_pool[row : row + 1] = (d_unit - u * jnp.sum(u * d_unit, axis=1, keepdims=True)) / root[row : row + 1]
    remote(rest, rest, xsem.at[4], xsem.at[5], p.sib()).wait_send()
    return len_p, len_q


def backward_part(p, len_p, len_q, d_pool, vec, prob_hbm, prob, prob_q, dxq_out, dxp_out, dvec_out, grads,
                  wa, wi, wo, d_low, k, v, d_inner, act_t, slope, x_t, q_t, ctx_t, norm_t, y1, r1, d_second, r2, ds_buf,
                  d_vec, v_in, v_out, chunks, psem, vsem, xsem):
    g_query, g_key, g_value, g_output, g_inner, g_outer = grads

    def load_prob(j):
        return pltpu.make_async_copy(prob_hbm.at[pl.ds(j * 2, 2)], prob.at[lax.rem(j, 2)], psem.at[lax.rem(j, 2)])

    load_prob(0).start()
    load_prob(1).start()

    def result(e, which):
        cols = pl.ds(pl.multiple_of(which * 384, 128), 384)
        if e < 4:
            return g_outer.at[pl.ds(e * 48, 48), cols]
        if e < 8:
            return g_inner.at[:, pl.ds(pl.multiple_of((e - 4) * 768 + which * 384, 128), 384)]
        return (g_output, g_query, g_key, g_value)[e - 8].at[:, cols]

    sc = Scatter(p, chunks, result)
    d_vec[...] = jnp.zeros_like(d_vec)

    def gain(row):
        return vec[row : row + 1, :768]

    def tally(row, value):
        d_vec[row : row + 1] += jnp.sum(value, axis=0, keepdims=True)

    pool_q = d_pool[0:1] / len_q
    pool_p = d_pool[1:2] / len_p

    def norm_back(d, row, yy, scale, rows):
        tally(row, d * yy)
        tally(row + 1, d)
        g = d * gain(row)
        d = (g - jnp.mean(g, axis=1, keepdims=True) - yy * jnp.mean(g * yy, axis=1, keepdims=True)) * scale
        d_second[rows] = d
        d_low[rows] = low(d)
        return d


    @pl.loop(0, 3)
    def _(n):
        rows = block(n, 192)
        at = wide(lax.broadcasted_iota(jnp.int32, (192, 1), 0) + n * 192)
        d_rows = jnp.where(at < S, jnp.where(at < len_p, pool_p, 0.0), jnp.where(at - S < len_q, pool_q, 0.0))
        d = norm_back(d_rows, 6, d_second[rows], r2[rows], rows)
        tally(3, wide(low(d)))


    def emit_outer(n):
        sc.emit(n, lambda: act_t[n * 768 : (n + 1) * 768], lambda cols: d_low[:, cols])

    def emit_inner(n):
        def bias(cols, values):
            d_vec[8 + n : 9 + n, cols] = jnp.sum(wide(values), axis=0, keepdims=True)
        sc.emit(4 + n, lambda: norm_t[...], lambda cols: d_inner[:, pl.ds(pl.multiple_of(n * 768 + cols.start, 256), 256)], bias)

    emit_outer(0)
    emit_outer(1)
    sc.stage0(0)
    emit_outer(2)
    sc.stage0(1)
    emit_outer(3)
    sc.stage0(2)

    def inner_back(low_n, high_n):
        @pl.loop(low_n, high_n)
        def _(n):
            cols = block(n, 768)
            d_inner[:, cols] = low(dot_nt(d_low[...], wo[n].reshape(768, 768)) * wide(slope[:, cols]))

    inner_back(0, 2)
    sc.stage0(3)
    sc.stage1(0)
    inner_back(2, 4)
    emit_inner(0)
    sc.stage1(1)
    emit_inner(1)
    sc.stage0(4)
    sc.stage2(0)
    emit_inner(2)
    sc.stage0(5)
    emit_inner(3)
    sc.stage0(6)
    sc.stage1(2)
    sc.stage2(1)

    def first_back(low_n, high_n):
        @pl.loop(low_n, high_n)
        def _(n):
            rows = block(n, 192)
            d = norm_back(d_second[rows] + dot_nt(d_inner[rows], wi[...].reshape(768, 3072)), 4, y1[rows], r1[rows], rows)
            tally(2, wide(low(d)))

    first_back(0, 1)
    sc.stage0(7)
    first_back(1, 3)
    sc.stage1(3)
    sc.stage2(2)
    sc.stage3(0)
    sc.emit(8, lambda: ctx_t[...], lambda cols: d_low[:, cols])

    def part(i):
        return pl.ds(i * 768, 768)

    def pair_cols(i, j):
        return pl.ds(pl.multiple_of(i * 768 + j * 128, 128), 128)

    def head_rows(i, head):
        return pl.ds(pl.multiple_of(i * 768 + head * 64, 64), 64)

    @pl.loop(0, 3)
    def _(n):
        rows = block(n, 192)
        d_inner[rows, part(3)] = low(dot_nt(d_low[rows], wa[3].reshape(768, 768)))
    act_t[part(2)] = d_inner[:, part(3)].T
    sc.stage0(8)

    def attention(low_j, high_j):
        @pl.loop(low_j, high_j)
        def _(j):
            load_prob(j).wait()
            slot = lax.rem(j, 2)
            cols = block(j, 128)
            for start, size, rb in SPANS:
                rows = slice(start, start + size)
                kp, vp = k[rows, cols], v[rows, cols]
                dq_parts = [None] * (size // rb)
                for h in range(2):
                    probs = (lambda sl: prob[slot, h, sl]) if size == S else (lambda sl: prob_q[2 * j + h, sl])
                    mask = head_mask(h)
                    for r in range(0, size, rb):
                        d_p = dot_nt(d_inner[start + r : start + r + rb, pair_cols(3, j)] * mask, vp)
                        w = wide(probs(slice(r, r + rb)))
                        ds = low(w * (d_p - jnp.sum(w * d_p, axis=1, keepdims=True)))
                        ds_buf[h, r : r + rb, :size] = ds
                        piece = dot(ds, kp * mask)
                        i = r // rb
                        dq_parts[i] = piece if dq_parts[i] is None else dq_parts[i] + piece
                    head = 2 * j + h
                    act_t[head_rows(1, head), rows] = low(dot(act_t[head_rows(2, head), rows], probs(slice(0, size))))
                    act_t[head_rows(0, head), rows] = low(dot(q_t[head_rows(0, head), rows], ds_buf[h, :size, :size]) * 0.125)
                for i, piece in enumerate(dq_parts):
                    d_inner[start + i * rb : start + (i + 1) * rb, pair_cols(0, j)] = low(piece * 0.125)

            @pl.when(j < 4)
            def _():
                load_prob(j + 2).start()

    attention(0, 2)
    sc.stage1(4)
    sc.stage2(3)
    sc.stage3(1)
    attention(2, 6)
    sc.stage1(5)
    sc.stage2(4)
    sc.stage3(2)
    d_inner[:, part(1)] = act_t[part(0)].T
    d_inner[:, part(2)] = act_t[part(1)].T

    def emit_first(n):
        row = (0, None, 1)[n]

        def bias(cols, values):
            d_vec[row : row + 1, cols] = jnp.sum(wide(values), axis=0, keepdims=True)
        sc.emit(9 + n, lambda: x_t[...], lambda cols: d_inner[:, pl.ds(pl.multiple_of(n * 768 + cols.start, 256), 256)], None if row is None else bias)

    emit_first(0)
    emit_first(1)
    sc.stage0(9)
    emit_first(2)
    sc.stage0(10)

    def vector(i, src, target):
        return remote(src, v_in.at[i], vsem.at[0, i], vsem.at[1, i], target)

    def vector_recv(i):
        vector(i, v_in.at[i], p.sib()).wait_recv()
        return v_in[i]

    vector(0, d_vec.at[:, sc.other], p.sib()).start()
    sc.stage1(6)
    sc.stage2(5)
    sc.stage3(3)
    sc.stage0(11)

    @pl.loop(0, 3)
    def _(n):
        rows = block(n, 192)
        d = d_second[rows]
        for i in range(3):
            d = d + dot_nt(d_inner[rows, part(i)], wa[i].reshape(768, 768))
        d_low[rows] = low(d)
    tokens = [(d_low.at[pl.ds(0, S)], dxp_out), (d_low.at[pl.ds(S, Q)], dxq_out)]
    mine = [pltpu.make_async_copy(src, out.at[p.c], xsem.at[i]) for i, (src, out) in enumerate(tokens)]
    theirs = [remote(src, out.at[p.c], xsem.at[2 + i], xsem.at[4 + i], p.sib()) for i, (src, out) in enumerate(tokens)]
    for copy in mine + theirs:
        copy.start()
    v_out[0] = d_vec[:, sc.own] + vector_recv(0)
    vector(1, v_out.at[0], p.n2()).start()
    sc.stage1(7)
    sc.stage2(6)
    sc.stage3(4)
    sc.stage1(8)
    sc.stage2(7)
    sc.stage3(5)
    sc.stage1(9)
    sc.stage2(8)
    sc.stage3(6)
    v_out[1] = v_out[0] + vector_recv(1)
    vector(2, v_out.at[1], p.n1()).start()
    sc.stage1(10)
    sc.stage2(9)
    sc.stage3(7)
    sc.stage1(11)
    v_out[2] = v_out[1] + vector_recv(2)
    for i in range(1, 4):
        vector(2 + i, v_out.at[2], p.up(i)).start()
    sc.stage2(10)
    sc.stage3(8)
    sc.stage2(11)
    dvec_out[:, sc.own] = v_out[2] + vector_recv(3) + vector_recv(4) + vector_recv(5)
    last = remote(dvec_out.at[:, sc.own], dvec_out.at[:, sc.own], vsem.at[0, 6], vsem.at[1, 6], p.sib())
    last.start()
    for e in range(9, 12):
        sc.stage3(e)
    for i, (src, out) in enumerate(tokens):
        mine[i].wait()
        theirs[i].wait_send()
        remote(out.at[1 - p.c], out.at[1 - p.c], xsem.at[2 + i], xsem.at[4 + i], p.sib()).wait_recv()
    remote(dvec_out.at[:, sc.other], dvec_out.at[:, sc.other], vsem.at[0, 6], vsem.at[1, 6], p.sib()).wait_recv()
    last.wait_send()
    for i in range(6):
        vector(i, v_in.at[i], p.sib()).wait_send()
    sc.finish(12)


def layer_kernel(inner, seq, lengths, targets, *refs):
    vector_shards, weights, (query_tokens, passage_tokens) = refs[:9], refs[9:15], refs[15:17]
    loss, dxq_out, dxp_out, dvec_out = refs[17:21]
    grads, prob_hbm = refs[21:27], refs[27]
    (wa, wi, wo, x, q, k, v, act, act_t, slope, x_t, q_t, ctx_t, norm_t, y1, r1, y2, r2, prob, prob_q, ds_buf, vec, d_pool, pooled,
     rows, packed, vectors, len_buf, d_vec, v_in, v_out) = refs[28:59]
    chunks, (g_ssem, g_rsem, g_lsem, g_vsem, psem, g_xsem, vsem, xsem) = refs[59:67], refs[67:75]
    p = Place(inner)
    len_p, len_q = forward_part(
        p, seq, lengths, targets, vector_shards, weights, query_tokens, passage_tokens, d_pool, loss, prob_hbm, vec, prob, prob_q,
        wa, wi, wo, x, q, k, v, act, act_t, slope, x_t, q_t, ctx_t, norm_t, y1, r1, y2, r2, pooled, rows, packed, vectors, len_buf,
        g_ssem, g_rsem, g_lsem, g_vsem, psem, g_xsem)
    backward_part(
        p, len_p, len_q, d_pool, vec, prob_hbm, prob, prob_q, dxq_out, dxp_out, dvec_out, grads,
        wa, wi, wo, x, k, v, act, act_t, slope, x_t, q_t, ctx_t, norm_t, y1, r1, y2, r2, ds_buf,
        d_vec, v_in, v_out, chunks, psem, vsem, xsem)


def layer_call(inner, seq, lengths, targets, vectors, weights, query_tokens, passage_tokens, cid=0):
    bf, f32 = jnp.bfloat16, jnp.float32
    sds, vmem, dma = jax.ShapeDtypeStruct, pltpu.VMEM, pltpu.SemaphoreType.DMA
    pairs = targets.shape[1]
    outs = [sds((8, 128), f32), sds((2, Q, 768), bf), sds((2, S, 768), bf), sds((16, 768), f32)]
    outs += [sds((48, 768), f32)] * 4 + [sds((48, 3072), f32), sds((192, 768), f32), sds((12, S, S), bf)]
    wide_rows, rows, turned, column = vmem((T, 768), f32), vmem((T, 768), bf), vmem((768, T), bf), vmem((T, 1), f32)
    scratch = [vmem((4, 4, 4, 48, 768), bf), vmem((4, 4, 48, 3072), bf), vmem((4, 4, 192, 768), bf)] + [rows] * 4
    scratch += [vmem((T, 3072), bf), vmem((3072, T), bf), vmem((T, 3072), bf)] + [turned] * 4 + [wide_rows, column] * 2
    scratch += [vmem((2, 2, S, S), bf), vmem((12, Q, Q), bf), vmem((2, S, S), bf), vmem((16, 3072), f32), vmem((2, 768), f32), vmem((2, 768), f32)]
    scratch += [vmem((pairs, 1, 1536), f32), vmem((16, 128), f32), vmem((4, 4, 16, 128), bf), vmem((2, 8, 128), f32)]
    scratch += [vmem((16, 768), f32), vmem((6, 16, 384), f32), vmem((3, 16, 384), f32)]
    scratch += [vmem((2, 4, 4, 48, 768), bf), vmem((4, 4, 4, 48, 384), bf), vmem((12, 4, 4, 48, 384), bf), vmem((12, 2, 4, 48, 384), bf)]
    scratch += [vmem((12, 4, 48, 384), bf), vmem((12, 3, 48, 384), bf), dma((12, 8)), dma((12, 8))]
    scratch += [dma((12, 16)), dma((12, 16)), dma((9,)), dma((2, 7)), dma((2,)), dma((6,)), dma((2, 7)), dma((6,))]
    return pl.pallas_call(
        functools.partial(layer_kernel, inner, seq),
        out_shape=outs,
        in_specs=[pl.BlockSpec(memory_space=pltpu.SMEM)] + [VM] * 10 + [ANY] * 8,
        out_specs=[VM, ANY, ANY] + [VM] * 7 + [ANY],
        scratch_shapes=scratch,
        compiler_params=pltpu.CompilerParams(collective_id=cid, has_side_effects=True, vmem_limit_bytes=63 << 20),
        name="layer",
    )(lengths, targets, *vectors, *weights, query_tokens, passage_tokens)


def outputs_kernel(inner, loss_in, dxq, dxp, d_vec, *refs):
    grads, (loss, q_out, p_out), g_outs, v_outs = refs[:6], refs[6:9], refs[9:15], refs[15:24]
    q_low, p_low, q_wide, p_wide, isem, osem, gsem = refs[24:]
    copies = [pltpu.make_async_copy(src, dst, gsem.at[i]) for i, (src, dst) in enumerate(zip(grads, g_outs))]
    parts = [(dxp.at[i, pl.ds(r, 256)], p_low.at[i, pl.ds(r, 256)], p_wide.at[i, pl.ds(r, 256)], p_out.at[i, pl.ds(r, 256)]) for i in range(2) for r in (0, 256)]
    parts.append((dxq, q_low, q_wide, q_out))
    loads = [pltpu.make_async_copy(part[0], part[1], isem.at[i]) for i, part in enumerate(parts)]
    for copy in loads + copies:
        copy.start()
    loss[...] = loss_in[0:1, 0:1]
    shard = lax.axis_index("dp") // inner
    for size, first, outs in ((48, 0, v_outs[:8]), (192, 8, v_outs[8:])):
        at = lax.broadcasted_iota(jnp.int32, (768, 1), 0) - lax.rem(shard * size, 768)
        pick = jnp.where(at == lax.broadcasted_iota(jnp.int32, (1, size), 1), 1.0, 0.0)
        rows = d_vec[0:8] if size == 48 else d_vec[8:16]
        mine = jnp.dot(rows, pick, precision=lax.Precision.HIGHEST, preferred_element_type=jnp.float32)
        if size == 48:
            for i in range(8):
                outs[i][...] = mine[i : i + 1]
        else:
            row = lax.broadcasted_iota(jnp.int32, (8, 1), 0)
            outs[0][...] = jnp.sum(jnp.where(row == shard // 4, mine, 0.0), axis=0, keepdims=True)
    stores = []
    for i, (_, source, wider, out) in enumerate(parts):
        loads[i].wait()
        wider[...] = wide(source[...])
        stores.append(pltpu.make_async_copy(wider, out, osem.at[i]))
        stores[-1].start()
    for copy in stores + copies:
        copy.wait()


def outputs_call(inner, loss, dxq, dxp, d_vec, grads):
    sds, f32, vmem, dma = jax.ShapeDtypeStruct, jnp.float32, pltpu.VMEM, pltpu.SemaphoreType.DMA
    outs = [sds((1, 1), f32), sds(dxq.shape, f32), sds(dxp.shape, f32)] + [sds(g.shape, f32) for g in grads]
    outs += [sds((1, 48), f32)] * 8 + [sds((1, 192), f32)]
    return pl.pallas_call(
        functools.partial(outputs_kernel, inner),
        out_shape=outs,
        in_specs=[VM, ANY, ANY, VM] + [VM] * 6,
        out_specs=[VM] + [ANY] * 8 + [VM] * 9,
        scratch_shapes=[vmem(dxq.shape, dxq.dtype), vmem(dxp.shape, dxp.dtype), vmem(dxq.shape, f32), vmem(dxp.shape, f32), dma((5,)), dma((5,)), dma((6,))],
        compiler_params=pltpu.CompilerParams(vmem_limit_bytes=62 << 20),
        name="write_outputs",
    )(loss, dxq, dxp, d_vec, *grads)


def per_device(
    query_tokens, passage_tokens, lengths, positives,
    query_weight, key_weight, value_weight, output_weight, inner_weight, outer_weight,
    query_bias, value_bias, output_bias, inner_bias, outer_bias,
    first_gain, first_shift, second_gain, second_shift,
):
    inner = lax.axis_size("dp") // 16
    groups = None if inner == 1 else [[h * inner + i for i in range(inner)] for h in range(16)]
    seq = passage_tokens.shape[1]

    def fetch(w):
        if groups is None:
            return w
        return lax.all_gather(w, "dp", axis=0, tiled=True, axis_index_groups=groups)

    weights = [fetch(w) for w in (query_weight, key_weight, value_weight, output_weight, inner_weight, outer_weight)]
    vectors = (query_bias, value_bias, output_bias, outer_bias, first_gain, first_shift, second_gain, second_shift, inner_bias)
    vectors = [fetch(w)[None] for w in vectors[:8]] + [fetch(inner_bias)]
    loss, dxq, dxp, d_vec, *grads, _ = layer_call(
        inner, float(seq), lengths, positives[None], vectors, weights, query_tokens, passage_tokens)
    loss, dxq, dxp, *grads = outputs_call(inner, loss, dxq, dxp, d_vec, grads)
    grads = [g.reshape(-1) if g.shape[0] == 1 else g for g in grads]

    def finish(x):
        if groups is None:
            return x
        return lax.psum_scatter(x, "dp", scatter_dimension=0, tiled=True, axis_index_groups=groups)

    grads = [finish(g) for g in grads]
    flat = grads[6:]
    return (loss[0, 0], dxq, dxp, *grads[:6], flat[0], flat[1], flat[2], flat[8], *flat[3:8])


def solution(mesh):
    rows3, rows2, rows1 = P("dp", None, None), P("dp", None), P("dp")
    return jax.shard_map(
        per_device,
        mesh=mesh,
        in_specs=(rows3, rows3, P("tower", "dp"), P()) + (rows2,) * 6 + (rows1,) * 9,
        out_specs=(P(), rows3, rows3) + (rows2,) * 6 + (rows1,) * 9,
        check_vma=False,
    )
```

```python
import functools

import jax
import jax.numpy as jnp
from jax import lax
from jax.experimental import pallas as pl
from jax.experimental.pallas import tpu as pltpu
from jax.sharding import PartitionSpec as P

MESH = pl.DeviceIdType.MESH
ANY = pl.BlockSpec(memory_space=pl.ANY)
VM = pl.BlockSpec(memory_space=pltpu.VMEM)


class Place:
    def __init__(self, inner):
        dp = lax.axis_index("dp")
        self.c = lax.axis_index("tower")
        self.inner = inner
        self.low = lax.rem(dp, inner)
        self.me = dp // inner
        self.z = self.me // 4
        self.quad = lax.rem(self.me, 4)
        s1 = 1 + self.c
        s2 = 2 - self.c
        b1 = lax.rem(self.quad // s1, 2)
        b2 = lax.rem(self.quad // s2, 2)
        self.q1 = self.quad + s1 * (1 - 2 * b1)
        self.q2 = self.quad + s2 * (1 - 2 * b2)
        self.q12 = 3 - self.quad
        self.quads = (self.quad, self.q1, self.q2, self.q12)

    def ring(self, k):
        return lax.rem(self.z + k, 4)

    def dev(self, group):
        return {"dp": group * self.inner + self.low, "tower": self.c}

    def n1(self):
        return self.dev(self.z * 4 + self.q1)

    def n2(self):
        return self.dev(self.z * 4 + self.q2)

    def up(self, k):
        return self.dev(self.ring(k) * 4 + self.quad)

    def sib(self):
        return {"dp": self.me * self.inner + self.low, "tower": 1 - self.c}

    def across(self, k):
        return {"dp": (self.ring(k) * 4 + self.quad) * self.inner + self.low, "tower": 1 - self.c}

    def greet(self):
        for target in (self.up(1), self.up(2), self.up(3), self.n1(), self.n2(), self.sib()):
            pl.semaphore_signal(pltpu.get_barrier_semaphore(), inc=1, device_id=target, device_id_type=MESH)

    def met(self):
        pl.semaphore_wait(pltpu.get_barrier_semaphore(), 6)


def remote(src, dst, send_sem, recv_sem, target):
    return pltpu.make_async_remote_copy(
        src_ref=src, dst_ref=dst, send_sem=send_sem, recv_sem=recv_sem, device_id=target, device_id_type=MESH
    )


S, Q = 512, 64
T = S + Q


def dot(left, right):
    return jnp.dot(left, right, preferred_element_type=jnp.float32)


def dot_nt(left, right):
    return lax.dot_general(left, right, (((1,), (1,)), ((), ())), preferred_element_type=jnp.float32)


def block(index, size):
    return pl.ds(pl.multiple_of(index * size, size), size)


def low(x):
    return x.astype(jnp.bfloat16)


def wide(x):
    return x.astype(jnp.float32)


def head_mask(h):
    lane = lax.broadcasted_iota(jnp.int32, (1, 128), 1)
    return low(jnp.where(lane // 64 == h, 1.0, 0.0))


SPANS = ((0, S, 256), (S, Q, Q))


class Gather:
    last = 10

    def __init__(self, p, shards, wa, wi, wo, ssem, rsem, lsem):
        self.p, self.shards, self.wa, self.wi, self.wo = p, shards, wa, wi, wo
        self.ssem, self.rsem, self.lsem = ssem, rsem, lsem

    def cols(self, t, which):
        if t < 8:
            return pl.ds(pl.multiple_of(which * 384 if t < 4 else (t - 4) * 768 + which * 384, 128), 384)
        return pl.ds(pl.multiple_of(which * 384 + (t - 8) * 128, 128), 128)

    def shard(self, t):
        ref = self.shards[(1, 0, 2, 3)[t]] if t < 4 else self.shards[4 if t < 8 else 5]
        return ref.at[:, self.cols(t, self.p.c)]

    def whole(self, t):
        return self.wa.at[(1, 0, 2, 3)[t]] if t < 4 else self.wi if t < 8 else self.wo

    def one(self, t, z, q):
        return self.whole(t).at[z, q, :, self.cols(t, self.p.c)]

    def four(self, t, q, which):
        return self.whole(t).at[:, q, :, self.cols(t, which)]

    def plane(self, t, z, which):
        return self.whole(t).at[z, :, :, self.cols(t, which)]

    def copy(self, src, dst, t, k, target):
        return remote(src, dst, self.ssem.at[t, k], self.rsem.at[t, k], target)

    def recv(self, t, k, ref):
        self.copy(ref, ref, t, k, self.p.sib()).wait_recv()

    def push(self, view, t, k, target):
        self.copy(view, view, t, k, target).start()

    def local(self, t):
        return pltpu.make_async_copy(self.shard(t), self.one(t, self.p.z, self.p.quad), self.lsem.at[t])

    def stage_own(self, t):
        p = self.p
        self.local(t).start()
        mine = self.one(t, p.z, p.quad)
        for k in range(1, 4) if t < self.last else ():
            self.copy(self.shard(t), mine, t, k, p.up(k)).start()
        self.copy(self.shard(t), mine, t, 4, p.n1()).start()
        self.copy(self.shard(t), mine, t, 5, p.n2()).start()

    def stage_z(self, t):
        p = self.p
        for k in range(1, 4):
            view = self.one(t, p.ring(4 - k), p.quad)
            self.recv(t, k, view)
            self.push(view, t, 4, p.n1())
            self.push(view, t, 5, p.n2())
        self.local(t).wait()
        self.push(self.four(t, p.quad, p.c), t, 8, p.sib())

    def stage_one(self, t):
        p = self.p
        view = self.four(t, p.q1, p.c)
        self.recv(t, 4, view)
        self.push(view, t, 6, p.n2())
        self.push(view, t, 9, p.sib())

    def stage_two(self, t):
        p = self.p
        for k, q in ((5, p.q2), (6, p.q12)):
            view = self.four(t, q, p.c)
            self.recv(t, k, view)
            self.push(view, t, k + 5, p.sib())

    def stage_sib(self, t):
        p = self.p
        for k, q in ((8, p.quad), (9, p.q2), (10, p.q1), (11, p.q12)):
            self.recv(t, k, self.four(t, q, 1 - p.c))

    def last_one(self):
        p, t = self.p, self.last
        view = self.one(t, p.z, p.q1)
        self.recv(t, 4, view)
        self.push(view, t, 6, p.n2())

    def last_two(self):
        p, t = self.p, self.last
        self.recv(t, 5, self.one(t, p.z, p.q2))
        self.recv(t, 6, self.one(t, p.z, p.q12))
        self.local(t).wait()
        view = self.plane(t, p.z, p.c)
        for k in range(1, 4):
            self.push(view, t, k, p.up(k))
        self.push(view, t, 8, p.sib())

    def last_z(self):
        p, t = self.p, self.last
        for k in range(1, 4):
            view = self.plane(t, p.ring(4 - k), p.c)
            self.recv(t, k, view)
            self.push(view, t, 8 + k, p.sib())

    def last_sib(self):
        p, t = self.p, self.last
        for k in range(4):
            self.recv(t, 8 + k, self.plane(t, p.ring(4 - k), 1 - p.c))

    def tick(self, i):
        for lag, stage in ((0, self.stage_z), (-AHEAD, self.stage_own), (LAGS[0], self.stage_one), (LAGS[1], self.stage_two), (LAGS[2], self.stage_sib)):
            if 0 <= i - lag < self.last:
                stage(i - lag)
        for at, stage in zip(LATE, (lambda: self.stage_own(self.last), self.last_one, self.last_two, self.last_z, self.last_sib)):
            if i == at:
                stage()

    def finish(self):
        p = self.p
        for t in range(self.last + 1):
            single, four, plane = self.one(t, p.z, p.quad), self.four(t, p.quad, p.c), self.plane(t, p.z, p.c)
            for k in (1, 2, 3, 4, 5, 6, 8, 9, 10, 11):
                view = (single if k < 4 else four) if t < self.last else (single if 4 <= k < 8 else plane)
                self.copy(view, view, t, k, p.sib()).wait_send()


def expand_vectors(shards, vec):
    at = wide(lax.broadcasted_iota(jnp.int32, (1, 768), 1))
    owner = jnp.floor((at + 0.5) * (1.0 / 48))
    lane = wide(lax.broadcasted_iota(jnp.int32, (128, 1), 0))
    rows = dot(shards.reshape(256, 128), low(jnp.where(lane == at - owner * 48, 1.0, 0.0))).reshape(16, 16, 768)
    shard = wide(lax.broadcasted_iota(jnp.int32, (16, 1, 1), 0))
    vec[:8, :768] = jnp.sum(jnp.where(owner[None] == shard, rows[:, :8], 0.0), axis=0)
    piece = wide(lax.broadcasted_iota(jnp.int32, (4, 4, 1), 0) * 4 + lax.broadcasted_iota(jnp.int32, (4, 4, 1), 1))
    for n in range(4):
        mine = jnp.sum(jnp.where(owner[None] == piece, rows[4 * n : 4 * n + 4, 8:12], 0.0), axis=0)
        vec[8:9, n * 768 : (n + 1) * 768] = jnp.sum(mine, axis=0, keepdims=True)


AHEAD = 4
LAGS = (1, 3, 4)
LATE = (0, 1, 5, 9, 13)


ALONG_Z = (0,)


class Scatter:
    def __init__(self, p, refs, result):
        self.p = p
        self.stage, self.r0, self.acc, self.r1, self.r2, self.r3, self.ssem, self.rsem = refs
        self.result = result
        self.own = pl.ds(pl.multiple_of(p.c * 384, 128), 384)
        self.other = pl.ds(pl.multiple_of((1 - p.c) * 384, 128), 384)

    def copy(self, src, dst, e, k, target):
        return remote(src, dst, self.ssem.at[e, k], self.rsem.at[e, k], target)

    def recv(self, e, k, ref):
        self.copy(ref, ref, e, k, self.p.sib()).wait_recv()

    def emit(self, e, left, right, extra=None):
        if e >= 2:
            self.shared(e - 2).wait_send()

        @pl.loop(0, 3)
        def _(n):
            cols = block(n, 256)
            values = right(cols)
            self.stage[e % 2, :, :, :, cols] = low(dot(left(), values)).reshape(4, 4, 48, 256)
            if extra is not None:
                extra(cols, values)
        self.shared(e).start()

    def shared(self, e):
        return self.copy(self.stage.at[e % 2, :, :, :, self.other], self.r0.at[e % 4], e, 0, self.p.sib())

    def stage0(self, e):
        p, acc = self.p, self.acc
        self.recv(e, 0, self.r0.at[e % 4])
        if e in ALONG_Z:
            for k in (1, 2, 3, 0):
                z = p.ring(k)
                acc[e, z] = self.stage[e % 2, z, :, :, self.own] + self.r0[e % 4, z]
                if k:
                    self.copy(acc.at[e, z], self.plane(e, k), e, k, p.up(k)).start()
            return
        for j, q in enumerate((p.q2, p.q12, p.q1, p.quad)):
            acc[e, :, q] = self.stage[e % 2, :, q, :, self.own] + self.r0[e % 4, :, q]
            if j < 2:
                self.copy(acc.at[e, :, q], self.r1.at[e, j], e, 1 + j, p.n2()).start()

    def plane(self, e, k):
        return self.r2.at[e] if k == 3 else self.r1.at[e, k - 1]

    def stage1(self, e):
        p, acc = self.p, self.acc
        if e in ALONG_Z:
            total = wide(acc[e, p.z])
            for k in range(1, 4):
                self.recv(e, k, self.plane(e, k))
                total = total + wide(self.plane(e, k)[...])
            acc[e, p.z] = low(total)
            for j, q in enumerate((p.q2, p.q12)):
                self.copy(acc.at[e, p.z, q], self.r3.at[e, j], e, 4 + j, p.n2()).start()
            return
        self.recv(e, 2, self.r1.at[e, 1])
        acc[e, :, p.q1] += self.r1[e, 1]
        self.copy(acc.at[e, :, p.q1], self.r2.at[e], e, 3, p.n1()).start()
        self.recv(e, 1, self.r1.at[e, 0])
        acc[e, :, p.quad] += self.r1[e, 0]

    def stage2(self, e):
        p, acc = self.p, self.acc
        if e in ALONG_Z:
            self.recv(e, 5, self.r3.at[e, 1])
            acc[e, p.z, p.q1] += self.r3[e, 1]
            self.copy(acc.at[e, p.z, p.q1], self.r3.at[e, 2], e, 6, p.n1()).start()
            self.recv(e, 4, self.r3.at[e, 0])
            return
        self.recv(e, 3, self.r2.at[e])
        acc[e, :, p.quad] += self.r2[e]
        for k in range(1, 4):
            self.copy(acc.at[e, p.ring(k), p.quad], self.r3.at[e, k - 1], e, 3 + k, p.up(k)).start()

    def stage3(self, e):
        p = self.p
        if e in ALONG_Z:
            self.recv(e, 6, self.r3.at[e, 2])
            total = wide(self.acc[e, p.z, p.quad]) + wide(self.r3[e, 0]) + wide(self.r3[e, 2])
        else:
            total = wide(self.acc[e, p.z, p.quad])
            for k in range(1, 4):
                self.recv(e, 3 + k, self.r3.at[e, k - 1])
                total = total + wide(self.r3[e, k - 1])
        view = self.result(e, p.c)
        view[...] = total
        self.copy(view, view, e, 7, p.sib()).start()

    def finish(self, count):
        for e in range(count):
            self.recv(e, 7, self.result(e, 1 - self.p.c))
            self.copy(self.result(e, self.p.c), self.result(e, self.p.c), e, 7, self.p.sib()).wait_send()
        for e in range(count - 2, count):
            self.shared(e).wait_send()
        four, one = self.r2.at[0], self.r3.at[0, 0]

        @pl.loop(0, count)
        def _(e):
            for k in range(1, 7):
                view = four if k < 4 else one
                self.copy(view, view, e, k, self.p.sib()).wait_send()


def forward_part(p, seq, lengths, targets, vector_shards, weights, query_tokens, passage_tokens, d_pool, loss, prob_out, vec, prob, prob_q,
                 wa, wi, wo, x, q, k, v, act, act_t, slope, x_t, q_t, ctx_t, norm_t, y1, r1, y2, r2, y_sum, rows, packed, vectors, len_buf,
                 ssem, rsem, lsem, vsem, psem, xsem):
    normed = q
    pairs = targets.shape[1]
    me = lax.axis_index("dp") * 2 + p.c

    def device(at):
        return {"dp": at // 2, "tower": lax.rem(at, 2)}

    x_loads = [pltpu.make_async_copy(passage_tokens.at[p.c], x.at[pl.ds(0, S)], xsem.at[0]), pltpu.make_async_copy(query_tokens.at[p.c], x.at[pl.ds(S, Q)], xsem.at[1])]
    for copy in x_loads:
        copy.start()
    barrier = pltpu.get_barrier_semaphore()

    @pl.loop(1, pairs)
    def _(i):
        pl.semaphore_signal(barrier, inc=1, device_id=device(lax.rem(me + i, pairs)), device_id_type=MESH)
    lane = lax.broadcasted_iota(jnp.int32, (8, 128), 1)
    len_buf[p.c] = jnp.where(lane == 0, lengths[0, 0].astype(jnp.float32), lengths[0, 1].astype(jnp.float32))
    packed[...] = jnp.zeros((16, 128), jnp.float32)
    for i, ref in enumerate(vector_shards[:8]):
        packed[i : i + 1, :48] = wide(ref[...])
    last = wide(vector_shards[8][...]).reshape(1, 192)
    for i in range(4):
        packed[8 + i : 9 + i, :48] = last[:, i * 48 : i * 48 + 48]
    vectors[p.z, p.quad] = low(packed[...])
    pl.semaphore_wait(barrier, pairs - 1)

    gather = Gather(p, weights, wa, wi, wo, ssem, rsem, lsem)
    len_copy = remote(len_buf.at[p.c], len_buf.at[p.c], xsem.at[2], xsem.at[3], p.sib())
    len_copy.start()

    def vector(i, q, target):
        view = vectors.at[p.z, p.quad] if i < 4 else vectors.at[:, q]
        return remote(view, view, vsem.at[0, i], vsem.at[1, i], target)

    for i in range(1, 4):
        vector(i, None, p.up(i)).start()
    for t in range(AHEAD):
        gather.stage_own(t)
    gather.tick(0)
    for i in range(1, 4):
        view = vectors.at[p.ring(4 - i), p.quad]
        remote(view, view, vsem.at[0, i], vsem.at[1, i], p.sib()).wait_recv()
    vector(4, p.quad, p.n1()).start()
    vector(5, p.quad, p.n2()).start()
    gather.tick(1)
    for copy in x_loads:
        copy.wait()
    x_t[...] = x[...].T
    gather.tick(2)
    vector(4, p.q1, p.sib()).wait_recv()
    vector(6, p.q1, p.n2()).start()
    for i in range(3, LAGS[2] + 1):
        gather.tick(i)
    remote(len_buf.at[1 - p.c], len_buf.at[1 - p.c], xsem.at[2], xsem.at[3], p.sib()).wait_recv()
    len_q, len_p = [jnp.sum(jnp.where(lane[:1] == p.c, len_buf[i, 0:1], 0.0), axis=1, keepdims=True) for i in range(2)]

    def project(m, out, row):
        @pl.loop(0, 3)
        def _(n):
            cols = block(n, 256)
            acc = dot(x[...], wa[m, :, :, :, cols].reshape(768, 256))
            if row is not None:
                acc = acc + vec[row : row + 1, cols]
            out[:, cols] = low(acc)

    def store_prob(j):
        return pltpu.make_async_copy(prob.at[lax.rem(j, 2)], prob_out.at[pl.ds(j * 2, 2)], psem.at[lax.rem(j, 2)])

    def attention(low_j, high_j):
        @pl.loop(low_j, high_j)
        def _(j):
            cols = block(j, 128)
            slot = lax.rem(j, 2)

            @pl.when(j >= 2)
            def _():
                store_prob(j - 2).wait()

            for (start, size, rb), length in zip(SPANS, (len_p, len_q)):
                span = slice(start, start + size)
                kp, vp = k[span, cols], v[span, cols]
                valid = wide(lax.broadcasted_iota(jnp.int32, (1, size), 1)) < length
                for r in range(0, size, rb):
                    qp = q[start + r : start + r + rb, cols]
                    total = None
                    for h in range(2):
                        mask = head_mask(h)
                        scores = dot_nt(qp * (mask * 0.125), kp)
                        scores = jnp.where(valid, scores, -1e9)
                        e = jnp.exp(scores - jnp.max(scores, axis=1, keepdims=True))
                        w = low(e * (1.0 / jnp.sum(e, axis=1, keepdims=True)))
                        if size == S:
                            prob[slot, h, r : r + rb] = w
                        else:
                            prob_q[2 * j + h] = w
                        piece = dot(w, vp * mask)
                        total = piece if total is None else total + piece
                    act[start + r : start + r + rb, cols] = low(total)
            store_prob(j).start()

    project(1, k, None)
    gather.tick(LAGS[2] + 1)
    vector(5, p.q2, p.sib()).wait_recv()
    vector(6, p.q12, p.sib()).wait_recv()
    expand_vectors(vectors[...], vec)
    project(0, q, 0)
    q_t[...] = q[...].T
    gather.tick(LAGS[2] + 2)
    project(2, v, 1)
    attention(0, 1)

    gather.tick(LAGS[2] + 3)
    attention(1, 3)
    gather.tick(LAGS[2] + 4)
    attention(3, 5)
    gather.tick(LAGS[2] + 5)
    attention(5, 6)
    ctx_t[...] = act[:, :768].T

    def gain(row):
        return vec[row : row + 1, :768]

    @pl.loop(0, 3)
    def _(n):
        span = block(n, 192)
        first = wide(x[span]) + (dot(act[span, :768], wa[3].reshape(768, 768)) + gain(2))
        center = first - jnp.mean(first, axis=1, keepdims=True)
        scale = lax.rsqrt(jnp.mean(center * center, axis=1, keepdims=True) + 1e-12)
        y = center * scale
        y1[span] = y
        r1[span] = scale
        normed[span] = low(y * gain(4) + gain(5))

    def hidden(low_n, high_n):
        @pl.loop(low_n, high_n)
        def _(n):
            cols = block(n, 256)
            u = dot(normed[...], wi[:, :, :, cols].reshape(768, 256)) + vec[8:9, cols]
            cdf = 0.5 * (1.0 + lax.erf(u * 0.7071067811865476))
            act[:, cols] = low(u * cdf)
            slope[:, cols] = low(cdf + u * (0.3989422804014327 * jnp.exp(-0.5 * u * u)))

    gather.tick(LAGS[2] + 6)
    norm_t[...] = normed[...].T
    hidden(0, 6)
    gather.tick(LAGS[2] + 7)
    hidden(6, 12)

    y_sum[...] = jnp.zeros_like(y_sum)

    def turn_act():
        for b in range(4):
            turned = act[:, b * 768 : (b + 1) * 768].T
            for s in range(4):
                for n in range(4):
                    row = n * 768 + (b * 4 + s) * 48
                    act_t[row : row + 48] = turned[s * 192 + n * 48 : s * 192 + n * 48 + 48]

    def outer(i):
        cols = [slice(which * 384 + i * 128, which * 384 + i * 128 + 128) for which in range(2)]
        right = jnp.concatenate([wo[:, :, :, c].reshape(3072, 128) for c in cols], axis=1)
        add = dot(act[...], right)
        for which, c in enumerate(cols):
            y2[:, c] = add[:, which * 128 : which * 128 + 128] + (y1[:, c] * vec[4:5, c] + vec[5:6, c] + vec[3:4, c])

    for i in range(3):
        gather.tick(LAGS[2] + 8 + i)
        if i == 0:
            turn_act()
        outer(i)

    @pl.loop(0, 3)
    def _(n):
        span = block(n, 192)
        second = y2[span]
        center = second - jnp.mean(second, axis=1, keepdims=True)
        scale = lax.rsqrt(jnp.mean(center * center, axis=1, keepdims=True) + 1e-12)
        y = center * scale
        y2[span] = y
        r2[span] = scale
        at = wide(lax.broadcasted_iota(jnp.int32, (192, 1), 0) + n * 192)
        for row, keep in ((0, (at >= S) & (at - S < len_q)), (1, (at < S) & (at < len_p))):
            y_sum[row : row + 1] += jnp.sum(jnp.where(keep, y, 0.0), axis=0, keepdims=True)

    mine = jnp.concatenate([y_sum[0:1] / len_q, y_sum[1:2] / len_p]) * gain(6) + gain(7)
    root = jnp.sqrt(jnp.sum(mine * mine, axis=1, keepdims=True) + 1e-6)
    unit = mine / root
    rows[me, :, :768] = unit[0:1]
    rows[me, :, 768:] = unit[1:2]

    @pl.loop(1, pairs)
    def _(i):
        remote(rows.at[me], rows.at[me], xsem.at[4], xsem.at[5], device(lax.rem(me + i, pairs))).start()
    gather.finish()
    len_copy.wait_send()
    for i in range(1, 7):
        vector(i, p.quad, p.sib()).wait_send()
    store_prob(4).wait()
    store_prob(5).wait()
    rest = rows.at[pl.ds(0, pairs - 1)]
    remote(rest, rest, xsem.at[4], xsem.at[5], p.sib()).wait_recv()
    step = 768 if pairs <= 64 else 128
    logits = None
    for at in range(0, 768, step):
        part = lax.dot_general(
            rows[:, 0, 768 + at : 768 + at + step], rows[:, 0, at : at + step], (((1,), (1,)), ((), ())),
            precision=lax.Precision.HIGHEST, preferred_element_type=jnp.float32)
        logits = part if logits is None else logits + part
    logits = logits / 0.01
    hit = targets[...] == lax.broadcasted_iota(jnp.int32, (pairs, pairs), 0)
    top = jnp.max(logits, axis=0, keepdims=True)
    lse = jnp.log(jnp.sum(jnp.exp(logits - top), axis=0, keepdims=True)) + top
    picked = jnp.sum(jnp.where(hit, logits, 0.0), axis=0, keepdims=True)
    loss[...] = jnp.broadcast_to(jnp.sum(lse - picked, axis=1, keepdims=True) / pairs, loss.shape)
    d_logits = seq * (jnp.exp(logits - lse) - jnp.where(hit, 1.0, 0.0))
    across = lax.broadcasted_iota(jnp.int32, (pairs, pairs), 1)
    down = lax.broadcasted_iota(jnp.int32, (pairs, pairs), 0)
    for_q = jnp.sum(jnp.where(across == me, d_logits, 0.0), axis=1, keepdims=True)
    for_p = jnp.sum(jnp.where(down == me, d_logits, 0.0), axis=0, keepdims=True)
    for_p = jnp.sum(jnp.where(across == down, for_p, 0.0), axis=1, keepdims=True)
    for row, weight in enumerate((for_q, for_p)):
        d_unit = jnp.sum(weight * rows[:, 0, (1 - row) * 768 : (2 - row) * 768], axis=0, keepdims=True) / 0.01
        u = unit[row : row + 1]
        d_pool[row : row + 1] = (d_unit - u * jnp.sum(u * d_unit, axis=1, keepdims=True)) / root[row : row + 1]
    remote(rest, rest, xsem.at[4], xsem.at[5], p.sib()).wait_send()
    return len_p, len_q


def backward_part(p, len_p, len_q, d_pool, y_sum, vec, prob_hbm, prob, prob_q, dxq_out, dxp_out, dvec_out, grads,
                  wa, wi, wo, d_low, k, v, d_inner, act_t, slope, x_t, q_t, ctx_t, norm_t, y1, r1, d_second, r2, ds_buf,
                  d_vec, v_in, v_out, chunks, psem, vsem, xsem):
    g_query, g_key, g_value, g_output, g_inner, g_outer = grads

    def load_prob(j):
        return pltpu.make_async_copy(prob_hbm.at[pl.ds(j * 2, 2)], prob.at[lax.rem(j, 2)], psem.at[lax.rem(j, 2)])

    load_prob(0).start()
    load_prob(1).start()

    def result(e, which):
        cols = pl.ds(pl.multiple_of(which * 384, 128), 384)
        if e < 4:
            return g_outer.at[pl.ds(e * 48, 48), cols]
        if e < 8:
            return g_inner.at[:, pl.ds(pl.multiple_of((e - 4) * 768 + which * 384, 128), 384)]
        return (g_output, g_query, g_key, g_value)[e - 8].at[:, cols]

    sc = Scatter(p, chunks, result)
    d_vec[...] = jnp.zeros_like(d_vec)

    def gain(row):
        return vec[row : row + 1, :768]

    def tally(row, value):
        d_vec[row : row + 1] += jnp.sum(value, axis=0, keepdims=True)

    pool_q = d_pool[0:1] / len_q
    pool_p = d_pool[1:2] / len_p

    def norm_back(d, row, yy, scale, rows):
        g = d * gain(row)
        d = (g - jnp.mean(g, axis=1, keepdims=True) - yy * jnp.mean(g * yy, axis=1, keepdims=True)) * scale
        d_second[rows] = d
        d_low[rows] = low(d)
        return d


    @pl.loop(0, 3)
    def _(n):
        rows = block(n, 192)
        at = wide(lax.broadcasted_iota(jnp.int32, (192, 1), 0) + n * 192)
        d_rows = jnp.where(at < S, jnp.where(at < len_p, pool_p, 0.0), jnp.where(at - S < len_q, pool_q, 0.0))
        norm_back(d_rows, 6, d_second[rows], r2[rows], rows)


    def emit_outer(n):
        def bias(cols, values):
            d_vec[3:4, cols] = jnp.sum(wide(values), axis=0, keepdims=True)
        sc.emit(n, lambda: act_t[n * 768 : (n + 1) * 768], lambda cols: d_low[:, cols], bias if n == 3 else None)

    def emit_inner(n):
        def bias(cols, values):
            d_vec[8 + n : 9 + n, cols] = jnp.sum(wide(values), axis=0, keepdims=True)
        sc.emit(4 + n, lambda: norm_t[...], lambda cols: d_inner[:, pl.ds(pl.multiple_of(n * 768 + cols.start, 256), 256)], bias)

    emit_outer(0)
    d_vec[6:7] = pool_q * y_sum[0:1] + pool_p * y_sum[1:2]
    d_vec[7:8] = d_pool[0:1] + d_pool[1:2]
    emit_outer(1)
    sc.stage0(0)
    emit_outer(2)
    sc.stage0(1)
    emit_outer(3)
    sc.stage0(2)

    def inner_back(low_n, high_n):
        @pl.loop(low_n, high_n)
        def _(n):
            cols = block(n, 768)
            d_inner[:, cols] = low(dot_nt(d_low[...], wo[n].reshape(768, 768)) * wide(slope[:, cols]))

    inner_back(0, 2)
    sc.stage0(3)
    inner_back(2, 4)
    emit_inner(0)
    sc.stage1(1)
    emit_inner(1)
    sc.stage0(4)
    emit_inner(2)
    sc.stage0(5)
    emit_inner(3)
    sc.stage0(6)
    sc.stage1(2)
    sc.stage2(1)

    def first_back(low_n, high_n):
        @pl.loop(low_n, high_n)
        def _(n):
            rows = block(n, 192)
            y = y1[rows]
            d = d_second[rows] + dot_nt(d_inner[rows], wi[...].reshape(768, 3072))
            tally(4, d * y)
            tally(5, d)
            d = norm_back(d, 4, y, r1[rows], rows)
            tally(2, wide(low(d)))

    first_back(0, 1)
    sc.stage0(7)
    first_back(1, 3)
    sc.stage1(3)
    sc.stage1(0)
    sc.stage2(2)
    sc.emit(8, lambda: ctx_t[...], lambda cols: d_low[:, cols])

    def part(i):
        return pl.ds(i * 768, 768)

    def pair_cols(i, j):
        return pl.ds(pl.multiple_of(i * 768 + j * 128, 128), 128)

    def head_rows(i, head):
        return pl.ds(pl.multiple_of(i * 768 + head * 64, 64), 64)

    @pl.loop(0, 3)
    def _(n):
        rows = block(n, 192)
        d_inner[rows, part(3)] = low(dot_nt(d_low[rows], wa[3].reshape(768, 768)))
    act_t[part(2)] = d_inner[:, part(3)].T
    sc.stage0(8)

    def attention(low_j, high_j):
        @pl.loop(low_j, high_j)
        def _(j):
            load_prob(j).wait()
            slot = lax.rem(j, 2)
            cols = block(j, 128)
            for start, size, rb in SPANS:
                rows = slice(start, start + size)
                kp, vp = k[rows, cols], v[rows, cols]
                dq_parts = [None] * (size // rb)
                for h in range(2):
                    probs = (lambda sl: prob[slot, h, sl]) if size == S else (lambda sl: prob_q[2 * j + h, sl])
                    mask = head_mask(h)
                    for r in range(0, size, rb):
                        d_p = dot_nt(d_inner[start + r : start + r + rb, pair_cols(3, j)] * mask, vp)
                        w = wide(probs(slice(r, r + rb)))
                        ds = low(w * (d_p - jnp.sum(w * d_p, axis=1, keepdims=True)))
                        ds_buf[h, r : r + rb, :size] = ds
                        piece = dot(ds, kp * mask)
                        i = r // rb
                        dq_parts[i] = piece if dq_parts[i] is None else dq_parts[i] + piece
                    head = 2 * j + h
                    act_t[head_rows(1, head), rows] = low(dot(act_t[head_rows(2, head), rows], probs(slice(0, size))))
                    act_t[head_rows(0, head), rows] = low(dot(q_t[head_rows(0, head), rows], ds_buf[h, :size, :size]) * 0.125)
                for i, piece in enumerate(dq_parts):
                    d_inner[start + i * rb : start + (i + 1) * rb, pair_cols(0, j)] = low(piece * 0.125)

            @pl.when(j < 4)
            def _():
                load_prob(j + 2).start()

    attention(0, 2)
    sc.stage1(4)
    sc.stage2(3)
    sc.stage3(1)
    attention(2, 6)
    sc.stage1(5)
    sc.stage2(4)
    sc.stage2(0)
    sc.stage3(2)
    d_inner[:, part(1)] = act_t[part(0)].T
    d_inner[:, part(2)] = act_t[part(1)].T

    def emit_first(n):
        row = (0, None, 1)[n]

        def bias(cols, values):
            d_vec[row : row + 1, cols] = jnp.sum(wide(values), axis=0, keepdims=True)
        sc.emit(9 + n, lambda: x_t[...], lambda cols: d_inner[:, pl.ds(pl.multiple_of(n * 768 + cols.start, 256), 256)], None if row is None else bias)

    emit_first(0)
    emit_first(1)
    sc.stage0(9)
    emit_first(2)
    sc.stage0(10)

    def vector(i, src, target):
        return remote(src, v_in.at[i], vsem.at[0, i], vsem.at[1, i], target)

    def vector_recv(i):
        vector(i, v_in.at[i], p.sib()).wait_recv()
        return v_in[i]

    vector(0, d_vec.at[:, sc.other], p.sib()).start()
    sc.stage1(6)
    sc.stage2(5)
    sc.stage3(3)
    sc.stage3(0)
    sc.stage0(11)

    @pl.loop(0, 3)
    def _(n):
        rows = block(n, 192)
        d = d_second[rows]
        for i in range(3):
            d = d + dot_nt(d_inner[rows, part(i)], wa[i].reshape(768, 768))
        d_low[rows] = low(d)
    tokens = [(d_low.at[pl.ds(0, S)], dxp_out), (d_low.at[pl.ds(S, Q)], dxq_out)]
    mine = [pltpu.make_async_copy(src, out.at[p.c], xsem.at[i]) for i, (src, out) in enumerate(tokens)]
    theirs = [remote(src, out.at[p.c], xsem.at[2 + i], xsem.at[4 + i], p.sib()) for i, (src, out) in enumerate(tokens)]
    for copy in mine + theirs:
        copy.start()
    v_out[0] = d_vec[:, sc.own] + vector_recv(0)
    vector(1, v_out.at[0], p.n2()).start()
    sc.stage1(7)
    sc.stage2(6)
    sc.stage3(4)
    sc.stage1(8)
    sc.stage2(7)
    sc.stage3(5)
    sc.stage1(9)
    sc.stage2(8)
    sc.stage3(6)
    v_out[1] = v_out[0] + vector_recv(1)
    vector(2, v_out.at[1], p.n1()).start()
    sc.stage1(10)
    sc.stage2(9)
    sc.stage3(7)
    sc.stage1(11)
    v_out[2] = v_out[1] + vector_recv(2)
    for i in range(1, 4):
        vector(2 + i, v_out.at[2], p.up(i)).start()
    sc.stage2(10)
    sc.stage3(8)
    sc.stage2(11)
    dvec_out[:, sc.own] = v_out[2] + vector_recv(3) + vector_recv(4) + vector_recv(5)
    last = remote(dvec_out.at[:, sc.own], dvec_out.at[:, sc.own], vsem.at[0, 6], vsem.at[1, 6], p.sib())
    last.start()
    for e in range(9, 12):
        sc.stage3(e)
    for i, (src, out) in enumerate(tokens):
        mine[i].wait()
        theirs[i].wait_send()
        remote(out.at[1 - p.c], out.at[1 - p.c], xsem.at[2 + i], xsem.at[4 + i], p.sib()).wait_recv()
    remote(dvec_out.at[:, sc.other], dvec_out.at[:, sc.other], vsem.at[0, 6], vsem.at[1, 6], p.sib()).wait_recv()
    last.wait_send()
    for i in range(6):
        vector(i, v_in.at[i], p.sib()).wait_send()
    sc.finish(12)


def layer_kernel(inner, seq, lengths, targets, *refs):
    vector_shards, weights, (query_tokens, passage_tokens) = refs[:9], refs[9:15], refs[15:17]
    loss, dxq_out, dxp_out, dvec_out = refs[17:21]
    grads, prob_hbm = refs[21:27], refs[27]
    (wa, wi, wo, x, q, k, v, act, act_t, slope, x_t, q_t, ctx_t, norm_t, y1, r1, y2, r2, prob, prob_q, ds_buf, vec, d_pool, y_sum,
     rows, packed, vectors, len_buf, d_vec, v_in, v_out) = refs[28:59]
    chunks, (g_ssem, g_rsem, g_lsem, g_vsem, psem, g_xsem, vsem, xsem) = refs[59:67], refs[67:75]
    p = Place(inner)
    len_p, len_q = forward_part(
        p, seq, lengths, targets, vector_shards, weights, query_tokens, passage_tokens, d_pool, loss, prob_hbm, vec, prob, prob_q,
        wa, wi, wo, x, q, k, v, act, act_t, slope, x_t, q_t, ctx_t, norm_t, y1, r1, y2, r2, y_sum, rows, packed, vectors, len_buf,
        g_ssem, g_rsem, g_lsem, g_vsem, psem, g_xsem)
    backward_part(
        p, len_p, len_q, d_pool, y_sum, vec, prob_hbm, prob, prob_q, dxq_out, dxp_out, dvec_out, grads,
        wa, wi, wo, x, k, v, act, act_t, slope, x_t, q_t, ctx_t, norm_t, y1, r1, y2, r2, ds_buf,
        d_vec, v_in, v_out, chunks, psem, vsem, xsem)


def layer_call(inner, seq, lengths, targets, vectors, weights, query_tokens, passage_tokens, cid=0):
    bf, f32 = jnp.bfloat16, jnp.float32
    sds, vmem, dma = jax.ShapeDtypeStruct, pltpu.VMEM, pltpu.SemaphoreType.DMA
    pairs = targets.shape[1]
    outs = [sds((8, 128), f32), sds((2, Q, 768), bf), sds((2, S, 768), bf), sds((16, 768), f32)]
    outs += [sds((48, 768), f32)] * 4 + [sds((48, 3072), f32), sds((192, 768), f32), sds((12, S, S), bf)]
    wide_rows, rows, turned, column = vmem((T, 768), f32), vmem((T, 768), bf), vmem((768, T), bf), vmem((T, 1), f32)
    scratch = [vmem((4, 4, 4, 48, 768), bf), vmem((4, 4, 48, 3072), bf), vmem((4, 4, 192, 768), bf)] + [rows] * 4
    scratch += [vmem((T, 3072), bf), vmem((3072, T), bf), vmem((T, 3072), bf)] + [turned] * 4 + [wide_rows, column] * 2
    scratch += [vmem((2, 2, S, S), bf), vmem((12, Q, Q), bf), vmem((2, S, S), bf), vmem((16, 3072), f32), vmem((2, 768), f32), vmem((2, 768), f32)]
    scratch += [vmem((pairs, 1, 1536), f32), vmem((16, 128), f32), vmem((4, 4, 16, 128), bf), vmem((2, 8, 128), f32)]
    scratch += [vmem((16, 768), f32), vmem((6, 16, 384), f32), vmem((3, 16, 384), f32)]
    scratch += [vmem((2, 4, 4, 48, 768), bf), vmem((4, 4, 4, 48, 384), bf), vmem((12, 4, 4, 48, 384), bf), vmem((12, 2, 4, 48, 384), bf)]
    scratch += [vmem((12, 4, 48, 384), bf), vmem((12, 3, 48, 384), bf), dma((12, 8)), dma((12, 8))]
    scratch += [dma((11, 12)), dma((11, 12)), dma((11,)), dma((2, 7)), dma((2,)), dma((6,)), dma((2, 7)), dma((6,))]
    return pl.pallas_call(
        functools.partial(layer_kernel, inner, seq),
        out_shape=outs,
        in_specs=[pl.BlockSpec(memory_space=pltpu.SMEM)] + [VM] * 10 + [ANY] * 8,
        out_specs=[VM, ANY, ANY] + [VM] * 7 + [ANY],
        scratch_shapes=scratch,
        compiler_params=pltpu.CompilerParams(collective_id=cid, has_side_effects=True, vmem_limit_bytes=63 << 20),
        name="layer",
    )(lengths, targets, *vectors, *weights, query_tokens, passage_tokens)


def outputs_kernel(inner, loss_in, dxq, dxp, d_vec, *refs):
    grads, (loss, q_out, p_out), g_outs, v_outs = refs[:6], refs[6:9], refs[9:15], refs[15:24]
    q_low, p_low, q_wide, p_wide, isem, osem, gsem = refs[24:]
    copies = [pltpu.make_async_copy(src, dst, gsem.at[i]) for i, (src, dst) in enumerate(zip(grads, g_outs))]
    parts = [(dxp.at[i, pl.ds(r, 256)], p_low.at[i, pl.ds(r, 256)], p_wide.at[i, pl.ds(r, 256)], p_out.at[i, pl.ds(r, 256)]) for i in range(2) for r in (0, 256)]
    parts.append((dxq, q_low, q_wide, q_out))
    loads = [pltpu.make_async_copy(part[0], part[1], isem.at[i]) for i, part in enumerate(parts)]
    for copy in loads + copies:
        copy.start()
    loss[...] = loss_in[0:1, 0:1]
    shard = lax.axis_index("dp") // inner
    for size, first, outs in ((48, 0, v_outs[:8]), (192, 8, v_outs[8:])):
        at = lax.broadcasted_iota(jnp.int32, (768, 1), 0) - lax.rem(shard * size, 768)
        pick = jnp.where(at == lax.broadcasted_iota(jnp.int32, (1, size), 1), 1.0, 0.0)
        rows = d_vec[0:8] if size == 48 else d_vec[8:16]
        mine = jnp.dot(rows, pick, precision=lax.Precision.HIGHEST, preferred_element_type=jnp.float32)
        if size == 48:
            for i in range(8):
                outs[i][...] = mine[i : i + 1]
        else:
            row = lax.broadcasted_iota(jnp.int32, (8, 1), 0)
            outs[0][...] = jnp.sum(jnp.where(row == shard // 4, mine, 0.0), axis=0, keepdims=True)
    stores = []
    for i, (_, source, wider, out) in enumerate(parts):
        loads[i].wait()
        wider[...] = wide(source[...])
        stores.append(pltpu.make_async_copy(wider, out, osem.at[i]))
        stores[-1].start()
    for copy in stores + copies:
        copy.wait()


def outputs_call(inner, loss, dxq, dxp, d_vec, grads):
    sds, f32, vmem, dma = jax.ShapeDtypeStruct, jnp.float32, pltpu.VMEM, pltpu.SemaphoreType.DMA
    outs = [sds((1, 1), f32), sds(dxq.shape, f32), sds(dxp.shape, f32)] + [sds(g.shape, f32) for g in grads]
    outs += [sds((1, 48), f32)] * 8 + [sds((1, 192), f32)]
    return pl.pallas_call(
        functools.partial(outputs_kernel, inner),
        out_shape=outs,
        in_specs=[VM, ANY, ANY, VM] + [VM] * 6,
        out_specs=[VM] + [ANY] * 8 + [VM] * 9,
        scratch_shapes=[vmem(dxq.shape, dxq.dtype), vmem(dxp.shape, dxp.dtype), vmem(dxq.shape, f32), vmem(dxp.shape, f32), dma((5,)), dma((5,)), dma((6,))],
        compiler_params=pltpu.CompilerParams(vmem_limit_bytes=62 << 20),
        name="write_outputs",
    )(loss, dxq, dxp, d_vec, *grads)


def per_device(
    query_tokens, passage_tokens, lengths, positives,
    query_weight, key_weight, value_weight, output_weight, inner_weight, outer_weight,
    query_bias, value_bias, output_bias, inner_bias, outer_bias,
    first_gain, first_shift, second_gain, second_shift,
):
    inner = lax.axis_size("dp") // 16
    groups = None if inner == 1 else [[h * inner + i for i in range(inner)] for h in range(16)]
    seq = passage_tokens.shape[1]

    def fetch(w):
        if groups is None:
            return w
        return lax.all_gather(w, "dp", axis=0, tiled=True, axis_index_groups=groups)

    weights = [fetch(w) for w in (query_weight, key_weight, value_weight, output_weight, inner_weight, outer_weight)]
    vectors = (query_bias, value_bias, output_bias, outer_bias, first_gain, first_shift, second_gain, second_shift, inner_bias)
    vectors = [fetch(w)[None] for w in vectors[:8]] + [fetch(inner_bias)]
    loss, dxq, dxp, d_vec, *grads, _ = layer_call(
        inner, float(seq), lengths, positives[None], vectors, weights, query_tokens, passage_tokens)
    loss, dxq, dxp, *grads = outputs_call(inner, loss, dxq, dxp, d_vec, grads)
    grads = [g.reshape(-1) if g.shape[0] == 1 else g for g in grads]

    def finish(x):
        if groups is None:
            return x
        return lax.psum_scatter(x, "dp", scatter_dimension=0, tiled=True, axis_index_groups=groups)

    grads = [finish(g) for g in grads]
    flat = grads[6:]
    return (loss[0, 0], dxq, dxp, *grads[:6], flat[0], flat[1], flat[2], flat[8], *flat[3:8])


def solution(mesh):
    rows3, rows2, rows1 = P("dp", None, None), P("dp", None), P("dp")
    return jax.shard_map(
        per_device,
        mesh=mesh,
        in_specs=(rows3, rows3, P("tower", "dp"), P()) + (rows2,) * 6 + (rows1,) * 9,
        out_specs=(P(), rows3, rows3) + (rows2,) * 6 + (rows1,) * 9,
        check_vma=False,
    )
```

```python
import functools

import jax
import jax.numpy as jnp
from jax import lax
from jax.experimental import pallas as pl
from jax.experimental.pallas import tpu as pltpu
from jax.sharding import PartitionSpec as P

MESH = pl.DeviceIdType.MESH
ANY = pl.BlockSpec(memory_space=pl.ANY)
VM = pl.BlockSpec(memory_space=pltpu.VMEM)


class Place:
    def __init__(self, inner):
        dp = lax.axis_index("dp")
        self.c = lax.axis_index("tower")
        self.inner = inner
        self.low = lax.rem(dp, inner)
        self.me = dp // inner
        self.z = self.me // 4
        self.quad = lax.rem(self.me, 4)
        s1 = 1 + self.c
        s2 = 2 - self.c
        b1 = lax.rem(self.quad // s1, 2)
        b2 = lax.rem(self.quad // s2, 2)
        self.q1 = self.quad + s1 * (1 - 2 * b1)
        self.q2 = self.quad + s2 * (1 - 2 * b2)
        self.q12 = 3 - self.quad
        self.quads = (self.quad, self.q1, self.q2, self.q12)

    def ring(self, k):
        return lax.rem(self.z + k, 4)

    def dev(self, group):
        return {"dp": group * self.inner + self.low, "tower": self.c}

    def n1(self):
        return self.dev(self.z * 4 + self.q1)

    def n2(self):
        return self.dev(self.z * 4 + self.q2)

    def up(self, k):
        return self.dev(self.ring(k) * 4 + self.quad)

    def sib(self):
        return {"dp": self.me * self.inner + self.low, "tower": 1 - self.c}

    def across(self, k):
        return {"dp": (self.ring(k) * 4 + self.quad) * self.inner + self.low, "tower": 1 - self.c}

    def greet(self):
        for target in (self.up(1), self.up(2), self.up(3), self.n1(), self.n2(), self.sib()):
            pl.semaphore_signal(pltpu.get_barrier_semaphore(), inc=1, device_id=target, device_id_type=MESH)

    def met(self):
        pl.semaphore_wait(pltpu.get_barrier_semaphore(), 6)


def remote(src, dst, send_sem, recv_sem, target):
    return pltpu.make_async_remote_copy(
        src_ref=src, dst_ref=dst, send_sem=send_sem, recv_sem=recv_sem, device_id=target, device_id_type=MESH
    )


S, Q = 512, 64
T = S + Q


def dot(left, right):
    return jnp.dot(left, right, preferred_element_type=jnp.float32)


def dot_nt(left, right):
    return lax.dot_general(left, right, (((1,), (1,)), ((), ())), preferred_element_type=jnp.float32)


def block(index, size):
    return pl.ds(pl.multiple_of(index * size, size), size)


def low(x):
    return x.astype(jnp.bfloat16)


def wide(x):
    return x.astype(jnp.float32)


def head_mask(h):
    lane = lax.broadcasted_iota(jnp.int32, (1, 128), 1)
    return low(jnp.where(lane // 64 == h, 1.0, 0.0))


SPANS = ((0, S, 256), (S, Q, Q))


class Gather:
    last = 10

    def __init__(self, p, shards, wa, wi, wo, ssem, rsem, lsem):
        self.p, self.shards, self.wa, self.wi, self.wo = p, shards, wa, wi, wo
        self.ssem, self.rsem, self.lsem = ssem, rsem, lsem

    def cols(self, t, which):
        if t < 8:
            return pl.ds(pl.multiple_of(which * 384 if t < 4 else (t - 4) * 768 + which * 384, 128), 384)
        return pl.ds(pl.multiple_of(which * 384 + (t - 8) * 128, 128), 128)

    def shard(self, t):
        ref = self.shards[(1, 0, 2, 3)[t]] if t < 4 else self.shards[4 if t < 8 else 5]
        return ref.at[:, self.cols(t, self.p.c)]

    def whole(self, t):
        return self.wa.at[(1, 0, 2, 3)[t]] if t < 4 else self.wi if t < 8 else self.wo

    def one(self, t, z, q):
        return self.whole(t).at[z, q, :, self.cols(t, self.p.c)]

    def four(self, t, q, which):
        return self.whole(t).at[:, q, :, self.cols(t, which)]

    def plane(self, t, z, which):
        return self.whole(t).at[z, :, :, self.cols(t, which)]

    def copy(self, src, dst, t, k, target):
        return remote(src, dst, self.ssem.at[t, k], self.rsem.at[t, k], target)

    def recv(self, t, k, ref):
        self.copy(ref, ref, t, k, self.p.sib()).wait_recv()

    def push(self, view, t, k, target):
        self.copy(view, view, t, k, target).start()

    def local(self, t):
        return pltpu.make_async_copy(self.shard(t), self.one(t, self.p.z, self.p.quad), self.lsem.at[t])

    def stage_own(self, t):
        p = self.p
        self.local(t).start()
        mine = self.one(t, p.z, p.quad)
        for k in range(1, 4) if t < self.last else ():
            self.copy(self.shard(t), mine, t, k, p.up(k)).start()
        self.copy(self.shard(t), mine, t, 4, p.n1()).start()
        self.copy(self.shard(t), mine, t, 5, p.n2()).start()

    def stage_z(self, t):
        p = self.p
        for k in range(1, 4):
            view = self.one(t, p.ring(4 - k), p.quad)
            self.recv(t, k, view)
            self.push(view, t, 4, p.n1())
            self.push(view, t, 5, p.n2())
        self.local(t).wait()
        self.push(self.four(t, p.quad, p.c), t, 8, p.sib())

    def stage_one(self, t):
        p = self.p
        view = self.four(t, p.q1, p.c)
        self.recv(t, 4, view)
        self.push(view, t, 6, p.n2())
        self.push(view, t, 9, p.sib())

    def stage_two(self, t):
        p = self.p
        for k, q in ((5, p.q2), (6, p.q12)):
            view = self.four(t, q, p.c)
            self.recv(t, k, view)
            self.push(view, t, k + 5, p.sib())

    def stage_sib(self, t):
        p = self.p
        for k, q in ((8, p.quad), (9, p.q2), (10, p.q1), (11, p.q12)):
            self.recv(t, k, self.four(t, q, 1 - p.c))

    def last_one(self):
        p, t = self.p, self.last
        view = self.one(t, p.z, p.q1)
        self.recv(t, 4, view)
        self.push(view, t, 6, p.n2())

    def last_two(self):
        p, t = self.p, self.last
        self.recv(t, 5, self.one(t, p.z, p.q2))
        self.recv(t, 6, self.one(t, p.z, p.q12))
        self.local(t).wait()
        view = self.plane(t, p.z, p.c)
        for k in range(1, 4):
            self.push(view, t, k, p.up(k))
        self.push(view, t, 8, p.sib())

    def last_z(self):
        p, t = self.p, self.last
        for k in range(1, 4):
            view = self.plane(t, p.ring(4 - k), p.c)
            self.recv(t, k, view)
            self.push(view, t, 8 + k, p.sib())

    def last_sib(self):
        p, t = self.p, self.last
        for k in range(4):
            self.recv(t, 8 + k, self.plane(t, p.ring(4 - k), 1 - p.c))

    def tick(self, i):
        for lag, stage in ((0, self.stage_z), (-AHEAD, self.stage_own), (LAGS[0], self.stage_one), (LAGS[1], self.stage_two), (LAGS[2], self.stage_sib)):
            if 0 <= i - lag < self.last:
                stage(i - lag)
        for at, stage in zip(LATE, (lambda: self.stage_own(self.last), self.last_one, self.last_two, self.last_z, self.last_sib)):
            if i == at:
                stage()

    def finish(self):
        p = self.p
        for t in range(self.last + 1):
            single, four, plane = self.one(t, p.z, p.quad), self.four(t, p.quad, p.c), self.plane(t, p.z, p.c)
            for k in (1, 2, 3, 4, 5, 6, 8, 9, 10, 11):
                view = (single if k < 4 else four) if t < self.last else (single if 4 <= k < 8 else plane)
                self.copy(view, view, t, k, p.sib()).wait_send()


def expand_vectors(shards, vec):
    at = wide(lax.broadcasted_iota(jnp.int32, (1, 768), 1))
    owner = jnp.floor((at + 0.5) * (1.0 / 48))
    lane = wide(lax.broadcasted_iota(jnp.int32, (128, 1), 0))
    rows = dot(shards.reshape(256, 128), low(jnp.where(lane == at - owner * 48, 1.0, 0.0))).reshape(16, 16, 768)
    shard = wide(lax.broadcasted_iota(jnp.int32, (16, 1, 1), 0))
    vec[:8, :768] = jnp.sum(jnp.where(owner[None] == shard, rows[:, :8], 0.0), axis=0)
    piece = wide(lax.broadcasted_iota(jnp.int32, (4, 4, 1), 0) * 4 + lax.broadcasted_iota(jnp.int32, (4, 4, 1), 1))
    for n in range(4):
        mine = jnp.sum(jnp.where(owner[None] == piece, rows[4 * n : 4 * n + 4, 8:12], 0.0), axis=0)
        vec[8:9, n * 768 : (n + 1) * 768] = jnp.sum(mine, axis=0, keepdims=True)


AHEAD = 4
LAGS = (1, 3, 4)
LATE = (0, 1, 5, 9, 13)


ALONG_Z = (0,)


class Scatter:
    def __init__(self, p, refs, result):
        self.p = p
        self.stage, self.r0, self.acc, self.r1, self.r2, self.r3, self.ssem, self.rsem = refs
        self.result = result
        self.own = pl.ds(pl.multiple_of(p.c * 384, 128), 384)
        self.other = pl.ds(pl.multiple_of((1 - p.c) * 384, 128), 384)

    def copy(self, src, dst, e, k, target):
        return remote(src, dst, self.ssem.at[e, k], self.rsem.at[e, k], target)

    def recv(self, e, k, ref):
        self.copy(ref, ref, e, k, self.p.sib()).wait_recv()

    def emit(self, e, left, right, extra=None):
        if e >= 2:
            self.shared(e - 2).wait_send()

        @pl.loop(0, 3)
        def _(n):
            cols = block(n, 256)
            values = right(cols)
            self.stage[e % 2, :, :, :, cols] = low(dot(left(), values)).reshape(4, 4, 48, 256)
            if extra is not None:
                extra(cols, values)
        self.shared(e).start()

    def shared(self, e):
        return self.copy(self.stage.at[e % 2, :, :, :, self.other], self.r0.at[e % 4], e, 0, self.p.sib())

    def stage0(self, e):
        p, acc = self.p, self.acc
        self.recv(e, 0, self.r0.at[e % 4])
        if e in ALONG_Z:
            for k in (1, 2, 3, 0):
                z = p.ring(k)
                acc[e, z] = self.stage[e % 2, z, :, :, self.own] + self.r0[e % 4, z]
                if k:
                    self.copy(acc.at[e, z], self.plane(e, k), e, k, p.up(k)).start()
            return
        for j, q in enumerate((p.q2, p.q12, p.q1, p.quad)):
            acc[e, :, q] = self.stage[e % 2, :, q, :, self.own] + self.r0[e % 4, :, q]
            if j < 2:
                self.copy(acc.at[e, :, q], self.r1.at[e, j], e, 1 + j, p.n2()).start()

    def plane(self, e, k):
        return self.r2.at[e] if k == 3 else self.r1.at[e, k - 1]

    def stage1(self, e):
        p, acc = self.p, self.acc
        if e in ALONG_Z:
            total = wide(acc[e, p.z])
            for k in range(1, 4):
                self.recv(e, k, self.plane(e, k))
                total = total + wide(self.plane(e, k)[...])
            acc[e, p.z] = low(total)
            for j, q in enumerate((p.q2, p.q12)):
                self.copy(acc.at[e, p.z, q], self.r3.at[e, j], e, 4 + j, p.n2()).start()
            return
        self.recv(e, 2, self.r1.at[e, 1])
        acc[e, :, p.q1] += self.r1[e, 1]
        self.copy(acc.at[e, :, p.q1], self.r2.at[e], e, 3, p.n1()).start()
        self.recv(e, 1, self.r1.at[e, 0])
        acc[e, :, p.quad] += self.r1[e, 0]

    def stage2(self, e):
        p, acc = self.p, self.acc
        if e in ALONG_Z:
            self.recv(e, 5, self.r3.at[e, 1])
            acc[e, p.z, p.q1] += self.r3[e, 1]
            self.copy(acc.at[e, p.z, p.q1], self.r3.at[e, 2], e, 6, p.n1()).start()
            self.recv(e, 4, self.r3.at[e, 0])
            return
        self.recv(e, 3, self.r2.at[e])
        acc[e, :, p.quad] += self.r2[e]
        for k in range(1, 4):
            self.copy(acc.at[e, p.ring(k), p.quad], self.r3.at[e, k - 1], e, 3 + k, p.up(k)).start()

    def stage3(self, e):
        p = self.p
        if e in ALONG_Z:
            self.recv(e, 6, self.r3.at[e, 2])
            total = wide(self.acc[e, p.z, p.quad]) + wide(self.r3[e, 0]) + wide(self.r3[e, 2])
        else:
            total = wide(self.acc[e, p.z, p.quad])
            for k in range(1, 4):
                self.recv(e, 3 + k, self.r3.at[e, k - 1])
                total = total + wide(self.r3[e, k - 1])
        view = self.result(e, p.c)
        view[...] = total
        self.copy(view, view, e, 7, p.sib()).start()

    def finish(self, count):
        for e in range(count):
            self.recv(e, 7, self.result(e, 1 - self.p.c))
            self.copy(self.result(e, self.p.c), self.result(e, self.p.c), e, 7, self.p.sib()).wait_send()
        for e in range(count - 2, count):
            self.shared(e).wait_send()
        four, one = self.r2.at[0], self.r3.at[0, 0]

        @pl.loop(0, count)
        def _(e):
            for k in range(1, 7):
                view = four if k < 4 else one
                self.copy(view, view, e, k, self.p.sib()).wait_send()


def forward_part(p, seq, lengths, targets, vector_shards, weights, query_tokens, passage_tokens, d_pool, loss, prob_out, vec, prob, prob_q,
                 wa, wi, wo, x, q, k, v, act, act_t, slope, x_t, q_t, ctx_t, norm_t, y1, r1, y2, r2, y_sum, rows, packed, vectors, len_buf,
                 ssem, rsem, lsem, vsem, psem, xsem):
    normed = q
    pairs = targets.shape[1]
    me = lax.axis_index("dp") * 2 + p.c

    def device(at):
        return {"dp": at // 2, "tower": lax.rem(at, 2)}

    x_loads = [pltpu.make_async_copy(passage_tokens.at[p.c], x.at[pl.ds(0, S)], xsem.at[0]), pltpu.make_async_copy(query_tokens.at[p.c], x.at[pl.ds(S, Q)], xsem.at[1])]
    for copy in x_loads:
        copy.start()
    barrier = pltpu.get_barrier_semaphore()

    @pl.loop(1, pairs)
    def _(i):
        pl.semaphore_signal(barrier, inc=1, device_id=device(lax.rem(me + i, pairs)), device_id_type=MESH)
    lane = lax.broadcasted_iota(jnp.int32, (8, 128), 1)
    len_buf[p.c] = jnp.where(lane == 0, lengths[0, 0].astype(jnp.float32), lengths[0, 1].astype(jnp.float32))
    packed[...] = jnp.zeros((16, 128), jnp.float32)
    for i, ref in enumerate(vector_shards[:8]):
        packed[i : i + 1, :48] = wide(ref[...])
    last = wide(vector_shards[8][...]).reshape(1, 192)
    for i in range(4):
        packed[8 + i : 9 + i, :48] = last[:, i * 48 : i * 48 + 48]
    vectors[p.z, p.quad] = low(packed[...])
    pl.semaphore_wait(barrier, pairs - 1)

    gather = Gather(p, weights, wa, wi, wo, ssem, rsem, lsem)
    len_copy = remote(len_buf.at[p.c], len_buf.at[p.c], xsem.at[2], xsem.at[3], p.sib())
    len_copy.start()

    def vector(i, q, target):
        view = vectors.at[p.z, p.quad] if i < 4 else vectors.at[:, q]
        return remote(view, view, vsem.at[0, i], vsem.at[1, i], target)

    for i in range(1, 4):
        vector(i, None, p.up(i)).start()
    for t in range(AHEAD):
        gather.stage_own(t)
    gather.tick(0)
    for i in range(1, 4):
        view = vectors.at[p.ring(4 - i), p.quad]
        remote(view, view, vsem.at[0, i], vsem.at[1, i], p.sib()).wait_recv()
    vector(4, p.quad, p.n1()).start()
    vector(5, p.quad, p.n2()).start()
    gather.tick(1)
    for copy in x_loads:
        copy.wait()
    gather.tick(2)
    vector(4, p.q1, p.sib()).wait_recv()
    vector(6, p.q1, p.n2()).start()
    for i in range(3, LAGS[2] + 1):
        gather.tick(i)
    remote(len_buf.at[1 - p.c], len_buf.at[1 - p.c], xsem.at[2], xsem.at[3], p.sib()).wait_recv()
    len_q, len_p = [jnp.sum(jnp.where(lane[:1] == p.c, len_buf[i, 0:1], 0.0), axis=1, keepdims=True) for i in range(2)]

    def project(m, out, row):
        @pl.loop(0, 3)
        def _(n):
            cols = block(n, 256)
            acc = dot(x[...], wa[m, :, :, :, cols].reshape(768, 256))
            if row is not None:
                acc = acc + vec[row : row + 1, cols]
            out[:, cols] = low(acc)

    def store_prob(j):
        return pltpu.make_async_copy(prob.at[lax.rem(j, 2)], prob_out.at[pl.ds(j * 2, 2)], psem.at[lax.rem(j, 2)])

    def attention(low_j, high_j):
        @pl.loop(low_j, high_j)
        def _(j):
            cols = block(j, 128)
            slot = lax.rem(j, 2)

            @pl.when(j >= 2)
            def _():
                store_prob(j - 2).wait()

            for (start, size, rb), length in zip(SPANS, (len_p, len_q)):
                span = slice(start, start + size)
                kp, vp = k[span, cols], v[span, cols]
                valid = wide(lax.broadcasted_iota(jnp.int32, (1, size), 1)) < length
                for r in range(0, size, rb):
                    qp = q[start + r : start + r + rb, cols]
                    total = None
                    for h in range(2):
                        mask = head_mask(h)
                        scores = dot_nt(qp * (mask * 0.125), kp)
                        scores = jnp.where(valid, scores, -1e9)
                        e = jnp.exp(scores - jnp.max(scores, axis=1, keepdims=True))
                        w = low(e * (1.0 / jnp.sum(e, axis=1, keepdims=True)))
                        if size == S:
                            prob[slot, h, r : r + rb] = w
                        else:
                            prob_q[2 * j + h] = w
                        piece = dot(w, vp * mask)
                        total = piece if total is None else total + piece
                    act[start + r : start + r + rb, cols] = low(total)
            store_prob(j).start()

    project(1, k, None)
    gather.tick(LAGS[2] + 1)
    vector(5, p.q2, p.sib()).wait_recv()
    vector(6, p.q12, p.sib()).wait_recv()
    expand_vectors(vectors[...], vec)
    project(0, q, 0)
    q_t[...] = q[...].T
    def gain(row):
        return vec[row : row + 1, :768]

    def attended():
        ctx_t[...] = act[:, :768].T
        pl.loop(0, 3)(first_norm)

    def first_norm(n):
        span = block(n, 192)
        first = wide(x[span]) + (dot(act[span, :768], wa[3].reshape(768, 768)) + gain(2))
        center = first - jnp.mean(first, axis=1, keepdims=True)
        scale = lax.rsqrt(jnp.mean(center * center, axis=1, keepdims=True) + 1e-12)
        y = center * scale
        y1[span] = y
        r1[span] = scale
        normed[span] = low(y * gain(4) + gain(5))

    def hidden(low_n, high_n):
        @pl.loop(low_n, high_n)
        def _(n):
            cols = block(n, 256)
            u = dot(normed[...], wi[:, :, :, cols].reshape(768, 256)) + vec[8:9, cols]
            cdf = 0.5 * (1.0 + lax.erf(u * 0.7071067811865476))
            act[:, cols] = low(u * cdf)
            slope[:, cols] = low(cdf + u * (0.3989422804014327 * jnp.exp(-0.5 * u * u)))

    gather.tick(LAGS[2] + 2)
    project(2, v, 1)
    attention(0, 2)
    gather.tick(LAGS[2] + 3)
    attention(2, 4)
    gather.tick(LAGS[2] + 4)
    attention(4, 6)
    attended()
    gather.tick(LAGS[2] + 5)
    hidden(0, 6)
    gather.tick(LAGS[2] + 6)
    hidden(6, 9)
    gather.tick(LAGS[2] + 7)
    hidden(9, 12)
    y_sum[...] = jnp.zeros_like(y_sum)

    def outer(i):
        cols = [slice(which * 384 + i * 128, which * 384 + i * 128 + 128) for which in range(2)]
        right = jnp.concatenate([wo[:, :, :, c].reshape(3072, 128) for c in cols], axis=1)
        add = dot(act[...], right)
        for which, c in enumerate(cols):
            y2[:, c] = add[:, which * 128 : which * 128 + 128] + (y1[:, c] * vec[4:5, c] + vec[5:6, c] + vec[3:4, c])

    for i in range(3):
        gather.tick(LAGS[2] + 8 + i)
        outer(i)

    @pl.loop(0, 3)
    def _(n):
        span = block(n, 192)
        second = y2[span]
        center = second - jnp.mean(second, axis=1, keepdims=True)
        scale = lax.rsqrt(jnp.mean(center * center, axis=1, keepdims=True) + 1e-12)
        y = center * scale
        y2[span] = y
        r2[span] = scale
        at = wide(lax.broadcasted_iota(jnp.int32, (192, 1), 0) + n * 192)
        for row, keep in ((0, (at >= S) & (at - S < len_q)), (1, (at < S) & (at < len_p))):
            y_sum[row : row + 1] += jnp.sum(jnp.where(keep, y, 0.0), axis=0, keepdims=True)

    def turn_act():
        for b in range(4):
            turned = act[:, b * 768 : (b + 1) * 768].T
            for s in range(4):
                for n in range(4):
                    row = n * 768 + (b * 4 + s) * 48
                    act_t[row : row + 48] = turned[s * 192 + n * 48 : s * 192 + n * 48 + 48]

    mine = jnp.concatenate([y_sum[0:1] / len_q, y_sum[1:2] / len_p]) * gain(6) + gain(7)
    root = jnp.sqrt(jnp.sum(mine * mine, axis=1, keepdims=True) + 1e-6)
    unit = mine / root
    rows[me, :, :768] = unit[0:1]
    rows[me, :, 768:] = unit[1:2]

    @pl.loop(1, pairs)
    def _(i):
        remote(rows.at[me], rows.at[me], xsem.at[4], xsem.at[5], device(lax.rem(me + i, pairs))).start()
    turn_act()
    norm_t[...] = normed[...].T
    x_t[...] = x[...].T
    gather.finish()
    len_copy.wait_send()
    for i in range(1, 7):
        vector(i, p.quad, p.sib()).wait_send()
    store_prob(4).wait()
    store_prob(5).wait()
    rest = rows.at[pl.ds(0, pairs - 1)]
    remote(rest, rest, xsem.at[4], xsem.at[5], p.sib()).wait_recv()
    step = 768 if pairs <= 64 else 128
    logits = None
    for at in range(0, 768, step):
        part = lax.dot_general(
            rows[:, 0, 768 + at : 768 + at + step], rows[:, 0, at : at + step], (((1,), (1,)), ((), ())),
            precision=lax.Precision.HIGHEST, preferred_element_type=jnp.float32)
        logits = part if logits is None else logits + part
    logits = logits / 0.01
    hit = targets[...] == lax.broadcasted_iota(jnp.int32, (pairs, pairs), 0)
    top = jnp.max(logits, axis=0, keepdims=True)
    lse = jnp.log(jnp.sum(jnp.exp(logits - top), axis=0, keepdims=True)) + top
    picked = jnp.sum(jnp.where(hit, logits, 0.0), axis=0, keepdims=True)
    loss[...] = jnp.broadcast_to(jnp.sum(lse - picked, axis=1, keepdims=True) / pairs, loss.shape)
    d_logits = seq * (jnp.exp(logits - lse) - jnp.where(hit, 1.0, 0.0))
    across = lax.broadcasted_iota(jnp.int32, (pairs, pairs), 1)
    down = lax.broadcasted_iota(jnp.int32, (pairs, pairs), 0)
    for_q = jnp.sum(jnp.where(across == me, d_logits, 0.0), axis=1, keepdims=True)
    for_p = jnp.sum(jnp.where(down == me, d_logits, 0.0), axis=0, keepdims=True)
    for_p = jnp.sum(jnp.where(across == down, for_p, 0.0), axis=1, keepdims=True)
    for row, weight in enumerate((for_q, for_p)):
        d_unit = jnp.sum(weight * rows[:, 0, (1 - row) * 768 : (2 - row) * 768], axis=0, keepdims=True) / 0.01
        u = unit[row : row + 1]
        d_pool[row : row + 1] = (d_unit - u * jnp.sum(u * d_unit, axis=1, keepdims=True)) / root[row : row + 1]
    remote(rest, rest, xsem.at[4], xsem.at[5], p.sib()).wait_send()
    return len_p, len_q


def backward_part(p, len_p, len_q, d_pool, y_sum, vec, prob_hbm, prob, prob_q, dxq_out, dxp_out, dvec_out, grads,
                  wa, wi, wo, d_low, k, v, d_inner, act_t, slope, x_t, q_t, ctx_t, norm_t, y1, r1, d_second, r2, ds_buf,
                  d_vec, v_in, v_out, chunks, psem, vsem, xsem):
    g_query, g_key, g_value, g_output, g_inner, g_outer = grads

    def load_prob(j):
        return pltpu.make_async_copy(prob_hbm.at[pl.ds(j * 2, 2)], prob.at[lax.rem(j, 2)], psem.at[lax.rem(j, 2)])

    load_prob(0).start()
    load_prob(1).start()

    def result(e, which):
        cols = pl.ds(pl.multiple_of(which * 384, 128), 384)
        if e < 4:
            return g_outer.at[pl.ds(e * 48, 48), cols]
        if e < 8:
            return g_inner.at[:, pl.ds(pl.multiple_of((e - 4) * 768 + which * 384, 128), 384)]
        return (g_output, g_query, g_key, g_value)[e - 8].at[:, cols]

    sc = Scatter(p, chunks, result)
    d_vec[...] = jnp.zeros_like(d_vec)

    def gain(row):
        return vec[row : row + 1, :768]

    def tally(row, value):
        d_vec[row : row + 1] += jnp.sum(value, axis=0, keepdims=True)

    pool_q = d_pool[0:1] / len_q
    pool_p = d_pool[1:2] / len_p

    def norm_back(d, row, yy, scale, rows):
        g = d * gain(row)
        d = (g - jnp.mean(g, axis=1, keepdims=True) - yy * jnp.mean(g * yy, axis=1, keepdims=True)) * scale
        d_second[rows] = d
        d_low[rows] = low(d)
        return d


    @pl.loop(0, 3)
    def _(n):
        rows = block(n, 192)
        at = wide(lax.broadcasted_iota(jnp.int32, (192, 1), 0) + n * 192)
        d_rows = jnp.where(at < S, jnp.where(at < len_p, pool_p, 0.0), jnp.where(at - S < len_q, pool_q, 0.0))
        norm_back(d_rows, 6, d_second[rows], r2[rows], rows)


    def emit_outer(n):
        def bias(cols, values):
            d_vec[3:4, cols] = jnp.sum(wide(values), axis=0, keepdims=True)
        sc.emit(n, lambda: act_t[n * 768 : (n + 1) * 768], lambda cols: d_low[:, cols], bias if n == 3 else None)

    def emit_inner(n):
        def bias(cols, values):
            d_vec[8 + n : 9 + n, cols] = jnp.sum(wide(values), axis=0, keepdims=True)
        sc.emit(4 + n, lambda: norm_t[...], lambda cols: d_inner[:, pl.ds(pl.multiple_of(n * 768 + cols.start, 256), 256)], bias)

    emit_outer(0)
    d_vec[6:7] = pool_q * y_sum[0:1] + pool_p * y_sum[1:2]
    d_vec[7:8] = d_pool[0:1] + d_pool[1:2]
    emit_outer(1)
    sc.stage0(0)
    emit_outer(2)
    sc.stage0(1)
    emit_outer(3)
    sc.stage0(2)

    def inner_back(low_n, high_n):
        @pl.loop(low_n, high_n)
        def _(n):
            cols = block(n, 768)
            d_inner[:, cols] = low(dot_nt(d_low[...], wo[n].reshape(768, 768)) * wide(slope[:, cols]))

    inner_back(0, 2)
    sc.stage0(3)
    inner_back(2, 4)
    emit_inner(0)
    sc.stage1(1)
    emit_inner(1)
    sc.stage0(4)
    emit_inner(2)
    sc.stage0(5)
    emit_inner(3)
    sc.stage0(6)
    sc.stage1(2)
    sc.stage2(1)

    def first_back(low_n, high_n):
        @pl.loop(low_n, high_n)
        def _(n):
            rows = block(n, 192)
            y = y1[rows]
            d = d_second[rows] + dot_nt(d_inner[rows], wi[...].reshape(768, 3072))
            tally(4, d * y)
            tally(5, d)
            d = norm_back(d, 4, y, r1[rows], rows)
            tally(2, wide(low(d)))

    first_back(0, 1)
    sc.stage0(7)
    first_back(1, 3)
    sc.stage1(3)
    sc.stage1(0)
    sc.stage2(2)
    sc.emit(8, lambda: ctx_t[...], lambda cols: d_low[:, cols])

    def part(i):
        return pl.ds(i * 768, 768)

    def pair_cols(i, j):
        return pl.ds(pl.multiple_of(i * 768 + j * 128, 128), 128)

    def head_rows(i, head):
        return pl.ds(pl.multiple_of(i * 768 + head * 64, 64), 64)

    @pl.loop(0, 3)
    def _(n):
        rows = block(n, 192)
        d_inner[rows, part(3)] = low(dot_nt(d_low[rows], wa[3].reshape(768, 768)))
    act_t[part(2)] = d_inner[:, part(3)].T
    sc.stage0(8)

    def attention(low_j, high_j):
        @pl.loop(low_j, high_j)
        def _(j):
            load_prob(j).wait()
            slot = lax.rem(j, 2)
            cols = block(j, 128)
            for start, size, rb in SPANS:
                rows = slice(start, start + size)
                kp, vp = k[rows, cols], v[rows, cols]
                dq_parts = [None] * (size // rb)
                for h in range(2):
                    probs = (lambda sl: prob[slot, h, sl]) if size == S else (lambda sl: prob_q[2 * j + h, sl])
                    mask = head_mask(h)
                    for r in range(0, size, rb):
                        d_p = dot_nt(d_inner[start + r : start + r + rb, pair_cols(3, j)] * mask, vp)
                        w = wide(probs(slice(r, r + rb)))
                        ds = low(w * (d_p - jnp.sum(w * d_p, axis=1, keepdims=True)))
                        ds_buf[h, r : r + rb, :size] = ds
                        piece = dot(ds, kp * mask)
                        i = r // rb
                        dq_parts[i] = piece if dq_parts[i] is None else dq_parts[i] + piece
                    head = 2 * j + h
                    act_t[head_rows(1, head), rows] = low(dot(act_t[head_rows(2, head), rows], probs(slice(0, size))))
                    act_t[head_rows(0, head), rows] = low(dot(q_t[head_rows(0, head), rows], ds_buf[h, :size, :size]) * 0.125)
                for i, piece in enumerate(dq_parts):
                    d_inner[start + i * rb : start + (i + 1) * rb, pair_cols(0, j)] = low(piece * 0.125)

            @pl.when(j < 4)
            def _():
                load_prob(j + 2).start()

    attention(0, 2)
    sc.stage1(4)
    sc.stage2(3)
    sc.stage3(1)
    attention(2, 6)
    sc.stage1(5)
    sc.stage2(4)
    sc.stage2(0)
    sc.stage3(2)
    d_inner[:, part(1)] = act_t[part(0)].T
    d_inner[:, part(2)] = act_t[part(1)].T

    def emit_first(n):
        row = (0, None, 1)[n]

        def bias(cols, values):
            d_vec[row : row + 1, cols] = jnp.sum(wide(values), axis=0, keepdims=True)
        sc.emit(9 + n, lambda: x_t[...], lambda cols: d_inner[:, pl.ds(pl.multiple_of(n * 768 + cols.start, 256), 256)], None if row is None else bias)

    emit_first(0)
    emit_first(1)
    sc.stage0(9)
    emit_first(2)
    sc.stage0(10)

    def vector(i, src, target):
        return remote(src, v_in.at[i], vsem.at[0, i], vsem.at[1, i], target)

    def vector_recv(i):
        vector(i, v_in.at[i], p.sib()).wait_recv()
        return v_in[i]

    vector(0, d_vec.at[:, sc.other], p.sib()).start()
    sc.stage1(6)
    sc.stage2(5)
    sc.stage3(3)
    sc.stage3(0)
    sc.stage0(11)

    @pl.loop(0, 3)
    def _(n):
        rows = block(n, 192)
        d = d_second[rows]
        for i in range(3):
            d = d + dot_nt(d_inner[rows, part(i)], wa[i].reshape(768, 768))
        d_low[rows] = low(d)
    tokens = [(d_low.at[pl.ds(0, S)], dxp_out), (d_low.at[pl.ds(S, Q)], dxq_out)]
    mine = [pltpu.make_async_copy(src, out.at[p.c], xsem.at[i]) for i, (src, out) in enumerate(tokens)]
    theirs = [remote(src, out.at[p.c], xsem.at[2 + i], xsem.at[4 + i], p.sib()) for i, (src, out) in enumerate(tokens)]
    for copy in mine + theirs:
        copy.start()
    v_out[0] = d_vec[:, sc.own] + vector_recv(0)
    vector(1, v_out.at[0], p.n2()).start()
    sc.stage1(7)
    sc.stage2(6)
    sc.stage3(4)
    sc.stage1(8)
    sc.stage2(7)
    sc.stage3(5)
    sc.stage1(9)
    sc.stage2(8)
    sc.stage3(6)
    v_out[1] = v_out[0] + vector_recv(1)
    vector(2, v_out.at[1], p.n1()).start()
    sc.stage1(10)
    sc.stage2(9)
    sc.stage3(7)
    sc.stage1(11)
    v_out[2] = v_out[1] + vector_recv(2)
    for i in range(1, 4):
        vector(2 + i, v_out.at[2], p.up(i)).start()
    sc.stage2(10)
    sc.stage3(8)
    sc.stage2(11)
    dvec_out[:, sc.own] = v_out[2] + vector_recv(3) + vector_recv(4) + vector_recv(5)
    last = remote(dvec_out.at[:, sc.own], dvec_out.at[:, sc.own], vsem.at[0, 6], vsem.at[1, 6], p.sib())
    last.start()
    for e in range(9, 12):
        sc.stage3(e)
    for i, (src, out) in enumerate(tokens):
        mine[i].wait()
        theirs[i].wait_send()
        remote(out.at[1 - p.c], out.at[1 - p.c], xsem.at[2 + i], xsem.at[4 + i], p.sib()).wait_recv()
    remote(dvec_out.at[:, sc.other], dvec_out.at[:, sc.other], vsem.at[0, 6], vsem.at[1, 6], p.sib()).wait_recv()
    last.wait_send()
    for i in range(6):
        vector(i, v_in.at[i], p.sib()).wait_send()
    sc.finish(12)


def layer_kernel(inner, seq, lengths, targets, *refs):
    vector_shards, weights, (query_tokens, passage_tokens) = refs[:9], refs[9:15], refs[15:17]
    loss, dxq_out, dxp_out, dvec_out = refs[17:21]
    grads, prob_hbm = refs[21:27], refs[27]
    (wa, wi, wo, x, q, k, v, act, act_t, slope, x_t, q_t, ctx_t, norm_t, y1, r1, y2, r2, prob, prob_q, ds_buf, vec, d_pool, y_sum,
     rows, packed, vectors, len_buf, d_vec, v_in, v_out) = refs[28:59]
    chunks, (g_ssem, g_rsem, g_lsem, g_vsem, psem, g_xsem, vsem, xsem) = refs[59:67], refs[67:75]
    p = Place(inner)
    len_p, len_q = forward_part(
        p, seq, lengths, targets, vector_shards, weights, query_tokens, passage_tokens, d_pool, loss, prob_hbm, vec, prob, prob_q,
        wa, wi, wo, x, q, k, v, act, act_t, slope, x_t, q_t, ctx_t, norm_t, y1, r1, y2, r2, y_sum, rows, packed, vectors, len_buf,
        g_ssem, g_rsem, g_lsem, g_vsem, psem, g_xsem)
    backward_part(
        p, len_p, len_q, d_pool, y_sum, vec, prob_hbm, prob, prob_q, dxq_out, dxp_out, dvec_out, grads,
        wa, wi, wo, x, k, v, act, act_t, slope, x_t, q_t, ctx_t, norm_t, y1, r1, y2, r2, ds_buf,
        d_vec, v_in, v_out, chunks, psem, vsem, xsem)


def layer_call(inner, seq, lengths, targets, vectors, weights, query_tokens, passage_tokens, cid=0):
    bf, f32 = jnp.bfloat16, jnp.float32
    sds, vmem, dma = jax.ShapeDtypeStruct, pltpu.VMEM, pltpu.SemaphoreType.DMA
    pairs = targets.shape[1]
    outs = [sds((8, 128), f32), sds((2, Q, 768), bf), sds((2, S, 768), bf), sds((16, 768), f32)]
    outs += [sds((48, 768), f32)] * 4 + [sds((48, 3072), f32), sds((192, 768), f32), sds((12, S, S), bf)]
    wide_rows, rows, turned, column = vmem((T, 768), f32), vmem((T, 768), bf), vmem((768, T), bf), vmem((T, 1), f32)
    scratch = [vmem((4, 4, 4, 48, 768), bf), vmem((4, 4, 48, 3072), bf), vmem((4, 4, 192, 768), bf)] + [rows] * 4
    scratch += [vmem((T, 3072), bf), vmem((3072, T), bf), vmem((T, 3072), bf)] + [turned] * 4 + [wide_rows, column] * 2
    scratch += [vmem((2, 2, S, S), bf), vmem((12, Q, Q), bf), vmem((2, S, S), bf), vmem((16, 3072), f32), vmem((2, 768), f32), vmem((2, 768), f32)]
    scratch += [vmem((pairs, 1, 1536), f32), vmem((16, 128), f32), vmem((4, 4, 16, 128), bf), vmem((2, 8, 128), f32)]
    scratch += [vmem((16, 768), f32), vmem((6, 16, 384), f32), vmem((3, 16, 384), f32)]
    scratch += [vmem((2, 4, 4, 48, 768), bf), vmem((4, 4, 4, 48, 384), bf), vmem((12, 4, 4, 48, 384), bf), vmem((12, 2, 4, 48, 384), bf)]
    scratch += [vmem((12, 4, 48, 384), bf), vmem((12, 3, 48, 384), bf), dma((12, 8)), dma((12, 8))]
    scratch += [dma((11, 12)), dma((11, 12)), dma((11,)), dma((2, 7)), dma((2,)), dma((6,)), dma((2, 7)), dma((6,))]
    return pl.pallas_call(
        functools.partial(layer_kernel, inner, seq),
        out_shape=outs,
        in_specs=[pl.BlockSpec(memory_space=pltpu.SMEM)] + [VM] * 10 + [ANY] * 8,
        out_specs=[VM, ANY, ANY] + [VM] * 7 + [ANY],
        scratch_shapes=scratch,
        compiler_params=pltpu.CompilerParams(collective_id=cid, has_side_effects=True, vmem_limit_bytes=63 << 20),
        name="layer",
    )(lengths, targets, *vectors, *weights, query_tokens, passage_tokens)


def outputs_kernel(inner, loss_in, dxq, dxp, d_vec, *refs):
    grads, (loss, q_out, p_out), g_outs, v_outs = refs[:6], refs[6:9], refs[9:15], refs[15:24]
    q_low, p_low, q_wide, p_wide, v_buf = refs[24:29]
    g_bufs, (isem, osem, gsem, vsem) = refs[29:35], refs[35:]
    parts = [(dxp.at[i, pl.ds(r, 256)], p_low.at[i, pl.ds(r, 256)], p_wide.at[i, pl.ds(r, 256)], p_out.at[i, pl.ds(r, 256)]) for i in range(2) for r in (0, 256)]
    parts.append((dxq, q_low, q_wide, q_out))
    loads = [pltpu.make_async_copy(part[0], part[1], isem.at[i]) for i, part in enumerate(parts)]
    v_load = pltpu.make_async_copy(d_vec, v_buf, vsem)
    g_loads = [pltpu.make_async_copy(src, buf, gsem.at[0, i]) for i, (src, buf) in enumerate(zip(grads, g_bufs))]
    g_stores = [pltpu.make_async_copy(buf, dst, gsem.at[1, i]) for i, (buf, dst) in enumerate(zip(g_bufs, g_outs))]
    for copy in loads + [v_load] + g_loads:
        copy.start()
    loss[...] = loss_in[0:1, 0:1]
    stores = []
    for i, (_, source, wider, out) in enumerate(parts):
        loads[i].wait()
        wider[...] = wide(source[...])
        stores.append(pltpu.make_async_copy(wider, out, osem.at[i]))
        stores[-1].start()
    for load, store in zip(g_loads, g_stores):
        load.wait()
        store.start()
    v_load.wait()
    shard = lax.axis_index("dp") // inner
    for size, first, outs in ((48, 0, v_outs[:8]), (192, 8, v_outs[8:])):
        at = lax.broadcasted_iota(jnp.int32, (768, 1), 0) - lax.rem(shard * size, 768)
        pick = jnp.where(at == lax.broadcasted_iota(jnp.int32, (1, size), 1), 1.0, 0.0)
        mine = jnp.dot(v_buf[first : first + 8], pick, precision=lax.Precision.HIGHEST, preferred_element_type=jnp.float32)
        if size == 48:
            for i in range(8):
                outs[i][...] = mine[i : i + 1]
        else:
            row = lax.broadcasted_iota(jnp.int32, (8, 1), 0)
            outs[0][...] = jnp.sum(jnp.where(row == shard // 4, mine, 0.0), axis=0, keepdims=True)
    for copy in stores + g_stores:
        copy.wait()


def outputs_call(inner, loss, dxq, dxp, d_vec, grads):
    sds, f32, vmem, dma = jax.ShapeDtypeStruct, jnp.float32, pltpu.VMEM, pltpu.SemaphoreType.DMA
    outs = [sds((1, 1), f32), sds(dxq.shape, f32), sds(dxp.shape, f32)] + [sds(g.shape, f32) for g in grads]
    outs += [sds((1, 48), f32)] * 8 + [sds((1, 192), f32)]
    scratch = [vmem(dxq.shape, dxq.dtype), vmem(dxp.shape, dxp.dtype), vmem(dxq.shape, f32), vmem(dxp.shape, f32), vmem(d_vec.shape, f32)]
    scratch += [vmem(g.shape, f32) for g in grads] + [dma((5,)), dma((5,)), dma((2, 6)), dma]
    return pl.pallas_call(
        functools.partial(outputs_kernel, inner),
        out_shape=outs,
        in_specs=[VM] + [ANY] * 9,
        out_specs=[VM] + [ANY] * 8 + [VM] * 9,
        scratch_shapes=scratch,
        compiler_params=pltpu.CompilerParams(vmem_limit_bytes=62 << 20),
        name="write_outputs",
    )(loss, dxq, dxp, d_vec, *grads)


def per_device(
    query_tokens, passage_tokens, lengths, positives,
    query_weight, key_weight, value_weight, output_weight, inner_weight, outer_weight,
    query_bias, value_bias, output_bias, inner_bias, outer_bias,
    first_gain, first_shift, second_gain, second_shift,
):
    inner = lax.axis_size("dp") // 16
    groups = None if inner == 1 else [[h * inner + i for i in range(inner)] for h in range(16)]
    seq = passage_tokens.shape[1]

    def fetch(w):
        if groups is None:
            return w
        return lax.all_gather(w, "dp", axis=0, tiled=True, axis_index_groups=groups)

    weights = [fetch(w) for w in (query_weight, key_weight, value_weight, output_weight, inner_weight, outer_weight)]
    vectors = (query_bias, value_bias, output_bias, outer_bias, first_gain, first_shift, second_gain, second_shift, inner_bias)
    vectors = [fetch(w)[None] for w in vectors[:8]] + [fetch(inner_bias)]
    loss, dxq, dxp, d_vec, *grads, _ = layer_call(
        inner, float(seq), lengths, positives[None], vectors, weights, query_tokens, passage_tokens)
    loss, dxq, dxp, *grads = outputs_call(inner, loss, dxq, dxp, d_vec, grads)
    grads = [g.reshape(-1) if g.shape[0] == 1 else g for g in grads]

    def finish(x):
        if groups is None:
            return x
        return lax.psum_scatter(x, "dp", scatter_dimension=0, tiled=True, axis_index_groups=groups)

    grads = [finish(g) for g in grads]
    flat = grads[6:]
    return (loss[0, 0], dxq, dxp, *grads[:6], flat[0], flat[1], flat[2], flat[8], *flat[3:8])


def solution(mesh):
    rows3, rows2, rows1 = P("dp", None, None), P("dp", None), P("dp")
    return jax.shard_map(
        per_device,
        mesh=mesh,
        in_specs=(rows3, rows3, P("tower", "dp"), P()) + (rows2,) * 6 + (rows1,) * 9,
        out_specs=(P(), rows3, rows3) + (rows2,) * 6 + (rows1,) * 9,
        check_vma=False,
    )
```

```python
import functools

import jax
import jax.numpy as jnp
from jax import lax
from jax.experimental import pallas as pl
from jax.experimental.pallas import tpu as pltpu
from jax.sharding import PartitionSpec as P

MESH = pl.DeviceIdType.MESH
ANY = pl.BlockSpec(memory_space=pl.ANY)
VM = pl.BlockSpec(memory_space=pltpu.VMEM)


class Place:
    def __init__(self, inner):
        dp = lax.axis_index("dp")
        self.c = lax.axis_index("tower")
        self.inner = inner
        self.low = lax.rem(dp, inner)
        self.me = dp // inner
        self.z = self.me // 4
        self.quad = lax.rem(self.me, 4)
        s1 = 1 + self.c
        s2 = 2 - self.c
        b1 = lax.rem(self.quad // s1, 2)
        b2 = lax.rem(self.quad // s2, 2)
        self.q1 = self.quad + s1 * (1 - 2 * b1)
        self.q2 = self.quad + s2 * (1 - 2 * b2)
        self.q12 = 3 - self.quad
        self.quads = (self.quad, self.q1, self.q2, self.q12)

    def ring(self, k):
        return lax.rem(self.z + k, 4)

    def dev(self, group):
        return {"dp": group * self.inner + self.low, "tower": self.c}

    def n1(self):
        return self.dev(self.z * 4 + self.q1)

    def n2(self):
        return self.dev(self.z * 4 + self.q2)

    def up(self, k):
        return self.dev(self.ring(k) * 4 + self.quad)

    def sib(self):
        return {"dp": self.me * self.inner + self.low, "tower": 1 - self.c}

    def across(self, k):
        return {"dp": (self.ring(k) * 4 + self.quad) * self.inner + self.low, "tower": 1 - self.c}

    def greet(self):
        for target in (self.up(1), self.up(2), self.up(3), self.n1(), self.n2(), self.sib()):
            pl.semaphore_signal(pltpu.get_barrier_semaphore(), inc=1, device_id=target, device_id_type=MESH)

    def met(self):
        pl.semaphore_wait(pltpu.get_barrier_semaphore(), 6)


def remote(src, dst, send_sem, recv_sem, target):
    return pltpu.make_async_remote_copy(
        src_ref=src, dst_ref=dst, send_sem=send_sem, recv_sem=recv_sem, device_id=target, device_id_type=MESH
    )


S, Q = 512, 64
T = S + Q


def dot(left, right):
    return jnp.dot(left, right, preferred_element_type=jnp.float32)


def dot_nt(left, right):
    return lax.dot_general(left, right, (((1,), (1,)), ((), ())), preferred_element_type=jnp.float32)


def block(index, size):
    return pl.ds(pl.multiple_of(index * size, size), size)


def low(x):
    return x.astype(jnp.bfloat16)


def wide(x):
    return x.astype(jnp.float32)


def head_mask(h):
    lane = lax.broadcasted_iota(jnp.int32, (1, 128), 1)
    return low(jnp.where(lane // 64 == h, 1.0, 0.0))


SPANS = ((0, S, 256), (S, Q, Q))


class Gather:
    last = 10

    def __init__(self, p, shards, wa, wi, wo, ssem, rsem, lsem):
        self.p, self.shards, self.wa, self.wi, self.wo = p, shards, wa, wi, wo
        self.ssem, self.rsem, self.lsem = ssem, rsem, lsem

    def cols(self, t, which):
        if t < 8:
            return pl.ds(pl.multiple_of(which * 384 if t < 4 else (t - 4) * 768 + which * 384, 128), 384)
        return pl.ds(pl.multiple_of(which * 384 + (t - 8) * 128, 128), 128)

    def shard(self, t):
        ref = self.shards[(1, 0, 2, 3)[t]] if t < 4 else self.shards[4 if t < 8 else 5]
        return ref.at[:, self.cols(t, self.p.c)]

    def whole(self, t):
        return self.wa.at[(1, 0, 2, 3)[t]] if t < 4 else self.wi if t < 8 else self.wo

    def one(self, t, z, q):
        return self.whole(t).at[z, q, :, self.cols(t, self.p.c)]

    def four(self, t, q, which):
        return self.whole(t).at[:, q, :, self.cols(t, which)]

    def plane(self, t, z, which):
        return self.whole(t).at[z, :, :, self.cols(t, which)]

    def copy(self, src, dst, t, k, target):
        return remote(src, dst, self.ssem.at[t, k], self.rsem.at[t, k], target)

    def recv(self, t, k, ref):
        self.copy(ref, ref, t, k, self.p.sib()).wait_recv()

    def push(self, view, t, k, target):
        self.copy(view, view, t, k, target).start()

    def local(self, t):
        return pltpu.make_async_copy(self.shard(t), self.one(t, self.p.z, self.p.quad), self.lsem.at[t])

    def stage_own(self, t):
        p = self.p
        self.local(t).start()
        mine = self.one(t, p.z, p.quad)
        for k in range(1, 4) if t < self.last else ():
            self.copy(self.shard(t), mine, t, k, p.up(k)).start()
        self.copy(self.shard(t), mine, t, 4, p.n1()).start()
        self.copy(self.shard(t), mine, t, 5, p.n2()).start()

    def stage_z(self, t):
        p = self.p
        for k in range(1, 4):
            view = self.one(t, p.ring(4 - k), p.quad)
            self.recv(t, k, view)
            self.push(view, t, 4, p.n1())
            self.push(view, t, 5, p.n2())
        self.local(t).wait()
        self.push(self.four(t, p.quad, p.c), t, 8, p.sib())

    def stage_one(self, t):
        p = self.p
        view = self.four(t, p.q1, p.c)
        self.recv(t, 4, view)
        self.push(view, t, 6, p.n2())
        self.push(view, t, 9, p.sib())

    def stage_two(self, t):
        p = self.p
        for k, q in ((5, p.q2), (6, p.q12)):
            view = self.four(t, q, p.c)
            self.recv(t, k, view)
            self.push(view, t, k + 5, p.sib())

    def stage_sib(self, t):
        p = self.p
        for k, q in ((8, p.quad), (9, p.q2), (10, p.q1), (11, p.q12)):
            self.recv(t, k, self.four(t, q, 1 - p.c))

    def last_one(self):
        p, t = self.p, self.last
        view = self.one(t, p.z, p.q1)
        self.recv(t, 4, view)
        self.push(view, t, 6, p.n2())

    def last_two(self):
        p, t = self.p, self.last
        self.recv(t, 5, self.one(t, p.z, p.q2))
        self.recv(t, 6, self.one(t, p.z, p.q12))
        self.local(t).wait()
        view = self.plane(t, p.z, p.c)
        for k in range(1, 4):
            self.push(view, t, k, p.up(k))
        self.push(view, t, 8, p.sib())

    def last_z(self):
        p, t = self.p, self.last
        for k in range(1, 4):
            view = self.plane(t, p.ring(4 - k), p.c)
            self.recv(t, k, view)
            self.push(view, t, 8 + k, p.sib())

    def last_sib(self):
        p, t = self.p, self.last
        for k in range(4):
            self.recv(t, 8 + k, self.plane(t, p.ring(4 - k), 1 - p.c))

    def tick(self, i):
        for lag, stage in ((0, self.stage_z), (-AHEAD, self.stage_own), (LAGS[0], self.stage_one), (LAGS[1], self.stage_two), (LAGS[2], self.stage_sib)):
            if 0 <= i - lag < self.last:
                stage(i - lag)
        for at, stage in zip(LATE, (lambda: self.stage_own(self.last), self.last_one, self.last_two, self.last_z, self.last_sib)):
            if i == at:
                stage()

    def finish(self):
        p = self.p
        for t in range(self.last + 1):
            single, four, plane = self.one(t, p.z, p.quad), self.four(t, p.quad, p.c), self.plane(t, p.z, p.c)
            for k in (1, 2, 3, 4, 5, 6, 8, 9, 10, 11):
                view = (single if k < 4 else four) if t < self.last else (single if 4 <= k < 8 else plane)
                self.copy(view, view, t, k, p.sib()).wait_send()


def expand_vectors(shards, vec):
    at = wide(lax.broadcasted_iota(jnp.int32, (1, 768), 1))
    owner = jnp.floor((at + 0.5) * (1.0 / 48))
    lane = wide(lax.broadcasted_iota(jnp.int32, (128, 1), 0))
    rows = dot(shards.reshape(256, 128), low(jnp.where(lane == at - owner * 48, 1.0, 0.0))).reshape(16, 16, 768)
    shard = wide(lax.broadcasted_iota(jnp.int32, (16, 1, 1), 0))
    vec[:8, :768] = jnp.sum(jnp.where(owner[None] == shard, rows[:, :8], 0.0), axis=0)
    piece = wide(lax.broadcasted_iota(jnp.int32, (4, 4, 1), 0) * 4 + lax.broadcasted_iota(jnp.int32, (4, 4, 1), 1))
    for n in range(4):
        mine = jnp.sum(jnp.where(owner[None] == piece, rows[4 * n : 4 * n + 4, 8:12], 0.0), axis=0)
        vec[8:9, n * 768 : (n + 1) * 768] = jnp.sum(mine, axis=0, keepdims=True)


AHEAD = 4
LAGS = (1, 3, 4)
LATE = (0, 1, 5, 9, 13)


ALONG_Z = (0,)


class Scatter:
    def __init__(self, p, refs, result):
        self.p = p
        self.stage, self.r0, self.acc, self.r1, self.r2, self.r3, self.ssem, self.rsem = refs
        self.result = result
        self.own = pl.ds(pl.multiple_of(p.c * 384, 128), 384)
        self.other = pl.ds(pl.multiple_of((1 - p.c) * 384, 128), 384)

    def copy(self, src, dst, e, k, target):
        return remote(src, dst, self.ssem.at[e, k], self.rsem.at[e, k], target)

    def recv(self, e, k, ref):
        self.copy(ref, ref, e, k, self.p.sib()).wait_recv()

    def emit(self, e, left, right, extra=None):
        if e >= 2:
            self.shared(e - 2).wait_send()

        @pl.loop(0, 3)
        def _(n):
            cols = block(n, 256)
            values = right(cols)
            self.stage[e % 2, :, :, :, cols] = low(dot(left(), values)).reshape(4, 4, 48, 256)
            if extra is not None:
                extra(cols, values)
        self.shared(e).start()

    def shared(self, e):
        return self.copy(self.stage.at[e % 2, :, :, :, self.other], self.r0.at[e % 4], e, 0, self.p.sib())

    def stage0(self, e):
        p, acc = self.p, self.acc
        self.recv(e, 0, self.r0.at[e % 4])
        if e in ALONG_Z:
            for k in (1, 2, 3, 0):
                z = p.ring(k)
                acc[e, z] = self.stage[e % 2, z, :, :, self.own] + self.r0[e % 4, z]
                if k:
                    self.copy(acc.at[e, z], self.plane(e, k), e, k, p.up(k)).start()
            return
        for j, q in enumerate((p.q2, p.q12, p.q1, p.quad)):
            acc[e, :, q] = self.stage[e % 2, :, q, :, self.own] + self.r0[e % 4, :, q]
            if j < 2:
                self.copy(acc.at[e, :, q], self.r1.at[e, j], e, 1 + j, p.n2()).start()

    def plane(self, e, k):
        return self.r2.at[e] if k == 3 else self.r1.at[e, k - 1]

    def stage1(self, e):
        p, acc = self.p, self.acc
        if e in ALONG_Z:
            total = wide(acc[e, p.z])
            for k in range(1, 4):
                self.recv(e, k, self.plane(e, k))
                total = total + wide(self.plane(e, k)[...])
            acc[e, p.z] = low(total)
            for j, q in enumerate((p.q2, p.q12)):
                self.copy(acc.at[e, p.z, q], self.r3.at[e, j], e, 4 + j, p.n2()).start()
            return
        self.recv(e, 2, self.r1.at[e, 1])
        acc[e, :, p.q1] += self.r1[e, 1]
        self.copy(acc.at[e, :, p.q1], self.r2.at[e], e, 3, p.n1()).start()
        self.recv(e, 1, self.r1.at[e, 0])
        acc[e, :, p.quad] += self.r1[e, 0]

    def stage2(self, e):
        p, acc = self.p, self.acc
        if e in ALONG_Z:
            self.recv(e, 5, self.r3.at[e, 1])
            acc[e, p.z, p.q1] += self.r3[e, 1]
            self.copy(acc.at[e, p.z, p.q1], self.r3.at[e, 2], e, 6, p.n1()).start()
            self.recv(e, 4, self.r3.at[e, 0])
            return
        self.recv(e, 3, self.r2.at[e])
        acc[e, :, p.quad] += self.r2[e]
        for k in range(1, 4):
            self.copy(acc.at[e, p.ring(k), p.quad], self.r3.at[e, k - 1], e, 3 + k, p.up(k)).start()

    def stage3(self, e):
        p = self.p
        if e in ALONG_Z:
            self.recv(e, 6, self.r3.at[e, 2])
            total = wide(self.acc[e, p.z, p.quad]) + wide(self.r3[e, 0]) + wide(self.r3[e, 2])
        else:
            total = wide(self.acc[e, p.z, p.quad])
            for k in range(1, 4):
                self.recv(e, 3 + k, self.r3.at[e, k - 1])
                total = total + wide(self.r3[e, k - 1])
        view = self.result(e, p.c)
        view[...] = total
        self.copy(view, view, e, 7, p.sib()).start()

    def finish(self, count):
        for e in range(count):
            self.recv(e, 7, self.result(e, 1 - self.p.c))
            self.copy(self.result(e, self.p.c), self.result(e, self.p.c), e, 7, self.p.sib()).wait_send()
        for e in range(count - 2, count):
            self.shared(e).wait_send()
        four, one = self.r2.at[0], self.r3.at[0, 0]

        @pl.loop(0, count)
        def _(e):
            for k in range(1, 7):
                view = four if k < 4 else one
                self.copy(view, view, e, k, self.p.sib()).wait_send()


def forward_part(p, seq, lengths, targets, vector_shards, weights, query_tokens, passage_tokens, d_pool, loss, prob_out, vec, prob, prob_q,
                 wa, wi, wo, x, q, k, v, act, act_t, slope, x_t, q_t, ctx_t, norm_t, y1, r1, y2, r2, y_sum, rows, packed, vectors, len_buf,
                 ssem, rsem, lsem, vsem, psem, xsem):
    normed = q
    pairs = targets.shape[1]
    me = lax.axis_index("dp") * 2 + p.c

    def device(at):
        return {"dp": at // 2, "tower": lax.rem(at, 2)}

    x_loads = [pltpu.make_async_copy(passage_tokens.at[p.c], x.at[pl.ds(0, S)], xsem.at[0]), pltpu.make_async_copy(query_tokens.at[p.c], x.at[pl.ds(S, Q)], xsem.at[1])]
    for copy in x_loads:
        copy.start()
    barrier = pltpu.get_barrier_semaphore()

    @pl.loop(1, pairs)
    def _(i):
        pl.semaphore_signal(barrier, inc=1, device_id=device(lax.rem(me + i, pairs)), device_id_type=MESH)
    lane = lax.broadcasted_iota(jnp.int32, (8, 128), 1)
    len_buf[p.c] = jnp.where(lane == 0, lengths[0, 0].astype(jnp.float32), lengths[0, 1].astype(jnp.float32))
    packed[...] = jnp.zeros((16, 128), jnp.float32)
    for i, ref in enumerate(vector_shards[:8]):
        packed[i : i + 1, :48] = wide(ref[...])
    last = wide(vector_shards[8][...]).reshape(1, 192)
    for i in range(4):
        packed[8 + i : 9 + i, :48] = last[:, i * 48 : i * 48 + 48]
    vectors[p.z, p.quad] = low(packed[...])
    pl.semaphore_wait(barrier, pairs - 1)

    gather = Gather(p, weights, wa, wi, wo, ssem, rsem, lsem)
    len_copy = remote(len_buf.at[p.c], len_buf.at[p.c], xsem.at[2], xsem.at[3], p.sib())
    len_copy.start()

    def vector(i, q, target):
        view = vectors.at[p.z, p.quad] if i < 4 else vectors.at[:, q]
        return remote(view, view, vsem.at[0, i], vsem.at[1, i], target)

    for i in range(1, 4):
        vector(i, None, p.up(i)).start()
    for t in range(AHEAD):
        gather.stage_own(t)
    gather.tick(0)
    for i in range(1, 4):
        view = vectors.at[p.ring(4 - i), p.quad]
        remote(view, view, vsem.at[0, i], vsem.at[1, i], p.sib()).wait_recv()
    vector(4, p.quad, p.n1()).start()
    vector(5, p.quad, p.n2()).start()
    gather.tick(1)
    for copy in x_loads:
        copy.wait()
    gather.tick(2)
    vector(4, p.q1, p.sib()).wait_recv()
    vector(6, p.q1, p.n2()).start()
    for i in range(3, LAGS[2] + 1):
        gather.tick(i)
    remote(len_buf.at[1 - p.c], len_buf.at[1 - p.c], xsem.at[2], xsem.at[3], p.sib()).wait_recv()
    len_q, len_p = [jnp.sum(jnp.where(lane[:1] == p.c, len_buf[i, 0:1], 0.0), axis=1, keepdims=True) for i in range(2)]

    def project(m, out, row):
        @pl.loop(0, 3)
        def _(n):
            cols = block(n, 256)
            acc = dot(x[...], wa[m, :, :, :, cols].reshape(768, 256))
            if row is not None:
                acc = acc + vec[row : row + 1, cols]
            out[:, cols] = low(acc)

    def store_prob(j):
        return pltpu.make_async_copy(prob.at[lax.rem(j, 2)], prob_out.at[pl.ds(j * 2, 2)], psem.at[lax.rem(j, 2)])

    def attention(low_j, high_j):
        @pl.loop(low_j, high_j)
        def _(j):
            cols = block(j, 128)
            slot = lax.rem(j, 2)

            @pl.when(j >= 2)
            def _():
                store_prob(j - 2).wait()

            for (start, size, rb), length in zip(SPANS, (len_p, len_q)):
                span = slice(start, start + size)
                kp, vp = k[span, cols], v[span, cols]
                valid = wide(lax.broadcasted_iota(jnp.int32, (1, size), 1)) < length
                for r in range(0, size, rb):
                    qp = q[start + r : start + r + rb, cols]
                    total = None
                    for h in range(2):
                        mask = head_mask(h)
                        scores = dot_nt(qp * (mask * 0.125), kp)
                        scores = jnp.where(valid, scores, -1e9)
                        e = jnp.exp(scores - jnp.max(scores, axis=1, keepdims=True))
                        w = low(e * (1.0 / jnp.sum(e, axis=1, keepdims=True)))
                        if size == S:
                            prob[slot, h, r : r + rb] = w
                        else:
                            prob_q[2 * j + h] = w
                        piece = dot(w, vp * mask)
                        total = piece if total is None else total + piece
                    act[start + r : start + r + rb, cols] = low(total)
            store_prob(j).start()

    project(1, k, None)
    gather.tick(LAGS[2] + 1)
    vector(5, p.q2, p.sib()).wait_recv()
    vector(6, p.q12, p.sib()).wait_recv()
    expand_vectors(vectors[...], vec)
    project(0, q, 0)
    q_t[...] = q[...].T
    def gain(row):
        return vec[row : row + 1, :768]

    def attended():
        ctx_t[...] = act[:, :768].T
        pl.loop(0, 3)(first_norm)

    def first_norm(n):
        span = block(n, 192)
        first = wide(x[span]) + (dot(act[span, :768], wa[3].reshape(768, 768)) + gain(2))
        center = first - jnp.mean(first, axis=1, keepdims=True)
        scale = lax.rsqrt(jnp.mean(center * center, axis=1, keepdims=True) + 1e-12)
        y = center * scale
        y1[span] = y
        r1[span] = scale
        normed[span] = low(y * gain(4) + gain(5))

    def hidden(low_n, high_n):
        @pl.loop(low_n, high_n)
        def _(n):
            cols = block(n, 256)
            u = dot(normed[...], wi[:, :, :, cols].reshape(768, 256)) + vec[8:9, cols]
            cdf = 0.5 * (1.0 + lax.erf(u * 0.7071067811865476))
            act[:, cols] = low(u * cdf)
            slope[:, cols] = low(cdf + u * (0.3989422804014327 * jnp.exp(-0.5 * u * u)))

    gather.tick(LAGS[2] + 2)
    project(2, v, 1)
    attention(0, 2)
    gather.tick(LAGS[2] + 3)
    attention(2, 4)
    gather.tick(LAGS[2] + 4)
    attention(4, 6)
    attended()
    gather.tick(LAGS[2] + 5)
    hidden(0, 6)
    gather.tick(LAGS[2] + 6)
    hidden(6, 9)
    gather.tick(LAGS[2] + 7)
    hidden(9, 12)
    y_sum[...] = jnp.zeros_like(y_sum)

    def outer(i):
        cols = [slice(which * 384 + i * 128, which * 384 + i * 128 + 128) for which in range(2)]
        right = jnp.concatenate([wo[:, :, :, c].reshape(3072, 128) for c in cols], axis=1)
        add = dot(act[...], right)
        for which, c in enumerate(cols):
            y2[:, c] = add[:, which * 128 : which * 128 + 128] + (y1[:, c] * vec[4:5, c] + vec[5:6, c] + vec[3:4, c])

    for i in range(3):
        gather.tick(LAGS[2] + 8 + i)
        outer(i)

    @pl.loop(0, 3)
    def _(n):
        span = block(n, 192)
        second = y2[span]
        center = second - jnp.mean(second, axis=1, keepdims=True)
        scale = lax.rsqrt(jnp.mean(center * center, axis=1, keepdims=True) + 1e-12)
        y = center * scale
        y2[span] = y
        r2[span] = scale
        at = wide(lax.broadcasted_iota(jnp.int32, (192, 1), 0) + n * 192)
        for row, keep in ((0, (at >= S) & (at - S < len_q)), (1, (at < S) & (at < len_p))):
            y_sum[row : row + 1] += jnp.sum(jnp.where(keep, y, 0.0), axis=0, keepdims=True)

    def turn_act():
        for b in range(4):
            turned = act[:, b * 768 : (b + 1) * 768].T
            for s in range(4):
                for n in range(4):
                    row = n * 768 + (b * 4 + s) * 48
                    act_t[row : row + 48] = turned[s * 192 + n * 48 : s * 192 + n * 48 + 48]

    mine = jnp.concatenate([y_sum[0:1] / len_q, y_sum[1:2] / len_p]) * gain(6) + gain(7)
    root = jnp.sqrt(jnp.sum(mine * mine, axis=1, keepdims=True) + 1e-6)
    unit = mine / root
    rows[me, :, :768] = unit[0:1]
    rows[me, :, 768:] = unit[1:2]

    for first, end in ((pairs // 4, pairs), (1, pairs // 4)):

        @pl.loop(first, end)
        def _(i):
            remote(rows.at[me], rows.at[me], xsem.at[4], xsem.at[5], device(lax.rem(me + i, pairs))).start()
    turn_act()
    norm_t[...] = normed[...].T
    x_t[...] = x[...].T
    len_copy.wait_send()
    for i in range(1, 7):
        vector(i, p.quad, p.sib()).wait_send()
    store_prob(4).wait()
    store_prob(5).wait()
    rest = rows.at[pl.ds(0, pairs - 1)]
    remote(rest, rest, xsem.at[4], xsem.at[5], p.sib()).wait_recv()
    step = 768 if pairs <= 64 else 128
    logits = None
    for at in range(0, 768, step):
        part = lax.dot_general(
            rows[:, 0, 768 + at : 768 + at + step], rows[:, 0, at : at + step], (((1,), (1,)), ((), ())),
            precision=lax.Precision.HIGHEST, preferred_element_type=jnp.float32)
        logits = part if logits is None else logits + part
    logits = logits / 0.01
    hit = targets[...] == lax.broadcasted_iota(jnp.int32, (pairs, pairs), 0)
    top = jnp.max(logits, axis=0, keepdims=True)
    lse = jnp.log(jnp.sum(jnp.exp(logits - top), axis=0, keepdims=True)) + top
    picked = jnp.sum(jnp.where(hit, logits, 0.0), axis=0, keepdims=True)
    loss[...] = jnp.broadcast_to(jnp.sum(lse - picked, axis=1, keepdims=True) / pairs, loss.shape)
    d_logits = seq * (jnp.exp(logits - lse) - jnp.where(hit, 1.0, 0.0))
    across = lax.broadcasted_iota(jnp.int32, (pairs, pairs), 1)
    down = lax.broadcasted_iota(jnp.int32, (pairs, pairs), 0)
    for_q = jnp.sum(jnp.where(across == me, d_logits, 0.0), axis=1, keepdims=True)
    for_p = jnp.sum(jnp.where(down == me, d_logits, 0.0), axis=0, keepdims=True)
    for_p = jnp.sum(jnp.where(across == down, for_p, 0.0), axis=1, keepdims=True)
    for row, weight in enumerate((for_q, for_p)):
        d_unit = jnp.sum(weight * rows[:, 0, (1 - row) * 768 : (2 - row) * 768], axis=0, keepdims=True) / 0.01
        u = unit[row : row + 1]
        d_pool[row : row + 1] = (d_unit - u * jnp.sum(u * d_unit, axis=1, keepdims=True)) / root[row : row + 1]
    remote(rest, rest, xsem.at[4], xsem.at[5], p.sib()).wait_send()
    return len_p, len_q, gather.finish


def backward_part(p, settle, len_p, len_q, d_pool, y_sum, vec, prob_hbm, prob, prob_q, dxq_out, dxp_out, dvec_out, grads,
                  wa, wi, wo, d_low, k, v, d_inner, act_t, slope, x_t, q_t, ctx_t, norm_t, y1, r1, d_second, r2, ds_buf,
                  d_vec, v_in, v_out, chunks, psem, vsem, xsem):
    g_query, g_key, g_value, g_output, g_inner, g_outer = grads

    def load_prob(j):
        return pltpu.make_async_copy(prob_hbm.at[pl.ds(j * 2, 2)], prob.at[lax.rem(j, 2)], psem.at[lax.rem(j, 2)])

    load_prob(0).start()
    load_prob(1).start()

    def result(e, which):
        cols = pl.ds(pl.multiple_of(which * 384, 128), 384)
        if e < 4:
            return g_outer.at[pl.ds(e * 48, 48), cols]
        if e < 8:
            return g_inner.at[:, pl.ds(pl.multiple_of((e - 4) * 768 + which * 384, 128), 384)]
        return (g_output, g_query, g_key, g_value)[e - 8].at[:, cols]

    sc = Scatter(p, chunks, result)
    d_vec[...] = jnp.zeros_like(d_vec)

    def gain(row):
        return vec[row : row + 1, :768]

    def tally(row, value):
        d_vec[row : row + 1] += jnp.sum(value, axis=0, keepdims=True)

    pool_q = d_pool[0:1] / len_q
    pool_p = d_pool[1:2] / len_p

    def norm_back(d, row, yy, scale, rows):
        g = d * gain(row)
        d = (g - jnp.mean(g, axis=1, keepdims=True) - yy * jnp.mean(g * yy, axis=1, keepdims=True)) * scale
        d_second[rows] = d
        d_low[rows] = low(d)
        return d


    @pl.loop(0, 3)
    def _(n):
        rows = block(n, 192)
        at = wide(lax.broadcasted_iota(jnp.int32, (192, 1), 0) + n * 192)
        d_rows = jnp.where(at < S, jnp.where(at < len_p, pool_p, 0.0), jnp.where(at - S < len_q, pool_q, 0.0))
        norm_back(d_rows, 6, d_second[rows], r2[rows], rows)


    def emit_outer(n):
        def bias(cols, values):
            d_vec[3:4, cols] = jnp.sum(wide(values), axis=0, keepdims=True)
        sc.emit(n, lambda: act_t[n * 768 : (n + 1) * 768], lambda cols: d_low[:, cols], bias if n == 3 else None)

    def emit_inner(n):
        def bias(cols, values):
            d_vec[8 + n : 9 + n, cols] = jnp.sum(wide(values), axis=0, keepdims=True)
        sc.emit(4 + n, lambda: norm_t[...], lambda cols: d_inner[:, pl.ds(pl.multiple_of(n * 768 + cols.start, 256), 256)], bias)

    emit_outer(0)
    d_vec[6:7] = pool_q * y_sum[0:1] + pool_p * y_sum[1:2]
    d_vec[7:8] = d_pool[0:1] + d_pool[1:2]
    emit_outer(1)
    sc.stage0(0)
    emit_outer(2)
    sc.stage0(1)
    emit_outer(3)
    sc.stage0(2)

    def inner_back(low_n, high_n):
        @pl.loop(low_n, high_n)
        def _(n):
            cols = block(n, 768)
            d_inner[:, cols] = low(dot_nt(d_low[...], wo[n].reshape(768, 768)) * wide(slope[:, cols]))

    inner_back(0, 2)
    sc.stage0(3)
    inner_back(2, 4)
    emit_inner(0)
    sc.stage1(1)
    emit_inner(1)
    sc.stage0(4)
    emit_inner(2)
    sc.stage0(5)
    emit_inner(3)
    sc.stage0(6)
    sc.stage1(2)
    sc.stage2(1)

    def first_back(low_n, high_n):
        @pl.loop(low_n, high_n)
        def _(n):
            rows = block(n, 192)
            y = y1[rows]
            d = d_second[rows] + dot_nt(d_inner[rows], wi[...].reshape(768, 3072))
            tally(4, d * y)
            tally(5, d)
            d = norm_back(d, 4, y, r1[rows], rows)
            tally(2, wide(low(d)))

    first_back(0, 1)
    sc.stage0(7)
    first_back(1, 3)
    sc.stage1(3)
    sc.stage1(0)
    sc.stage2(2)
    sc.emit(8, lambda: ctx_t[...], lambda cols: d_low[:, cols])

    def part(i):
        return pl.ds(i * 768, 768)

    def pair_cols(i, j):
        return pl.ds(pl.multiple_of(i * 768 + j * 128, 128), 128)

    def head_rows(i, head):
        return pl.ds(pl.multiple_of(i * 768 + head * 64, 64), 64)

    @pl.loop(0, 3)
    def _(n):
        rows = block(n, 192)
        d_inner[rows, part(3)] = low(dot_nt(d_low[rows], wa[3].reshape(768, 768)))
    act_t[part(2)] = d_inner[:, part(3)].T
    sc.stage0(8)

    def attention(low_j, high_j):
        @pl.loop(low_j, high_j)
        def _(j):
            load_prob(j).wait()
            slot = lax.rem(j, 2)
            cols = block(j, 128)
            for start, size, rb in SPANS:
                rows = slice(start, start + size)
                kp, vp = k[rows, cols], v[rows, cols]
                dq_parts = [None] * (size // rb)
                for h in range(2):
                    probs = (lambda sl: prob[slot, h, sl]) if size == S else (lambda sl: prob_q[2 * j + h, sl])
                    mask = head_mask(h)
                    for r in range(0, size, rb):
                        d_p = dot_nt(d_inner[start + r : start + r + rb, pair_cols(3, j)] * mask, vp)
                        w = wide(probs(slice(r, r + rb)))
                        ds = low(w * (d_p - jnp.sum(w * d_p, axis=1, keepdims=True)))
                        ds_buf[h, r : r + rb, :size] = ds
                        piece = dot(ds, kp * mask)
                        i = r // rb
                        dq_parts[i] = piece if dq_parts[i] is None else dq_parts[i] + piece
                    head = 2 * j + h
                    act_t[head_rows(1, head), rows] = low(dot(act_t[head_rows(2, head), rows], probs(slice(0, size))))
                    act_t[head_rows(0, head), rows] = low(dot(q_t[head_rows(0, head), rows], ds_buf[h, :size, :size]) * 0.125)
                for i, piece in enumerate(dq_parts):
                    d_inner[start + i * rb : start + (i + 1) * rb, pair_cols(0, j)] = low(piece * 0.125)

            @pl.when(j < 4)
            def _():
                load_prob(j + 2).start()

    attention(0, 2)
    sc.stage1(4)
    sc.stage2(3)
    sc.stage3(1)
    attention(2, 6)
    sc.stage1(5)
    sc.stage2(4)
    sc.stage2(0)
    sc.stage3(2)
    d_inner[:, part(1)] = act_t[part(0)].T
    d_inner[:, part(2)] = act_t[part(1)].T

    def emit_first(n):
        row = (0, None, 1)[n]

        def bias(cols, values):
            d_vec[row : row + 1, cols] = jnp.sum(wide(values), axis=0, keepdims=True)
        sc.emit(9 + n, lambda: x_t[...], lambda cols: d_inner[:, pl.ds(pl.multiple_of(n * 768 + cols.start, 256), 256)], None if row is None else bias)

    emit_first(0)
    emit_first(1)
    sc.stage0(9)
    emit_first(2)
    sc.stage0(10)

    def vector(i, src, target):
        return remote(src, v_in.at[i], vsem.at[0, i], vsem.at[1, i], target)

    def vector_recv(i):
        vector(i, v_in.at[i], p.sib()).wait_recv()
        return v_in[i]

    vector(0, d_vec.at[:, sc.other], p.sib()).start()
    sc.stage1(6)
    sc.stage2(5)
    sc.stage3(3)
    sc.stage3(0)
    sc.stage0(11)

    @pl.loop(0, 3)
    def _(n):
        rows = block(n, 192)
        d = d_second[rows]
        for i in range(3):
            d = d + dot_nt(d_inner[rows, part(i)], wa[i].reshape(768, 768))
        d_low[rows] = low(d)
    tokens = [(d_low.at[pl.ds(0, S)], dxp_out), (d_low.at[pl.ds(S, Q)], dxq_out)]
    mine = [pltpu.make_async_copy(src, out.at[p.c], xsem.at[i]) for i, (src, out) in enumerate(tokens)]
    theirs = [remote(src, out.at[p.c], xsem.at[2 + i], xsem.at[4 + i], p.sib()) for i, (src, out) in enumerate(tokens)]
    for copy in mine + theirs:
        copy.start()
    v_out[0] = d_vec[:, sc.own] + vector_recv(0)
    vector(1, v_out.at[0], p.n2()).start()
    settle()
    sc.stage1(7)
    sc.stage2(6)
    sc.stage3(4)
    sc.stage1(8)
    sc.stage2(7)
    sc.stage3(5)
    sc.stage1(9)
    sc.stage2(8)
    sc.stage3(6)
    sc.stage1(10)
    v_out[1] = v_out[0] + vector_recv(1)
    vector(2, v_out.at[1], p.n1()).start()
    sc.stage2(9)
    sc.stage3(7)
    sc.stage1(11)
    sc.stage2(10)
    v_out[2] = v_out[1] + vector_recv(2)
    for i in range(1, 4):
        vector(2 + i, v_out.at[2], p.up(i)).start()
    sc.stage3(8)
    sc.stage2(11)
    dvec_out[:, sc.own] = v_out[2] + vector_recv(3) + vector_recv(4) + vector_recv(5)
    last = remote(dvec_out.at[:, sc.own], dvec_out.at[:, sc.own], vsem.at[0, 6], vsem.at[1, 6], p.sib())
    last.start()
    for e in range(9, 12):
        sc.stage3(e)
    for i, (src, out) in enumerate(tokens):
        mine[i].wait()
        theirs[i].wait_send()
        remote(out.at[1 - p.c], out.at[1 - p.c], xsem.at[2 + i], xsem.at[4 + i], p.sib()).wait_recv()
    remote(dvec_out.at[:, sc.other], dvec_out.at[:, sc.other], vsem.at[0, 6], vsem.at[1, 6], p.sib()).wait_recv()
    last.wait_send()
    for i in range(6):
        vector(i, v_in.at[i], p.sib()).wait_send()
    sc.finish(12)


def layer_kernel(inner, seq, lengths, targets, *refs):
    vector_shards, weights, (query_tokens, passage_tokens) = refs[:9], refs[9:15], refs[15:17]
    loss, dxq_out, dxp_out, dvec_out = refs[17:21]
    grads, prob_hbm = refs[21:27], refs[27]
    (wa, wi, wo, x, q, k, v, act, act_t, slope, x_t, q_t, ctx_t, norm_t, y1, r1, y2, r2, prob, prob_q, ds_buf, vec, d_pool, y_sum,
     rows, packed, vectors, len_buf, d_vec, v_in, v_out) = refs[28:59]
    chunks, (g_ssem, g_rsem, g_lsem, g_vsem, psem, g_xsem, vsem, xsem) = refs[59:67], refs[67:75]
    p = Place(inner)
    len_p, len_q, settle = forward_part(
        p, seq, lengths, targets, vector_shards, weights, query_tokens, passage_tokens, d_pool, loss, prob_hbm, vec, prob, prob_q,
        wa, wi, wo, x, q, k, v, act, act_t, slope, x_t, q_t, ctx_t, norm_t, y1, r1, y2, r2, y_sum, rows, packed, vectors, len_buf,
        g_ssem, g_rsem, g_lsem, g_vsem, psem, g_xsem)
    backward_part(
        p, settle, len_p, len_q, d_pool, y_sum, vec, prob_hbm, prob, prob_q, dxq_out, dxp_out, dvec_out, grads,
        wa, wi, wo, x, k, v, act, act_t, slope, x_t, q_t, ctx_t, norm_t, y1, r1, y2, r2, ds_buf,
        d_vec, v_in, v_out, chunks, psem, vsem, xsem)


def layer_call(inner, seq, lengths, targets, vectors, weights, query_tokens, passage_tokens, cid=0):
    bf, f32 = jnp.bfloat16, jnp.float32
    sds, vmem, dma = jax.ShapeDtypeStruct, pltpu.VMEM, pltpu.SemaphoreType.DMA
    pairs = targets.shape[1]
    outs = [sds((8, 128), f32), sds((2, Q, 768), bf), sds((2, S, 768), bf), sds((16, 768), f32)]
    outs += [sds((48, 768), f32)] * 4 + [sds((48, 3072), f32), sds((192, 768), f32), sds((12, S, S), bf)]
    wide_rows, rows, turned, column = vmem((T, 768), f32), vmem((T, 768), bf), vmem((768, T), bf), vmem((T, 1), f32)
    scratch = [vmem((4, 4, 4, 48, 768), bf), vmem((4, 4, 48, 3072), bf), vmem((4, 4, 192, 768), bf)] + [rows] * 4
    scratch += [vmem((T, 3072), bf), vmem((3072, T), bf), vmem((T, 3072), bf)] + [turned] * 4 + [wide_rows, column] * 2
    scratch += [vmem((2, 2, S, S), bf), vmem((12, Q, Q), bf), vmem((2, S, S), bf), vmem((16, 3072), f32), vmem((2, 768), f32), vmem((2, 768), f32)]
    scratch += [vmem((pairs, 1, 1536), f32), vmem((16, 128), f32), vmem((4, 4, 16, 128), bf), vmem((2, 8, 128), f32)]
    scratch += [vmem((16, 768), f32), vmem((6, 16, 384), f32), vmem((3, 16, 384), f32)]
    scratch += [vmem((2, 4, 4, 48, 768), bf), vmem((4, 4, 4, 48, 384), bf), vmem((12, 4, 4, 48, 384), bf), vmem((12, 2, 4, 48, 384), bf)]
    scratch += [vmem((12, 4, 48, 384), bf), vmem((12, 3, 48, 384), bf), dma((12, 8)), dma((12, 8))]
    scratch += [dma((11, 12)), dma((11, 12)), dma((11,)), dma((2, 7)), dma((2,)), dma((6,)), dma((2, 7)), dma((6,))]
    return pl.pallas_call(
        functools.partial(layer_kernel, inner, seq),
        out_shape=outs,
        in_specs=[pl.BlockSpec(memory_space=pltpu.SMEM)] + [VM] * 10 + [ANY] * 8,
        out_specs=[VM, ANY, ANY] + [VM] * 7 + [ANY],
        scratch_shapes=scratch,
        compiler_params=pltpu.CompilerParams(collective_id=cid, has_side_effects=True, vmem_limit_bytes=63 << 20),
        name="layer",
    )(lengths, targets, *vectors, *weights, query_tokens, passage_tokens)


def outputs_kernel(inner, loss_in, dxq, dxp, d_vec, *refs):
    grads, (loss, q_out, p_out), g_outs, v_outs = refs[:6], refs[6:9], refs[9:15], refs[15:24]
    q_low, p_low, q_wide, p_wide, v_buf = refs[24:29]
    g_bufs, (isem, osem, gsem, vsem) = refs[29:35], refs[35:]
    parts = [(dxp.at[i, pl.ds(r, 256)], p_low.at[i, pl.ds(r, 256)], p_wide.at[i, pl.ds(r, 256)], p_out.at[i, pl.ds(r, 256)]) for i in range(2) for r in (0, 256)]
    parts.append((dxq, q_low, q_wide, q_out))
    loads = [pltpu.make_async_copy(part[0], part[1], isem.at[i]) for i, part in enumerate(parts)]
    v_load = pltpu.make_async_copy(d_vec, v_buf, vsem)
    g_loads = [pltpu.make_async_copy(src, buf, gsem.at[0, i]) for i, (src, buf) in enumerate(zip(grads, g_bufs))]
    g_stores = [pltpu.make_async_copy(buf, dst, gsem.at[1, i]) for i, (buf, dst) in enumerate(zip(g_bufs, g_outs))]
    for copy in loads + [v_load] + g_loads:
        copy.start()
    loss[...] = loss_in[0:1, 0:1]
    stores = []
    for i, (_, source, wider, out) in enumerate(parts):
        loads[i].wait()
        wider[...] = wide(source[...])
        stores.append(pltpu.make_async_copy(wider, out, osem.at[i]))
        stores[-1].start()
    for load, store in zip(g_loads, g_stores):
        load.wait()
        store.start()
    v_load.wait()
    shard = lax.axis_index("dp") // inner
    for size, first, outs in ((48, 0, v_outs[:8]), (192, 8, v_outs[8:])):
        at = lax.broadcasted_iota(jnp.int32, (768, 1), 0) - lax.rem(shard * size, 768)
        pick = jnp.where(at == lax.broadcasted_iota(jnp.int32, (1, size), 1), 1.0, 0.0)
        mine = jnp.dot(v_buf[first : first + 8], pick, precision=lax.Precision.HIGHEST, preferred_element_type=jnp.float32)
        if size == 48:
            for i in range(8):
                outs[i][...] = mine[i : i + 1]
        else:
            row = lax.broadcasted_iota(jnp.int32, (8, 1), 0)
            outs[0][...] = jnp.sum(jnp.where(row == shard // 4, mine, 0.0), axis=0, keepdims=True)
    for copy in stores + g_stores:
        copy.wait()


def outputs_call(inner, loss, dxq, dxp, d_vec, grads):
    sds, f32, vmem, dma = jax.ShapeDtypeStruct, jnp.float32, pltpu.VMEM, pltpu.SemaphoreType.DMA
    outs = [sds((1, 1), f32), sds(dxq.shape, f32), sds(dxp.shape, f32)] + [sds(g.shape, f32) for g in grads]
    outs += [sds((1, 48), f32)] * 8 + [sds((1, 192), f32)]
    scratch = [vmem(dxq.shape, dxq.dtype), vmem(dxp.shape, dxp.dtype), vmem(dxq.shape, f32), vmem(dxp.shape, f32), vmem(d_vec.shape, f32)]
    scratch += [vmem(g.shape, f32) for g in grads] + [dma((5,)), dma((5,)), dma((2, 6)), dma]
    return pl.pallas_call(
        functools.partial(outputs_kernel, inner),
        out_shape=outs,
        in_specs=[VM] + [ANY] * 9,
        out_specs=[VM] + [ANY] * 8 + [VM] * 9,
        scratch_shapes=scratch,
        compiler_params=pltpu.CompilerParams(vmem_limit_bytes=62 << 20),
        name="write_outputs",
    )(loss, dxq, dxp, d_vec, *grads)


def per_device(
    query_tokens, passage_tokens, lengths, positives,
    query_weight, key_weight, value_weight, output_weight, inner_weight, outer_weight,
    query_bias, value_bias, output_bias, inner_bias, outer_bias,
    first_gain, first_shift, second_gain, second_shift,
):
    inner = lax.axis_size("dp") // 16
    groups = None if inner == 1 else [[h * inner + i for i in range(inner)] for h in range(16)]
    seq = passage_tokens.shape[1]

    def fetch(w):
        if groups is None:
            return w
        return lax.all_gather(w, "dp", axis=0, tiled=True, axis_index_groups=groups)

    weights = [fetch(w) for w in (query_weight, key_weight, value_weight, output_weight, inner_weight, outer_weight)]
    vectors = (query_bias, value_bias, output_bias, outer_bias, first_gain, first_shift, second_gain, second_shift, inner_bias)
    vectors = [fetch(w)[None] for w in vectors[:8]] + [fetch(inner_bias)]
    loss, dxq, dxp, d_vec, *grads, _ = layer_call(
        inner, float(seq), lengths, positives[None], vectors, weights, query_tokens, passage_tokens)
    loss, dxq, dxp, *grads = outputs_call(inner, loss, dxq, dxp, d_vec, grads)
    grads = [g.reshape(-1) if g.shape[0] == 1 else g for g in grads]

    def finish(x):
        if groups is None:
            return x
        return lax.psum_scatter(x, "dp", scatter_dimension=0, tiled=True, axis_index_groups=groups)

    grads = [finish(g) for g in grads]
    flat = grads[6:]
    return (loss[0, 0], dxq, dxp, *grads[:6], flat[0], flat[1], flat[2], flat[8], *flat[3:8])


def solution(mesh):
    rows3, rows2, rows1 = P("dp", None, None), P("dp", None), P("dp")
    return jax.shard_map(
        per_device,
        mesh=mesh,
        in_specs=(rows3, rows3, P("tower", "dp"), P()) + (rows2,) * 6 + (rows1,) * 9,
        out_specs=(P(), rows3, rows3) + (rows2,) * 6 + (rows1,) * 9,
        check_vma=False,
    )
```
